32 devices in a mesh: depth: 8 (over y, x, core), strip: 4 (over z).
Axes of the slice: x: 2, y: 2, z: 4, core: 2. Of those that a mesh axis runs over, the one named last changes fastest.
Arguments:
- volume: float32 [32, 480, 1920], P('depth', 'strip'), may hold values from 0.001 to 4
- measured: float32 [480, 1920], P('strip'), may hold values from 0.032 to 0.32
- row_taps: float32 [32, 31], P('depth'), may hold values from 0.009677419 to 0.09677419
- col_taps: float32 [32, 15, 31], P('depth'), may hold values from 0.009677419 to 0.09677419
- phase_map: int32 [32, 15], P('depth'), may hold values from 0 to 14
- radius: int32 [32], P('depth'), may hold values from 1 to 15, as said below
Outputs:
- volume_out: float32 [32, 480, 1920], P('depth', 'strip')
The draws below stay inside these ranges and needn't reach their ends.
Inputs may be any that keep to these rules, and one draw needn't show every extreme that they name: Some plane's radius is exactly 15.
All inputs are finite; a program needn't handle non-finite values.
Results may differ from the reference program's by a relative error of at most 0.0032.
Values may be sent and summed in bfloat16 or wider, within the bound.
No kernel may reach another device: no remote copies, remote signals or barrier semaphores. Data moves between devices by JAX's collectives and lax.ppermute only.
A program may use at most 128 MiB of HBM per device.

```python
import math
import jax
import jax.numpy as jnp
from jax import lax

P_SIZE = 15
NFAM = 15
RMAX = 15
ITERS = 2
TAPS = 31
NX = 1920
NY = 480
NZ = 32


def shared_radius(key):
    spread_radii = jax.random.randint(jax.random.fold_in(key, 11), (NZ,), 1, RMAX + 1)
    widest = jax.random.randint(jax.random.fold_in(key, 12), (), 0, NZ)
    return jnp.where(jnp.arange(NZ) == widest, RMAX, spread_radii).astype(jnp.int32)


def draw_radius(key, part):
    return shared_radius(key)


def draw_volume(key, part):
    radii = shared_radius(key).astype(jnp.float32)
    footprint = (2.0 * radii + 1.0) * (2.0 * radii + 1.0)
    chance = 1.0 / footprint
    picker = jax.random.uniform(jax.random.fold_in(key, 21), (NZ, NY, NX), jnp.float32)
    levels = jax.random.uniform(jax.random.fold_in(key, 22), (NZ, NY, NX), jnp.float32)
    bright = jnp.exp(jnp.log(4.0) * levels)
    faint = 0.001 * jnp.exp(jnp.log(4.0) * levels)
    chosen = jnp.where(picker < chance[:, None, None], bright, faint)
    return jnp.clip(chosen, 0.001, 4.0).astype(jnp.float32)


def set_ends(entries, key, smallest, largest):
    spot = [jax.random.randint(jax.random.fold_in(key, axis), (), 0, length) for axis, length in enumerate(entries.shape)]
    longest = entries.shape.index(max(entries.shape))
    next_to = spot[:longest] + [(spot[longest] + 1) % entries.shape[longest]] + spot[longest + 1:]
    return entries.at[tuple(spot)].set(smallest).at[tuple(next_to)].set(largest)


def block_levels(rng, dims, split, low, high):
    level = 1.0
    for position, shards_of in split:
        steps = jax.random.uniform(jax.random.fold_in(jax.random.fold_in(rng, 6), position), (shards_of,), jnp.float32, low / len(split), high / len(split))
        level = level * jnp.repeat(jnp.exp(steps), dims[position] // shards_of).reshape((-1,) + (1,) * (len(dims) - 1 - position))
    return level


def setup_inputs(seed: int = 0) -> dict:
    key_list = jax.random.split(jax.random.key(seed), 7)
    return {
        "volume": draw_volume(jax.random.fold_in(key_list[6], 71), 0),
        "measured": jnp.clip(jnp.exp(math.log(0.32) - 2.30258502 * jax.random.uniform(key_list[1], (NY, NX), jnp.float32) ** block_levels(key_list[1], (NY, NX), ((0, 4),), -0.2, 0.2)), 0.032, 0.32),
        "row_taps": jnp.clip(jnp.exp(math.log(0.09677419) - 2.3025851 * jax.random.uniform(key_list[2], (NZ, TAPS), jnp.float32) ** block_levels(key_list[2], (NZ, TAPS), ((0, 8),), -0.2, 0.2)), 0.009677419, 0.09677419),
        "col_taps": jnp.clip(jnp.exp(math.log(0.09677419) - 2.3025851 * jax.random.uniform(key_list[3], (NZ, NFAM, TAPS), jnp.float32) ** block_levels(key_list[3], (NZ, NFAM, TAPS), ((0, 8),), -0.2, 0.2)), 0.009677419, 0.09677419),
        "phase_map": set_ends(jax.random.randint(key_list[4], (NZ, P_SIZE), 0, NFAM), jax.random.fold_in(key_list[4], 1), 0, NFAM - 1).astype(jnp.int32),
        "radius": draw_radius(jax.random.fold_in(key_list[6], 71), 0),
    }


def to_bf(value):
    return lax.optimization_barrier(value.astype(jnp.bfloat16)).astype(jnp.float32)


def displace(array, offset, axis_number):
    length = array.shape[axis_number]
    padding = [(0, 0)] * array.ndim
    padding[axis_number] = (max(offset, 0), max(-offset, 0))
    padded = jnp.pad(array, padding)
    return lax.slice_in_dim(padded, max(-offset, 0), max(-offset, 0) + length, axis=axis_number)


def plane_tables(row_tap, col_tap, phase_row, reach_limit):
    offsets = jnp.arange(TAPS, dtype=jnp.int32) - RMAX
    within = (jnp.abs(offsets) <= reach_limit).astype(jnp.float32)
    row_coef = to_bf(row_tap) * within
    family = phase_row[jnp.arange(NX, dtype=jnp.int32) % P_SIZE]
    col_coef = to_bf(col_tap[family]) * within[None, :]
    row_target = jnp.arange(NY, dtype=jnp.int32)[:, None] + offsets[None, :]
    row_grid = ((row_target >= 0) & (row_target < NY)).astype(jnp.float32)
    row_norm = jnp.sum(row_coef[None, :] * row_grid, axis=1)
    col_target = jnp.arange(NX, dtype=jnp.int32)[:, None] + offsets[None, :]
    col_grid = ((col_target >= 0) & (col_target < NX)).astype(jnp.float32)
    col_norm = jnp.sum(col_coef * col_grid, axis=1)
    return row_coef, col_coef, row_norm, col_norm


def reference(volume, measured, row_taps, col_taps, phase_map, radius):
    for iteration in range(ITERS):
        def project(sensor, plane):
            volume_plane, row_tap, col_tap, phase_row, reach_limit = plane
            row_coef, col_coef, row_norm, col_norm = plane_tables(row_tap, col_tap, phase_row, reach_limit)
            vol_bf = to_bf(volume_plane)
            spread = jnp.zeros((NY, NX), jnp.float32)
            for tap in range(TAPS):
                spread = spread + displace(vol_bf * col_coef[:, tap][None, :], tap - RMAX, 1)
            spread = to_bf(spread)
            for tap in range(TAPS):
                sensor = sensor + row_coef[tap] * displace(spread, tap - RMAX, 0)
            return sensor, None

        sensor, unused = lax.scan(project, jnp.zeros((NY, NX), jnp.float32),
                                  (volume, row_taps, col_taps, phase_map, radius))
        ratio_image = to_bf(measured / sensor)

        def update(plane):
            volume_plane, row_tap, col_tap, phase_row, reach_limit = plane
            row_coef, col_coef, row_norm, col_norm = plane_tables(row_tap, col_tap, phase_row, reach_limit)
            gathered = jnp.zeros((NY, NX), jnp.float32)
            for tap in range(TAPS):
                gathered = gathered + displace(ratio_image, RMAX - tap, 1) * col_coef[:, tap][None, :]
            gathered = to_bf(gathered)
            backproj = jnp.zeros((NY, NX), jnp.float32)
            for tap in range(TAPS):
                backproj = backproj + row_coef[tap] * displace(gathered, RMAX - tap, 0)
            return volume_plane * backproj / (row_norm[:, None] * col_norm[None, :])

        volume = lax.map(update, (volume, row_taps, col_taps, phase_map, radius))
    return volume
```

```python
import functools

import jax
import jax.numpy as jnp
from jax import lax
from jax.experimental import pallas as pl
from jax.experimental.pallas import tpu as pltpu
from jax.sharding import PartitionSpec as P

RMAX = 15
ITERS = 2
SIDE = 16
VMEM_LIMIT = 56 * 1024 * 1024

F32 = jnp.float32
BF16 = jnp.bfloat16
NT = (((1,), (1,)), ((), ()))


def round_up(value, step):
    return -(-value // step) * step


class Sizes:
    def __init__(self, planes, rows, cols, devices, pitch):
        self.planes, self.rows, self.cols, self.n, self.pitch = planes, rows, cols, devices, pitch
        self.w = cols // devices
        self.half = devices // 2
        assert cols % devices == 0 and self.w % pitch == 0 and self.w >= 2 * SIDE
        assert devices >= 2 and devices & (devices - 1) == 0 and rows >= 2 * RMAX and rows % 8 == 0
        self.wl = round_up(self.w, 128)
        self.kp = round_up(self.w + 2 * SIDE, 128)
        self.rp = round_up(rows, 128)
        self.e = rows + 2 * RMAX
        self.ep = round_up(self.e, 32)
        self.el = round_up(self.ep, 128)
        self.ar = round_up(max(self.w + SIDE, self.wl, 2 * pitch), pitch)


def iota(shape, axis):
    return lax.broadcasted_iota(jnp.int32, shape, axis)


def phase_rows(sz, z, phase_ref, col_ref, t_ref, a_ref):
    taps = col_ref.shape[2]
    t_ref[...] = jnp.zeros_like(t_ref)
    for p in range(sz.pitch):
        row = col_ref[z, pl.ds(phase_ref[z, p], 1), :]
        t_ref[p : p + 1, 0:taps] = row.astype(BF16).astype(F32)
    base = t_ref[0 : sz.pitch, :]
    for k in range(sz.ar // sz.pitch):
        a_ref[k * sz.pitch : (k + 1) * sz.pitch, :] = base


def spread_matrix(sz, reach, a_ref):
    main_rows = sz.w + SIDE
    main = pltpu.roll(a_ref[0:main_rows, 0 : sz.wl], sz.wl - RMAX, 1, stride=1, stride_axis=0)
    col = iota(main.shape, 1)
    main = jnp.where((jnp.abs(col - iota(main.shape, 0)) <= reach) & (col < sz.w), main, 0.0)
    first = (-SIDE) % sz.pitch
    tail = pltpu.roll(
        a_ref[first : first + SIDE, 0 : sz.wl], sz.wl - RMAX - SIDE, 1, stride=1, stride_axis=0
    )
    col = iota(tail.shape, 1)
    tail = jnp.where((jnp.abs(col - iota(tail.shape, 0) + SIDE) <= reach) & (col < sz.w), tail, 0.0)
    rest = jnp.zeros((sz.kp - main_rows - SIDE, sz.wl), F32)
    return jnp.concatenate([main, tail, rest], axis=0).astype(BF16)


def gather_matrix(sz, reach, a_ref):
    rows = a_ref[0 : sz.wl, :]
    main = pltpu.roll(rows, sz.kp - RMAX, 1, stride=1, stride_axis=0)
    col, row = iota(main.shape, 1), iota(main.shape, 0)
    main = jnp.where((jnp.abs(col - row) <= reach) & (col < sz.w + SIDE) & (row < sz.w), main, 0.0)
    tail = pltpu.roll(
        a_ref[0:SIDE, :], (sz.w + 2 * SIDE - RMAX) % sz.kp, 1, stride=1, stride_axis=0
    )
    col, row = iota(tail.shape, 1), iota(tail.shape, 0)
    inside = (col >= sz.w + SIDE) & (col < sz.w + 2 * SIDE)
    tail = jnp.where(inside & (jnp.abs(col - (sz.w + 2 * SIDE) - row) <= reach), tail, 0.0)
    top = main[0:SIDE] + tail
    return jnp.concatenate([top, main[SIDE:]], axis=0).astype(BF16)


def row_matrix(sz, z, reach, row_ref):
    taps = row_ref.shape[1]
    lane = iota((1, sz.el), 1)
    row = row_ref[pl.ds(z, 1), :].astype(BF16).astype(F32)
    row = jnp.concatenate([row, jnp.zeros((1, sz.el - taps), F32)], axis=1)
    row = jnp.where(jnp.abs(lane - RMAX) <= reach, row, 0.0)
    wide = jnp.broadcast_to(row, (sz.rp, sz.el))
    wide = pltpu.roll(wide, 0, 1, stride=1, stride_axis=0)
    return jnp.where(iota(wide.shape, 0) < sz.rows, wide, 0.0)


def put_block(sz, b, block, win_ref):
    lead = jnp.zeros((sz.rp - sz.rows, sz.w), F32)
    x = jnp.concatenate([block, lead], axis=0).astype(BF16)
    put_columns(sz, b, x, win_ref, sz.rp)


def put_columns(sz, b, x, win_ref, height):
    def rows(k):
        return slice(k * height, (k + 1) * height)

    win_ref[rows(b), 0 : sz.w] = x
    if b > 0:
        win_ref[rows(b - 1), sz.w : sz.w + SIDE] = x[:, 0:SIDE]
    if b < sz.n - 1:
        win_ref[rows(b + 1), sz.w + SIDE : sz.w + 2 * SIDE] = x[:, sz.w - SIDE :]


def columns_forward(sz, z, win_ref, matrix, s_ref):
    out = jnp.dot(win_ref[...], matrix, preferred_element_type=F32).astype(BF16)
    at = pl.ds(pl.multiple_of(z * sz.rp, sz.rp), sz.rp)
    for b in range(sz.n):
        s_ref[b, at, :] = out[b * sz.rp : (b + 1) * sz.rp, :]


def rows_forward(sz, me, rc_ref, s_ref, keep_ref, send_ref):
    core = lax.rem(me, 2)
    coef = rc_ref[...]
    for k in range(sz.half):
        for ref, block in ((send_ref, 2 * k + 1 - core), (keep_ref, 2 * k + core)):
            out = jnp.dot(coef, s_ref[block], preferred_element_type=F32)
            ref[k] = out[:, 0 : sz.w].astype(BF16)


def backward(sz, rwin_ref, bt, rt, g_ref):
    out = lax.dot_general(rwin_ref[...], bt, NT, preferred_element_type=F32).astype(BF16)
    for b in range(sz.n):
        g_ref[b, 0 : sz.ep, :] = out[b * sz.ep : (b + 1) * sz.ep, :]
    for b in range(sz.n):
        back = jnp.dot(rt, g_ref[b], preferred_element_type=F32)
        yield b, back[0 : sz.rows, 0 : sz.w]


def block_norm(sz, b, icn):
    kind = 1 if b == 0 else 2 if b == sz.n - 1 else 0
    return icn[kind : kind + 1, 0 : sz.w]


def window_ratio(sz, ratio_ref, rwin_ref, g_ref):
    rwin_ref[...] = jnp.zeros_like(rwin_ref)
    g_ref[...] = jnp.zeros_like(g_ref)
    for b in range(sz.n):
        put_columns(sz, b, ratio_ref[b], rwin_ref, sz.ep)


def first_kernel(
    sz, me_ref, radius_ref, phase_ref, row_ref, col_ref, vol_ref,
    wf_ref, rc_ref, keep_ref, send_ref, t_ref, a_ref, win_ref, s_ref,
):
    z = pl.program_id(0)

    @pl.when(z == 0)
    def _():
        win_ref[...] = jnp.zeros_like(win_ref)

    reach = radius_ref[z]
    phase_rows(sz, z, phase_ref, col_ref, t_ref, a_ref)
    wf_ref[0] = spread_matrix(sz, reach, a_ref)
    rt = row_matrix(sz, z, reach, row_ref)
    at = pl.ds(pl.multiple_of(z * sz.rp, sz.rp), sz.rp)
    rc_ref[:, at] = rt.T[0 : sz.ep, :].astype(BF16)
    for b in range(sz.n):
        put_block(sz, b, vol_ref[0, :, b * sz.w : (b + 1) * sz.w], win_ref)
    columns_forward(sz, z, win_ref, wf_ref[0], s_ref)

    @pl.when(z == sz.planes - 1)
    def _():
        rows_forward(sz, me_ref[0], rc_ref, s_ref, keep_ref, send_ref)


def table_kernel(
    sz, at_ref, radius_ref, phase_ref, row_ref, col_ref, after_ref,
    bt_ref, rt_ref, irn_ref, icn_ref, t_ref, a_ref,
):
    z = pl.program_id(0)
    reach = radius_ref[z]
    phase_rows(sz, z, phase_ref, col_ref, t_ref, a_ref)
    bt = gather_matrix(sz, reach, a_ref)
    bt_ref[0] = bt
    kind, col = iota((8, sz.kp), 0), iota((8, sz.kp), 1)
    below, above = col >= sz.w + SIDE, (col >= sz.w) & (col < sz.w + SIDE)
    ones = jnp.where(((kind == 1) & below) | ((kind == 2) & above), 0.0, 1.0).astype(BF16)
    norm = lax.dot_general(ones, bt, NT, preferred_element_type=F32)
    icn_ref[0] = jnp.where(norm > 0.0, 1.0 / norm, 0.0)
    rt = row_matrix(sz, z, reach, row_ref)
    rt_ref[0] = rt.astype(BF16)
    row = at_ref[0] + iota(rt.shape, 1) - RMAX
    norm = jnp.sum(jnp.where((row >= 0) & (row < at_ref[1]), rt, 0.0), axis=1, keepdims=True)
    irn_ref[0] = jnp.where(norm > 0.0, 1.0 / norm, 0.0)


def core_sum_kernel(sz, me_ref, keep_ref, recv_ref, own_ref, *out_refs):
    mine = me_ref[0] // 2
    own_ref[...] = keep_ref[mine].astype(F32) + recv_ref[mine].astype(F32)
    for j, ref in enumerate(out_refs, 1):
        other = mine ^ j
        ref[...] = (keep_ref[other].astype(F32) + recv_ref[other].astype(F32)).astype(BF16)


def chip_sum_kernel(sz, own_ref, meas_ref, *refs):
    recv_refs, (sum_ref, up_ref, down_ref) = refs[:-3], refs[-3:]
    total = own_ref[...]
    for ref in recv_refs:
        total = total + ref[...].astype(F32)
    sum_ref[...] = total
    for ref, first, row in ((up_ref, 0, 0), (down_ref, sz.rows, sz.rows - SIDE)):
        ref[0:32, :] = total[first : first + 32, :].astype(BF16)
        meas = meas_ref[row : row + SIDE, :]
        high = meas.astype(BF16)
        ref[32:48, :] = high
        ref[48:64, :] = (meas - high.astype(F32)).astype(BF16)


def ratio_kernel(sz, at_ref, sum_ref, meas_ref, above_ref, below_ref, ratio_ref, s_ref, m_ref):
    s_ref[...] = sum_ref[...]
    s_ref[0:32, :] += above_ref[0:32, :].astype(F32)
    s_ref[sz.rows : sz.rows + 32, :] += below_ref[0:32, :].astype(F32)
    m_ref[...] = jnp.zeros_like(m_ref)
    m_ref[RMAX : RMAX + sz.rows, :] = meas_ref[...]
    high, low = above_ref[32:48, :].astype(F32), above_ref[48:64, :].astype(F32)
    m_ref[0:RMAX, :] = (high + low)[SIDE - RMAX :, :]
    high, low = below_ref[32:48, :].astype(F32), below_ref[48:64, :].astype(F32)
    m_ref[RMAX + sz.rows : sz.e, :] = (high + low)[0:RMAX, :]
    row = iota(s_ref.shape, 0)
    spot = at_ref[0] + row - RMAX
    inside = (row < sz.e) & (spot >= 0) & (spot < at_ref[1])
    ratio_ref[...] = jnp.where(inside, m_ref[...] / s_ref[...], 0.0).astype(BF16)


def middle_kernel(
    sz, me_ref, ratio_ref, bt_ref, rt_ref, irn_ref, icn_ref, wf_ref, rc_ref, vol_ref,
    new_ref, keep_ref, send_ref, rwin_ref, g_ref, win_ref, s_ref,
):
    z = pl.program_id(0)

    @pl.when(z == 0)
    def _():
        win_ref[...] = jnp.zeros_like(win_ref)
        window_ratio(sz, ratio_ref, rwin_ref, g_ref)

    icn, irn = icn_ref[0], irn_ref[0][0 : sz.rows]
    for b, back in backward(sz, rwin_ref, bt_ref[0], rt_ref[0], g_ref):
        old = vol_ref[0, :, b * sz.w : (b + 1) * sz.w]
        new = old * back * (irn * block_norm(sz, b, icn))
        new_ref[0, b] = new
        put_block(sz, b, new, win_ref)
    columns_forward(sz, z, win_ref, wf_ref[0], s_ref)

    @pl.when(z == sz.planes - 1)
    def _():
        rows_forward(sz, me_ref[0], rc_ref, s_ref, keep_ref, send_ref)


def last_kernel(
    sz, ratio_ref, bt_ref, rt_ref, irn_ref, icn_ref, vol_ref, out_ref, rwin_ref, g_ref
):
    @pl.when(pl.program_id(0) == 0)
    def _():
        window_ratio(sz, ratio_ref, rwin_ref, g_ref)

    icn, irn = icn_ref[0], irn_ref[0][0 : sz.rows]
    for b, back in backward(sz, rwin_ref, bt_ref[0], rt_ref[0], g_ref):
        new = vol_ref[0, b] * back * (irn * block_norm(sz, b, icn))
        out_ref[0, :, b * sz.w : (b + 1) * sz.w] = new


def whole(shape):
    return pl.BlockSpec(shape, lambda z: (0,) * len(shape))


def plane(shape):
    return pl.BlockSpec((1,) + shape, lambda z: (z,) + (0,) * len(shape))


SMEM = pl.BlockSpec(memory_space=pltpu.SMEM)
ANY = pl.BlockSpec(memory_space=pl.ANY)


def shape(dims, dtype):
    return jax.ShapeDtypeStruct(dims, dtype)


def call(kernel, sz, name, grid, in_specs, out_specs, out_shape, scratch, args, flops=0, nbytes=0):
    return pl.pallas_call(
        functools.partial(kernel, sz),
        grid=grid,
        in_specs=in_specs,
        out_specs=out_specs,
        out_shape=out_shape,
        scratch_shapes=scratch,
        compiler_params=pltpu.CompilerParams(vmem_limit_bytes=VMEM_LIMIT),
        cost_estimate=pl.CostEstimate(flops=flops, bytes_accessed=nbytes, transcendentals=0),
        name=name,
    )(*args)


def local(volume, measured, row_taps, col_taps, phase_map, radius):
    n = lax.axis_size("depth")
    strips = lax.axis_size("strip")
    planes, rows, cols = volume.shape
    sz = Sizes(planes, rows, cols, n, phase_map.shape[1])
    me = lax.axis_index("depth")
    me_arg = me.reshape(1).astype(jnp.int32)
    at_arg = jnp.stack([lax.axis_index("strip") * rows, rows * strips]).astype(jnp.int32)
    to_core = [(i, i ^ 1) for i in range(n)]
    downward = [(i, i + 1) for i in range(strips - 1)]
    upward = [(i + 1, i) for i in range(strips - 1)]

    meas = lax.dynamic_slice_in_dim(measured, me * sz.w, sz.w, axis=1)

    vol_plane = plane((rows, cols))
    wf_plane, rc_whole = plane((sz.kp, sz.wl)), whole((sz.ep, planes * sz.rp))
    half_whole = whole((sz.half, sz.ep, sz.w))
    half_shape = shape((sz.half, sz.ep, sz.w), BF16)
    tap_specs = [SMEM, SMEM, whole(row_taps.shape), whole(col_taps.shape)]
    tap_scratch = [
        pltpu.VMEM((round_up(sz.pitch, 8), sz.kp), F32),
        pltpu.VMEM((sz.ar, sz.kp), F32),
    ]
    win_scratch = [
        pltpu.VMEM((n * sz.rp, sz.kp), BF16),
        pltpu.VMEM((n, planes * sz.rp, sz.wl), BF16),
    ]
    ratio_scratch = [
        pltpu.VMEM((n * sz.ep, sz.kp), BF16),
        pltpu.VMEM((n, sz.el, sz.wl), BF16),
    ]

    wf, rc, keep, send = call(
        first_kernel, sz, "first", (planes,),
        [SMEM] + tap_specs + [vol_plane],
        [wf_plane, rc_whole, half_whole, half_whole],
        [
            shape((planes, sz.kp, sz.wl), BF16),
            shape((sz.ep, planes * sz.rp), BF16),
            half_shape,
            half_shape,
        ],
        tap_scratch + win_scratch,
        (me_arg, radius, phase_map, row_taps, col_taps, volume),
    )

    tables = None
    current = volume
    for iteration in range(ITERS):
        recv = lax.ppermute(send, "depth", to_core)
        flat = shape((sz.ep, sz.w), BF16)
        own, *sends = call(
            core_sum_kernel, sz, "core_sum", (),
            [SMEM] + [pl.BlockSpec()] * 2,
            [pl.BlockSpec()] * sz.half,
            [shape((sz.ep, sz.w), F32)] + [flat] * (sz.half - 1),
            [], (me_arg, keep, recv),
        )
        recvs = [
            lax.ppermute(part, "depth", [(i, i ^ (2 * j)) for i in range(n)])
            for j, part in enumerate(sends, 1)
        ]
        total, to_above, to_below = call(
            chip_sum_kernel, sz, "chip_sum", (),
            [pl.BlockSpec()] * (2 + len(recvs)),
            [pl.BlockSpec()] * 3,
            [shape((sz.ep, sz.w), F32)] + [shape((64, sz.w), BF16)] * 2,
            [], (own, meas, *recvs),
        )
        from_below = lax.ppermute(to_above, "strip", upward)
        from_above = lax.ppermute(to_below, "strip", downward)
        ratio = call(
            ratio_kernel, sz, "ratio", (),
            [SMEM] + [pl.BlockSpec()] * 4,
            pl.BlockSpec(),
            flat,
            [pltpu.VMEM((sz.ep, sz.w), F32)] * 2,
            (at_arg, total, meas, from_above, from_below),
        )
        gathered = lax.all_gather(ratio, "depth", axis=0, tiled=False)
        if tables is None:
            tables = call(
                table_kernel, sz, "tables", (planes,),
                [SMEM] + tap_specs + [ANY],
                [plane((sz.wl, sz.kp)), plane((sz.rp, sz.el)), plane((sz.rp, 1)), plane((8, sz.wl))],
                [
                    shape((planes, sz.wl, sz.kp), BF16),
                    shape((planes, sz.rp, sz.el), BF16),
                    shape((planes, sz.rp, 1), F32),
                    shape((planes, 8, sz.wl), F32),
                ],
                tap_scratch,
                (at_arg, radius, phase_map, row_taps, col_taps, ratio),
            )
        table_specs = [
            plane((sz.wl, sz.kp)), plane((sz.rp, sz.el)), plane((sz.rp, 1)), plane((8, sz.wl))
        ]
        ratio_whole = whole((n, sz.ep, sz.w))
        blocked = plane((n, rows, sz.w))
        if iteration < ITERS - 1:
            current, keep, send = call(
                middle_kernel, sz, "middle", (planes,),
                [SMEM, ratio_whole] + table_specs + [wf_plane, rc_whole, vol_plane],
                [blocked, half_whole, half_whole],
                [shape((planes, n, rows, sz.w), F32), half_shape, half_shape],
                ratio_scratch + win_scratch,
                (me_arg, gathered, *tables, wf, rc, current),
            )
        else:
            current = call(
                last_kernel, sz, "last", (planes,),
                [ratio_whole] + table_specs + [blocked],
                vol_plane,
                shape(volume.shape, F32),
                ratio_scratch,
                (gathered, *tables, current),
            )
    return current


def solution(mesh):
    return jax.shard_map(
        local,
        mesh=mesh,
        in_specs=(
            P("depth", "strip", None),
            P("strip", None),
            P("depth", None),
            P("depth", None, None),
            P("depth", None),
            P("depth"),
        ),
        out_specs=P("depth", "strip", None),
        check_vma=False,
    )
```

```python
import functools

import jax
import jax.numpy as jnp
from jax import lax
from jax.experimental import pallas as pl
from jax.experimental.pallas import tpu as pltpu
from jax.sharding import PartitionSpec as P

RMAX = 15
ITERS = 2
SIDE = 16

F32 = jnp.float32
BF16 = jnp.bfloat16
NT = (((1,), (1,)), ((), ()))


def round_up(value, step):
    return -(-value // step) * step


class Sizes:
    def __init__(self, planes, rows, strips, cols, devices, pitch):
        self.total = rows * strips
        self.planes, self.rows, self.cols, self.n, self.pitch = planes, rows, cols, devices, pitch
        self.w = cols // devices
        self.half = devices // 2
        assert cols % devices == 0 and self.w % pitch == 0 and self.w >= 2 * SIDE
        assert devices >= 2 and devices & (devices - 1) == 0 and rows >= 2 * RMAX and rows % 8 == 0
        self.wl = round_up(self.w, 128)
        self.kp = round_up(self.w + 2 * SIDE, 128)
        self.rp = round_up(rows, 128)
        self.e = rows + 2 * RMAX
        self.ep = round_up(self.e, 32)
        self.el = round_up(self.ep, 128)
        self.ar = round_up(max(self.w + SIDE, self.wl, 2 * pitch), pitch)


def iota(shape, axis):
    return lax.broadcasted_iota(jnp.int32, shape, axis)


def phase_rows(sz, z, phase_ref, col_ref, t_ref, a_ref):
    taps = col_ref.shape[2]
    t_ref[...] = jnp.zeros_like(t_ref)
    for p in range(sz.pitch):
        row = col_ref[phase_ref[z, p], pl.ds(z, 1), :]
        t_ref[p : p + 1, 0:taps] = row.astype(BF16).astype(F32)
    base = t_ref[0 : sz.pitch, :]
    for k in range(sz.ar // sz.pitch):
        a_ref[k * sz.pitch : (k + 1) * sz.pitch, :] = base


def spread_matrix(sz, reach, a_ref):
    main_rows = sz.w + SIDE
    main = pltpu.roll(a_ref[0:main_rows, 0 : sz.wl], sz.wl - RMAX, 1, stride=1, stride_axis=0)
    col = iota(main.shape, 1)
    main = jnp.where((jnp.abs(col - iota(main.shape, 0)) <= reach) & (col < sz.w), main, 0.0)
    first = (-SIDE) % sz.pitch
    tail = pltpu.roll(
        a_ref[first : first + SIDE, 0 : sz.wl], sz.wl - RMAX - SIDE, 1, stride=1, stride_axis=0
    )
    col = iota(tail.shape, 1)
    tail = jnp.where((jnp.abs(col - iota(tail.shape, 0) + SIDE) <= reach) & (col < sz.w), tail, 0.0)
    rest = jnp.zeros((sz.kp - main_rows - SIDE, sz.wl), F32)
    return jnp.concatenate([main, tail, rest], axis=0).astype(BF16)


def gather_matrix(sz, reach, a_ref):
    rows = a_ref[0 : sz.wl, :]
    main = pltpu.roll(rows, sz.kp - RMAX, 1, stride=1, stride_axis=0)
    col, row = iota(main.shape, 1), iota(main.shape, 0)
    main = jnp.where((jnp.abs(col - row) <= reach) & (col < sz.w + SIDE) & (row < sz.w), main, 0.0)
    tail = pltpu.roll(
        a_ref[0:SIDE, :], (sz.w + 2 * SIDE - RMAX) % sz.kp, 1, stride=1, stride_axis=0
    )
    col, row = iota(tail.shape, 1), iota(tail.shape, 0)
    inside = (col >= sz.w + SIDE) & (col < sz.w + 2 * SIDE)
    tail = jnp.where(inside & (jnp.abs(col - (sz.w + 2 * SIDE) - row) <= reach), tail, 0.0)
    top = main[0:SIDE] + tail
    return jnp.concatenate([top, main[SIDE:]], axis=0).astype(BF16)


def row_matrix(sz, z, reach, row_ref):
    taps = row_ref.shape[1]
    lane = iota((1, sz.el), 1)
    row = row_ref[pl.ds(z, 1), :].astype(BF16).astype(F32)
    row = jnp.concatenate([row, jnp.zeros((1, sz.el - taps), F32)], axis=1)
    row = jnp.where(jnp.abs(lane - RMAX) <= reach, row, 0.0)
    wide = jnp.broadcast_to(row, (sz.rp, sz.el))
    wide = pltpu.roll(wide, 0, 1, stride=1, stride_axis=0)
    return jnp.where(iota(wide.shape, 0) < sz.rows, wide, 0.0)


def put_block(sz, b, block, win_ref):
    lead = jnp.zeros((sz.rp - sz.rows, sz.w), F32)
    x = jnp.concatenate([block, lead], axis=0).astype(BF16)

    def rows(k):
        return slice(k * sz.rp, (k + 1) * sz.rp)

    win_ref[rows(b), 0 : sz.w] = x
    if b > 0:
        win_ref[rows(b - 1), sz.w : sz.w + SIDE] = x[:, 0:SIDE]
    if b < sz.n - 1:
        win_ref[rows(b + 1), sz.w + SIDE : sz.w + 2 * SIDE] = x[:, sz.w - SIDE :]


def columns_forward(sz, z, win_ref, matrix, s_ref):
    out = jnp.dot(win_ref[...], matrix, preferred_element_type=F32).astype(BF16)
    at = pl.ds(pl.multiple_of(z * sz.rp, sz.rp), sz.rp)
    for b in range(sz.n):
        s_ref[b, at, :] = out[b * sz.rp : (b + 1) * sz.rp, :]


def rows_forward(sz, me, rc_ref, s_ref, keep_ref, send_ref):
    core = lax.rem(me, 2)
    coef = rc_ref[...]
    for k in range(sz.half):
        for ref, block in ((send_ref, 2 * k + 1 - core), (keep_ref, 2 * k + core)):
            out = jnp.dot(coef, s_ref[block], preferred_element_type=F32)
            ref[k] = out[:, 0 : sz.w].astype(ref.dtype)


def backward(sz, rwin_ref, bt, rt, g_ref):
    out = lax.dot_general(rwin_ref[...], bt, NT, preferred_element_type=F32).astype(BF16)
    for b in range(sz.n):
        g_ref[b, 0 : sz.ep, :] = out[b * sz.ep : (b + 1) * sz.ep, :]
    for b in range(sz.n):
        back = jnp.dot(rt, g_ref[b], preferred_element_type=F32)
        yield b, back[0 : sz.rows, 0 : sz.w]


def block_norm(sz, b, icn):
    kind = 1 if b == 0 else 2 if b == sz.n - 1 else 0
    return icn[kind : kind + 1, 0 : sz.w]


def window_ratio(sz, me, same_ref, other_ref, rwin_ref, g_ref):
    rwin_ref[...] = jnp.zeros_like(rwin_ref)
    g_ref[...] = jnp.zeros_like(g_ref)
    core = lax.rem(me, 2)

    def rows(k):
        return pl.ds(pl.multiple_of(k * sz.ep, sz.ep), sz.ep)

    for j in range(sz.half):
        chip = (me // 2) ^ j
        for ref, b in ((same_ref, 2 * chip + core), (other_ref, 2 * chip + 1 - core)):
            rwin_ref[rows(b), 0 : sz.w] = ref[j]

            @pl.when(b > 0)
            def _():
                rwin_ref[rows(b - 1), sz.w : sz.w + SIDE] = ref[j, :, 0:SIDE]

            @pl.when(b < sz.n - 1)
            def _():
                rwin_ref[rows(b + 1), sz.w + SIDE : sz.w + 2 * SIDE] = ref[j, :, sz.w - SIDE :]


def first_kernel(
    sz, me_ref, radius_hbm, phase_hbm, row_hbm, col_hbm, vol_hbm,
    wf_ref, rc_ref, keep_ref, send_ref,
    radius_ref, phase_ref, row_ref, col_ref, vol_ref, t_ref, a_ref, win_ref, s_ref, sems,
):
    pairs = ((radius_hbm, radius_ref), (phase_hbm, phase_ref), (row_hbm, row_ref), (col_hbm, col_ref))
    small = [pltpu.make_async_copy(a, b, sems.at[i]) for i, (a, b) in enumerate(pairs)]
    large = [
        pltpu.make_async_copy(vol_hbm.at[z], vol_ref.at[z], sems.at[4 + z])
        for z in range(sz.planes)
    ]
    for copy in small + large:
        copy.start()
    win_ref[...] = jnp.zeros_like(win_ref)
    for copy in small:
        copy.wait()
    for z in range(sz.planes):
        reach = radius_ref[z]
        phase_rows(sz, z, phase_ref, col_ref, t_ref, a_ref)
        wf_ref[z] = spread_matrix(sz, reach, a_ref)
        rt = row_matrix(sz, z, reach, row_ref)
        rc_ref[:, z * sz.rp : (z + 1) * sz.rp] = rt.T[0 : sz.ep, :].astype(BF16)
    for z in range(sz.planes):
        large[z].wait()
        for b in range(sz.n):
            put_block(sz, b, vol_ref[z, :, b * sz.w : (b + 1) * sz.w], win_ref)
        columns_forward(sz, z, win_ref, wf_ref[z], s_ref)
    rows_forward(sz, me_ref[0], rc_ref, s_ref, keep_ref, send_ref)


def table_kernel(
    sz, strip_ref, radius_hbm, phase_hbm, row_hbm, col_hbm, after_ref,
    bt_ref, rt_ref, irn_ref, icn_ref,
    radius_ref, phase_ref, row_ref, col_ref, t_ref, a_ref, sems,
):
    pairs = ((radius_hbm, radius_ref), (phase_hbm, phase_ref), (row_hbm, row_ref), (col_hbm, col_ref))
    small = [pltpu.make_async_copy(a, b, sems.at[i]) for i, (a, b) in enumerate(pairs)]
    for copy in small:
        copy.start()
    for copy in small:
        copy.wait()
    kind, col = iota((8, sz.kp), 0), iota((8, sz.kp), 1)
    below, above = col >= sz.w + SIDE, (col >= sz.w) & (col < sz.w + SIDE)
    ones = jnp.where(((kind == 1) & below) | ((kind == 2) & above), 0.0, 1.0).astype(BF16)
    for z in range(sz.planes):
        reach = radius_ref[z]
        phase_rows(sz, z, phase_ref, col_ref, t_ref, a_ref)
        bt = gather_matrix(sz, reach, a_ref)
        bt_ref[z] = bt
        norm = lax.dot_general(ones, bt, NT, preferred_element_type=F32)
        icn_ref[z] = jnp.where(norm > 0.0, 1.0 / norm, 0.0)
        rt = row_matrix(sz, z, reach, row_ref)
        rt_ref[z] = rt.astype(BF16)
        row = strip_ref[0] * sz.rows + iota(rt.shape, 1) - RMAX
        norm = jnp.sum(jnp.where((row >= 0) & (row < sz.total), rt, 0.0), axis=1, keepdims=True)
        irn_ref[z] = jnp.where(norm > 0.0, 1.0 / norm, 0.0)


def core_sum_kernel(sz, me_ref, keep_ref, recv_ref, own_ref, *out_refs):
    mine = me_ref[0] // 2
    own_ref[...] = keep_ref[mine] + recv_ref[mine].astype(F32)
    for j, ref in enumerate(out_refs, 1):
        other = mine ^ j
        ref[...] = (keep_ref[other] + recv_ref[other].astype(F32)).astype(BF16)


def chip_sum_kernel(sz, strip_ref, after_ref, own_ref, meas_ref, *refs):
    recv_refs, (sum_ref, first_ref, second_ref) = refs[:-3], refs[-3:]
    total = own_ref[...]
    for ref in recv_refs:
        total = total + ref[...].astype(F32)
    sum_ref[...] = total
    edges = []
    for first, row in ((0, 0), (sz.rows, sz.rows - SIDE)):
        meas = meas_ref[row : row + SIDE, :]
        high = meas.astype(BF16).astype(F32)
        edges.append(jnp.concatenate([total[first : first + 32, :], high, meas - high], axis=0))
    up, down = edges
    even = lax.rem(strip_ref[0], 2) == 0
    first_ref[...] = jnp.where(even, down, up).astype(BF16)
    second_ref[...] = jnp.where(even, up, down).astype(BF16)


def ratio_kernel(sz, strip_ref, sum_ref, meas_ref, first_ref, second_ref, ratio_ref, s_ref, m_ref):
    even = lax.rem(strip_ref[0], 2) == 0
    first, second = first_ref[...].astype(F32), second_ref[...].astype(F32)
    above, below = jnp.where(even, second, first), jnp.where(even, first, second)
    s_ref[...] = sum_ref[...]
    s_ref[0:32, :] += above[0:32, :]
    s_ref[sz.rows : sz.rows + 32, :] += below[0:32, :]
    m_ref[...] = jnp.zeros_like(m_ref)
    m_ref[RMAX : RMAX + sz.rows, :] = meas_ref[...]
    m_ref[0:RMAX, :] = (above[32:48, :] + above[48:64, :])[SIDE - RMAX :, :]
    m_ref[RMAX + sz.rows : sz.e, :] = (below[32:48, :] + below[48:64, :])[0:RMAX, :]
    row = iota(s_ref.shape, 0)
    spot = strip_ref[0] * sz.rows + row - RMAX
    inside = (row < sz.e) & (spot >= 0) & (spot < sz.total)
    ratio_ref[...] = jnp.where(inside, m_ref[...] / s_ref[...], 0.0).astype(BF16)


def middle_kernel(
    sz, me_ref, same_ref, other_ref, bt_ref, rt_ref, irn_ref, icn_ref, wf_ref, rc_ref, vol_hbm,
    new_ref, keep_ref, send_ref, vol_ref, rwin_ref, g_ref, win_ref, s_ref, sems,
):
    def fetch(z):
        return pltpu.make_async_copy(vol_hbm.at[z], vol_ref.at[z], sems.at[z])

    for z in range(sz.planes):
        fetch(z).start()
    win_ref[...] = jnp.zeros_like(win_ref)
    window_ratio(sz, me_ref[0], same_ref, other_ref, rwin_ref, g_ref)

    def step(z, carry):
        icn, irn = icn_ref[z], irn_ref[z][0 : sz.rows]
        fetch(z).wait()
        for b, back in backward(sz, rwin_ref, bt_ref[z], rt_ref[z], g_ref):
            old = vol_ref[z, :, b * sz.w : (b + 1) * sz.w]
            new = old * back * (irn * block_norm(sz, b, icn))
            new_ref[z, b] = new
            put_block(sz, b, new, win_ref)
        columns_forward(sz, z, win_ref, wf_ref[z], s_ref)
        return carry

    lax.fori_loop(0, sz.planes, step, 0)
    rows_forward(sz, me_ref[0], rc_ref, s_ref, keep_ref, send_ref)


def last_kernel(
    sz, me_ref, same_ref, other_ref, bt_ref, rt_ref, irn_ref, icn_ref, vol_ref,
    out_hbm, rwin_ref, g_ref, out_ref, sems,
):
    window_ratio(sz, me_ref[0], same_ref, other_ref, rwin_ref, g_ref)

    def copy(z):
        return pltpu.make_async_copy(out_ref.at[z], out_hbm.at[z], sems.at[z])

    def step(z, carry):
        icn, irn = icn_ref[z], irn_ref[z][0 : sz.rows]
        for b, back in backward(sz, rwin_ref, bt_ref[z], rt_ref[z], g_ref):
            new = vol_ref[z, b] * back * (irn * block_norm(sz, b, icn))
            out_ref[z, :, b * sz.w : (b + 1) * sz.w] = new
        copy(z).start()
        return carry

    lax.fori_loop(0, sz.planes, step, 0)
    for z in range(sz.planes):
        copy(z).wait()


SMEM = pl.BlockSpec(memory_space=pltpu.SMEM)
VMEM = pl.BlockSpec(memory_space=pltpu.VMEM)
ANY = pl.BlockSpec(memory_space=pl.ANY)
HBM = pl.BlockSpec(memory_space=pltpu.HBM)


def shape(dims, dtype):
    return jax.ShapeDtypeStruct(dims, dtype)


def call(kernel, sz, name, in_specs, out_specs, out_shape, scratch, args, mib, micros=1):
    return pl.pallas_call(
        functools.partial(kernel, sz),
        in_specs=in_specs,
        out_specs=out_specs,
        out_shape=out_shape,
        scratch_shapes=scratch,
        compiler_params=pltpu.CompilerParams(vmem_limit_bytes=mib * 1024 * 1024),
        cost_estimate=pl.CostEstimate(
            flops=0, bytes_accessed=micros * 3_000_000, transcendentals=0
        ),
        name=name,
    )(*args)


def local(volume, measured, row_taps, col_taps, phase_map, radius):
    n = lax.axis_size("depth")
    strips = lax.axis_size("strip")
    planes, rows, cols = volume.shape
    sz = Sizes(planes, rows, strips, cols, n, phase_map.shape[1])
    me = lax.axis_index("depth")
    strip = lax.axis_index("strip")
    me_arg = me.reshape(1).astype(jnp.int32)
    strip_arg = strip.reshape(1).astype(jnp.int32)
    to_core = [(i, i ^ 1) for i in range(n)]
    to_chip = [[(i, i ^ (2 * j)) for i in range(n)] for j in range(1, sz.half)]
    swaps = []
    for start in (0, 1):
        below = [(i, i + 1) for i in range(start, strips - 1, 2)]
        swaps.append(below + [(b, a) for a, b in below])

    volume = pltpu.with_memory_space_constraint(volume, pltpu.HBM)
    meas = lax.dynamic_slice_in_dim(measured, me * sz.w, sz.w, axis=1)
    by_family = col_taps.transpose(1, 0, 2)

    flat = shape((sz.ep, sz.w), BF16)
    halves = [shape((sz.half, sz.ep, sz.w), F32), shape((sz.half, sz.ep, sz.w), BF16)]
    blocked = shape((planes, n, rows, sz.w), F32)
    tap_args = tuple(
        pltpu.with_memory_space_constraint(x, pltpu.HBM)
        for x in (radius, phase_map, row_taps, by_family)
    )
    tap_scratch = [
        pltpu.SMEM(radius.shape, jnp.int32),
        pltpu.SMEM(phase_map.shape, jnp.int32),
        pltpu.VMEM(row_taps.shape, F32),
        pltpu.VMEM(by_family.shape, F32),
    ]
    row_scratch = [
        pltpu.VMEM((round_up(sz.pitch, 8), sz.kp), F32),
        pltpu.VMEM((sz.ar, sz.kp), F32),
    ]
    win_scratch = [
        pltpu.VMEM((n * sz.rp, sz.kp), BF16),
        pltpu.VMEM((n, planes * sz.rp, sz.wl), BF16),
    ]
    ratio_scratch = [
        pltpu.VMEM((n * sz.ep, sz.kp), BF16),
        pltpu.VMEM((n, sz.el, sz.wl), BF16),
    ]

    wf, rc, keep, send = call(
        first_kernel, sz, "first",
        [SMEM] + [HBM] * 5,
        [VMEM] * 4,
        [
            shape((planes, sz.kp, sz.wl), BF16),
            shape((sz.ep, planes * sz.rp), BF16),
            *halves,
        ],
        tap_scratch + [pltpu.VMEM(volume.shape, F32)] + row_scratch + win_scratch
        + [pltpu.SemaphoreType.DMA((4 + planes,))],
        (me_arg, *tap_args, volume),
        24, 4,
    )

    tables, current = None, volume
    for iteration in range(ITERS):
        recv = lax.ppermute(send, "depth", to_core)
        own, *sends = call(
            core_sum_kernel, sz, "core_sum",
            [SMEM, VMEM, VMEM],
            [VMEM] * sz.half,
            [shape((sz.ep, sz.w), F32)] + [flat] * (sz.half - 1),
            [], (me_arg, keep, recv), 4,
        )
        if tables is None:
            tables = call(
                table_kernel, sz, "tables",
                [SMEM] + [HBM] * 4 + [ANY],
                [VMEM] * 4,
                [
                    shape((planes, sz.wl, sz.kp), BF16),
                    shape((planes, sz.rp, sz.el), BF16),
                    shape((planes, sz.rp, 1), F32),
                    shape((planes, 8, sz.wl), F32),
                ],
                tap_scratch + row_scratch + [pltpu.SemaphoreType.DMA((4,))],
                (strip_arg, *tap_args, own),
                8, 2,
            )
        recvs = [lax.ppermute(part, "depth", pairs) for part, pairs in zip(sends, to_chip)]
        total, *edges = call(
            chip_sum_kernel, sz, "chip_sum",
            [SMEM, ANY] + [VMEM] * (2 + len(recvs)),
            [VMEM] * 3,
            [shape((sz.ep, sz.w), F32)] + [shape((64, sz.w), BF16)] * 2,
            [], (strip_arg, tables[3], own, meas, *recvs), 4,
        )
        edges = [lax.ppermute(part, "strip", pairs) for part, pairs in zip(edges, swaps)]
        ratio = call(
            ratio_kernel, sz, "ratio",
            [SMEM] + [VMEM] * 4,
            VMEM,
            flat,
            [pltpu.VMEM((sz.ep, sz.w), F32)] * 2,
            (strip_arg, total, meas, *edges), 4,
        )
        same = jnp.stack([ratio] + [lax.ppermute(ratio, "depth", pairs) for pairs in to_chip])
        other = lax.ppermute(same, "depth", to_core)
        if iteration < ITERS - 1:
            current, keep, send = call(
                middle_kernel, sz, "middle",
                [SMEM] + [VMEM] * 8 + [HBM],
                [VMEM] * 3,
                [blocked, *halves],
                [pltpu.VMEM(volume.shape, F32)] + ratio_scratch + win_scratch
                + [pltpu.SemaphoreType.DMA((planes,))],
                (me_arg, same, other, *tables, wf, rc, current),
                24, 5,
            )
        else:
            current = call(
                last_kernel, sz, "last",
                [SMEM] + [VMEM] * 7,
                HBM,
                shape(volume.shape, F32),
                ratio_scratch
                + [pltpu.VMEM(volume.shape, F32), pltpu.SemaphoreType.DMA((planes,))],
                (me_arg, same, other, *tables, current),
                24, 5,
            )
    return current


def solution(mesh):
    return jax.shard_map(
        local,
        mesh=mesh,
        in_specs=(
            P("depth", "strip", None),
            P("strip", None),
            P("depth", None),
            P("depth", None, None),
            P("depth", None),
            P("depth"),
        ),
        out_specs=P("depth", "strip", None),
        check_vma=False,
    )
```

```python
import functools

import jax
import jax.numpy as jnp
from jax import lax
from jax.experimental import pallas as pl
from jax.experimental.pallas import tpu as pltpu
from jax.sharding import PartitionSpec as P

RMAX = 15
ITERS = 2
SIDE = 16
LANES = 128

F32 = jnp.float32
BF16 = jnp.bfloat16


def round_up(value, step):
    return -(-value // step) * step


class Sizes:
    def __init__(self, planes, rows, strips, cols, devices, pitch):
        self.total = rows * strips
        self.planes, self.rows, self.cols, self.n, self.pitch = planes, rows, cols, devices, pitch
        self.w = cols // devices
        self.half = devices // 2
        assert cols % devices == 0 and self.w % pitch == 0 and self.w >= 2 * SIDE
        assert devices >= 2 and devices & (devices - 1) == 0 and rows >= 2 * RMAX and rows % 8 == 0
        self.wl = round_up(self.w, LANES)
        self.span = self.w + 2 * SIDE
        self.kp = round_up(self.span, LANES)
        self.kb = self.wl + 2 * LANES
        self.rp = round_up(rows, LANES)
        self.e = rows + 2 * RMAX
        self.ep = round_up(self.e, 32)
        self.el = round_up(self.ep, LANES)
        self.ar = round_up(max(self.span, self.wl) + pitch, pitch)
        self.starts = [LANES + b * self.w - SIDE for b in range(devices)]
        self.ka = round_up(max(s % LANES for s in self.starts) + self.span, LANES)
        self.xw = max(s // LANES * LANES for s in self.starts) + self.ka


def iota(shape, axis):
    return lax.broadcasted_iota(jnp.int32, shape, axis)


def phase_rows(sz, z, phase_ref, col_ref, t_ref, a_ref):
    taps = col_ref.shape[2]
    t_ref[...] = jnp.zeros_like(t_ref)
    for p in range(sz.pitch):
        row = col_ref[phase_ref[z, p], pl.ds(z, 1), :]
        t_ref[p : p + 1, 0:taps] = row.astype(BF16).astype(F32)
    base = t_ref[0 : sz.pitch, :]
    for k in range(sz.ar // sz.pitch):
        a_ref[k * sz.pitch : (k + 1) * sz.pitch, :] = base


def spread_matrix(sz, reach, a_ref):
    first = (-SIDE) % sz.pitch
    rows = a_ref[first : first + sz.span, 0 : sz.wl]
    rows = pltpu.roll(rows, sz.wl - RMAX - SIDE, 1, stride=1, stride_axis=0)
    col, row = iota(rows.shape, 1), iota(rows.shape, 0)
    return jnp.where((jnp.abs(col - row + SIDE) <= reach) & (col < sz.w), rows, 0.0)


def gather_matrix(sz, reach, a_ref):
    rows = pltpu.roll(a_ref[0 : sz.wl, 0 : sz.kp], SIDE - RMAX, 1, stride=1, stride_axis=0)
    col, row = iota(rows.shape, 1), iota(rows.shape, 0)
    rows = jnp.where((jnp.abs(col - SIDE - row) <= reach) & (row < sz.w), rows, 0.0)
    return rows.T[0 : sz.span, :]


def by_block(sz, matrix):
    def zeros(count):
        return [jnp.zeros((count, sz.wl), F32)] if count else []

    lead = sz.w - (sz.wl - LANES) - SIDE
    parts = [matrix[SIDE : SIDE + sz.w]] + zeros(sz.wl - sz.w)
    parts += [matrix[SIDE + sz.w :]] + zeros(LANES - SIDE)
    parts += zeros(lead) + [matrix[0:SIDE]] + zeros(sz.wl - sz.w)
    return jnp.concatenate(parts, axis=0).astype(BF16)


def row_matrix(sz, z, reach, row_ref):
    taps = row_ref.shape[1]
    lane = iota((1, sz.el), 1)
    row = row_ref[pl.ds(z, 1), :].astype(BF16).astype(F32)
    row = jnp.concatenate([row, jnp.zeros((1, sz.el - taps), F32)], axis=1)
    row = jnp.where(jnp.abs(lane - RMAX) <= reach, row, 0.0)
    wide = jnp.broadcast_to(row, (sz.rp, sz.el))
    wide = pltpu.roll(wide, 0, 1, stride=1, stride_axis=0)
    return jnp.where(iota(wide.shape, 0) < sz.rows, wide, 0.0)


def side_by_side(sz, ref, b, height):
    at = (b + 1) * height
    here = ref[at : at + height, :]
    after = ref[at + height : at + 2 * height, 0:LANES]
    before = ref[at - height : at, sz.wl - LANES :]
    return jnp.concatenate([here, after, before], axis=1)


def rows_forward(sz, me, rc_ref, s_ref, keep_ref, send_ref):
    core = lax.rem(me, 2)
    coef = rc_ref[...]
    for k in range(sz.half):
        for ref, block in ((send_ref, 2 * k + 1 - core), (keep_ref, 2 * k + core)):
            out = jnp.dot(coef, s_ref[block], preferred_element_type=F32)
            ref[k] = out.astype(ref.dtype)


def backward(sz, ratio_ref, matrix, rt, g_ref):
    for b in range(sz.n):
        window = side_by_side(sz, ratio_ref, b, sz.ep)
        out = jnp.dot(window, matrix, preferred_element_type=F32)
        g_ref[b, 0 : sz.ep, :] = out.astype(BF16)
    for b in range(sz.n):
        back = jnp.dot(rt, g_ref[b], preferred_element_type=F32)
        yield b, back[0 : sz.rows, :]


def block_norm(sz, b, icn):
    kind = 1 if b == 0 else 2 if b == sz.n - 1 else 0
    return icn[kind : kind + 1, :]


def place_ratio(sz, me, same_ref, other_ref, ratio_ref, g_ref):
    empty = jnp.zeros((sz.ep, sz.wl), BF16)
    ratio_ref[0 : sz.ep, :] = empty
    ratio_ref[(sz.n + 1) * sz.ep :, :] = empty
    g_ref[:, sz.ep :, :] = jnp.zeros((sz.n, sz.el - sz.ep, sz.wl), BF16)
    core = lax.rem(me, 2)
    for j in range(sz.half):
        chip = (me // 2) ^ j
        for ref, b in ((same_ref, 2 * chip + core), (other_ref, 2 * chip + 1 - core)):
            ratio_ref[pl.ds(pl.multiple_of((b + 1) * sz.ep, sz.ep), sz.ep), :] = ref[j]


def first_kernel(
    sz, me_ref, radius_hbm, phase_hbm, row_hbm, col_hbm, vol_hbm,
    rc_ref, keep_ref, send_ref,
    radius_ref, phase_ref, row_ref, col_ref, vol_ref, t_ref, a_ref, m_ref, x_ref, s_ref, sems,
):
    pairs = ((radius_hbm, radius_ref), (phase_hbm, phase_ref), (row_hbm, row_ref), (col_hbm, col_ref))
    small = [pltpu.make_async_copy(a, b, sems.at[i]) for i, (a, b) in enumerate(pairs)]
    large = [
        pltpu.make_async_copy(vol_hbm.at[z], vol_ref.at[z], sems.at[4 + z])
        for z in range(sz.planes)
    ]
    for copy in small + large:
        copy.start()
    m_ref[...] = jnp.zeros_like(m_ref)
    x_ref[...] = jnp.zeros_like(x_ref)
    for copy in small:
        copy.wait()
    for z in range(sz.planes):
        reach = radius_ref[z]
        phase_rows(sz, z, phase_ref, col_ref, t_ref, a_ref)
        matrix = spread_matrix(sz, reach, a_ref)
        rest = jnp.zeros((round_up(sz.span, 16) - sz.span, sz.wl), F32)
        matrix = jnp.concatenate([matrix, rest], axis=0) if rest.shape[0] else matrix
        m_ref[z, LANES : LANES + matrix.shape[0], :] = matrix.astype(BF16)
        rt = row_matrix(sz, z, reach, row_ref)
        rc_ref[:, z * sz.rp : (z + 1) * sz.rp] = rt.T[0 : sz.ep, :].astype(BF16)
    for z in range(sz.planes):
        large[z].wait()
        x = jnp.concatenate([vol_ref[z], jnp.zeros((sz.rp - sz.rows, sz.cols), F32)], axis=0)
        x_ref[z, :, LANES : LANES + sz.cols] = x.astype(BF16)
        for b, start in enumerate(sz.starts):
            shift = start % LANES
            window = x_ref[z, :, start - shift : start - shift + sz.ka]
            matrix = m_ref[z, LANES - shift : LANES - shift + sz.ka, :]
            out = jnp.dot(window, matrix, preferred_element_type=F32)
            s_ref[b, z * sz.rp : (z + 1) * sz.rp, :] = out.astype(BF16)
    rows_forward(sz, me_ref[0], rc_ref, s_ref, keep_ref, send_ref)


def table_kernel(
    sz, strip_ref, radius_hbm, phase_hbm, row_hbm, col_hbm, after_ref,
    wf_ref, wb_ref, rt_ref, irn_ref, icn_ref,
    radius_ref, phase_ref, row_ref, col_ref, t_ref, a_ref, sems,
):
    pairs = ((radius_hbm, radius_ref), (phase_hbm, phase_ref), (row_hbm, row_ref), (col_hbm, col_ref))
    small = [pltpu.make_async_copy(a, b, sems.at[i]) for i, (a, b) in enumerate(pairs)]
    for copy in small:
        copy.start()
    for copy in small:
        copy.wait()
    kind, col = iota((8, sz.kb), 0), iota((8, sz.kb), 1)
    after, before = (col >= sz.wl) & (col < sz.wl + LANES), col >= sz.wl + LANES
    ones = jnp.where(((kind == 1) & before) | ((kind == 2) & after), 0.0, 1.0).astype(BF16)
    for z in range(sz.planes):
        reach = radius_ref[z]
        phase_rows(sz, z, phase_ref, col_ref, t_ref, a_ref)
        wf_ref[z] = by_block(sz, spread_matrix(sz, reach, a_ref))
        matrix = by_block(sz, gather_matrix(sz, reach, a_ref))
        wb_ref[z] = matrix
        norm = jnp.dot(ones, matrix, preferred_element_type=F32)
        icn_ref[z] = jnp.where(norm > 0.0, 1.0 / norm, 0.0)
        rt = row_matrix(sz, z, reach, row_ref)
        rt_ref[z] = rt.astype(BF16)
        row = strip_ref[0] * sz.rows + iota(rt.shape, 1) - RMAX
        norm = jnp.sum(jnp.where((row >= 0) & (row < sz.total), rt, 0.0), axis=1, keepdims=True)
        irn_ref[z] = jnp.where(norm > 0.0, 1.0 / norm, 0.0)


def block_kernel(sz, vol_hbm, after_ref, blocks_ref, vol_ref, sems):
    copies = [
        pltpu.make_async_copy(vol_hbm.at[z], vol_ref.at[z], sems.at[z]) for z in range(sz.planes)
    ]
    for copy in copies:
        copy.start()
    for z, copy in enumerate(copies):
        copy.wait()
        for b in range(sz.n):
            block = vol_ref[z, :, b * sz.w : (b + 1) * sz.w]
            if sz.wl > sz.w:
                block = jnp.concatenate([block, jnp.zeros((sz.rows, sz.wl - sz.w), F32)], axis=1)
            blocks_ref[z, b] = block


def core_sum_kernel(sz, me_ref, keep_ref, recv_ref, own_ref, *out_refs):
    mine = me_ref[0] // 2
    own_ref[...] = keep_ref[mine] + recv_ref[mine].astype(F32)
    for j, ref in enumerate(out_refs, 1):
        other = mine ^ j
        ref[...] = (keep_ref[other] + recv_ref[other].astype(F32)).astype(BF16)


def chip_sum_kernel(sz, strip_ref, after_ref, own_ref, meas_ref, *refs):
    recv_refs, (sum_ref, first_ref, second_ref) = refs[:-3], refs[-3:]
    total = own_ref[...]
    for ref in recv_refs:
        total = total + ref[...].astype(F32)
    sum_ref[...] = total
    edges = []
    for first, row in ((0, 0), (sz.rows, sz.rows - SIDE)):
        meas = meas_ref[row : row + SIDE, :]
        high = meas.astype(BF16).astype(F32)
        edges.append(jnp.concatenate([total[first : first + 32, :], high, meas - high], axis=0))
    up, down = edges
    even = lax.rem(strip_ref[0], 2) == 0
    first_ref[...] = jnp.where(even, down, up).astype(BF16)
    second_ref[...] = jnp.where(even, up, down).astype(BF16)


def ratio_kernel(sz, strip_ref, sum_ref, meas_ref, first_ref, second_ref, ratio_ref, s_ref, m_ref):
    even = lax.rem(strip_ref[0], 2) == 0
    first, second = first_ref[...].astype(F32), second_ref[...].astype(F32)
    above, below = jnp.where(even, second, first), jnp.where(even, first, second)
    s_ref[...] = sum_ref[...]
    s_ref[0:32, :] += above[0:32, :]
    s_ref[sz.rows : sz.rows + 32, :] += below[0:32, :]
    m_ref[...] = jnp.zeros_like(m_ref)
    m_ref[RMAX : RMAX + sz.rows, :] = meas_ref[...]
    m_ref[0:RMAX, :] = (above[32:48, :] + above[48:64, :])[SIDE - RMAX :, :]
    m_ref[RMAX + sz.rows : sz.e, :] = (below[32:48, :] + below[48:64, :])[0:RMAX, :]
    row = iota(s_ref.shape, 0)
    spot = strip_ref[0] * sz.rows + row - RMAX
    inside = (row < sz.e) & (spot >= 0) & (spot < sz.total) & (iota(s_ref.shape, 1) < sz.w)
    ratio_ref[...] = jnp.where(inside, m_ref[...] / s_ref[...], 0.0).astype(BF16)


def stack_kernel(sz, after_ref, *refs):
    for j, ref in enumerate(refs[:-1]):
        refs[-1][j] = ref[...]


def middle_kernel(
    sz, me_ref, same_ref, other_ref, wf_ref, wb_ref, rt_ref, irn_ref, icn_ref, rc_ref, vol_ref,
    new_ref, keep_ref, send_ref, ratio_ref, g_ref, x_ref, s_ref,
):
    empty = jnp.zeros((sz.rp, sz.wl), BF16)
    x_ref[0 : sz.rp, :] = empty
    x_ref[(sz.n + 1) * sz.rp :, :] = empty
    place_ratio(sz, me_ref[0], same_ref, other_ref, ratio_ref, g_ref)
    lead = jnp.zeros((sz.rp - sz.rows, sz.wl), F32)

    def step(z, carry):
        icn, irn = icn_ref[z], irn_ref[z][0 : sz.rows]
        for b, back in backward(sz, ratio_ref, wb_ref[z], rt_ref[z], g_ref):
            new = vol_ref[z, b] * back * (irn * block_norm(sz, b, icn))
            new_ref[z, b] = new
            x_ref[(b + 1) * sz.rp : (b + 2) * sz.rp, :] = jnp.concatenate([new, lead]).astype(BF16)
        matrix = wf_ref[z]
        at = pl.ds(pl.multiple_of(z * sz.rp, sz.rp), sz.rp)
        for b in range(sz.n):
            window = side_by_side(sz, x_ref, b, sz.rp)
            out = jnp.dot(window, matrix, preferred_element_type=F32)
            s_ref[b, at, :] = out.astype(BF16)
        return carry

    for z in range(sz.planes):
        step(z, 0)
    rows_forward(sz, me_ref[0], rc_ref, s_ref, keep_ref, send_ref)


def last_kernel(
    sz, me_ref, same_ref, other_ref, wb_ref, rt_ref, irn_ref, icn_ref, vol_ref,
    out_hbm, ratio_ref, g_ref, out_ref, sems,
):
    place_ratio(sz, me_ref[0], same_ref, other_ref, ratio_ref, g_ref)

    def copy(z):
        return pltpu.make_async_copy(out_ref.at[z], out_hbm.at[z], sems.at[z])

    def step(z, carry):
        icn, irn = icn_ref[z], irn_ref[z][0 : sz.rows]
        for b, back in backward(sz, ratio_ref, wb_ref[z], rt_ref[z], g_ref):
            new = vol_ref[z, b] * back * (irn * block_norm(sz, b, icn))
            out_ref[z, :, b * sz.w : (b + 1) * sz.w] = new[:, 0 : sz.w]
        copy(z).start()
        return carry

    for z in range(sz.planes):
        step(z, 0)
    for z in range(sz.planes):
        copy(z).wait()


SMEM = pl.BlockSpec(memory_space=pltpu.SMEM)
VMEM = pl.BlockSpec(memory_space=pltpu.VMEM)
ANY = pl.BlockSpec(memory_space=pl.ANY)
HBM = pl.BlockSpec(memory_space=pltpu.HBM)


def shape(dims, dtype):
    return jax.ShapeDtypeStruct(dims, dtype)


def call(kernel, sz, name, in_specs, out_specs, out_shape, scratch, args, mib, micros=1):
    return pl.pallas_call(
        functools.partial(kernel, sz),
        in_specs=in_specs,
        out_specs=out_specs,
        out_shape=out_shape,
        scratch_shapes=scratch,
        compiler_params=pltpu.CompilerParams(vmem_limit_bytes=mib * 1024 * 1024),
        cost_estimate=pl.CostEstimate(
            flops=0, bytes_accessed=micros * 3_000_000, transcendentals=0
        ),
        name=name,
    )(*args)


def local(volume, measured, row_taps, col_taps, phase_map, radius):
    n = lax.axis_size("depth")
    strips = lax.axis_size("strip")
    planes, rows, cols = volume.shape
    sz = Sizes(planes, rows, strips, cols, n, phase_map.shape[1])
    me = lax.axis_index("depth")
    strip = lax.axis_index("strip")
    me_arg = me.reshape(1).astype(jnp.int32)
    strip_arg = strip.reshape(1).astype(jnp.int32)
    to_core = [(i, i ^ 1) for i in range(n)]
    to_chip = [[(i, i ^ (2 * j)) for i in range(n)] for j in range(1, sz.half)]
    swaps = []
    for start in (0, 1):
        below = [(i, i + 1) for i in range(start, strips - 1, 2)]
        swaps.append(below + [(b, a) for a, b in below])

    volume = pltpu.with_memory_space_constraint(volume, pltpu.HBM)
    meas = lax.dynamic_slice_in_dim(measured, me * sz.w, sz.w, axis=1)
    meas = jnp.pad(meas, ((0, 0), (0, sz.wl - sz.w)))
    by_family = col_taps.transpose(1, 0, 2)

    flat = shape((sz.ep, sz.wl), BF16)
    flat32 = shape((sz.ep, sz.wl), F32)
    edge = shape((64, sz.wl), BF16)
    halves = [shape((sz.half, sz.ep, sz.wl), F32), shape((sz.half, sz.ep, sz.wl), BF16)]
    blocked = shape((planes, n, rows, sz.wl), F32)
    tap_args = tuple(
        pltpu.with_memory_space_constraint(x, pltpu.HBM)
        for x in (radius, phase_map, row_taps, by_family)
    )
    tap_scratch = [
        pltpu.SMEM(radius.shape, jnp.int32),
        pltpu.SMEM(phase_map.shape, jnp.int32),
        pltpu.VMEM(row_taps.shape, F32),
        pltpu.VMEM(by_family.shape, F32),
    ]
    row_scratch = [
        pltpu.VMEM((round_up(sz.pitch, 8), sz.kp), F32),
        pltpu.VMEM((sz.ar, sz.kp), F32),
    ]
    s_scratch = pltpu.VMEM((n, planes * sz.rp, sz.wl), BF16)
    ratio_scratch = [
        pltpu.VMEM(((n + 2) * sz.ep, sz.wl), BF16),
        pltpu.VMEM((n, sz.el, sz.wl), BF16),
    ]
    vol_scratch = pltpu.VMEM(volume.shape, F32)

    rc, keep, send = call(
        first_kernel, sz, "first",
        [SMEM] + [HBM] * 5,
        [VMEM] * 3,
        [shape((sz.ep, planes * sz.rp), BF16), *halves],
        tap_scratch + [vol_scratch] + row_scratch
        + [
            pltpu.VMEM((planes, LANES + sz.ka, sz.wl), BF16),
            pltpu.VMEM((planes, sz.rp, sz.xw), BF16),
            s_scratch,
            pltpu.SemaphoreType.DMA((4 + planes,)),
        ],
        (me_arg, *tap_args, volume),
        24, 4,
    )

    tables, current = None, None
    for iteration in range(ITERS):
        recv = lax.ppermute(send, "depth", to_core)
        own, *sends = call(
            core_sum_kernel, sz, "core_sum",
            [SMEM, VMEM, VMEM],
            [VMEM] * sz.half,
            [flat32] + [flat] * (sz.half - 1),
            [], (me_arg, keep, recv), 4,
        )
        if tables is None:
            wf, *tables = call(
                table_kernel, sz, "tables",
                [SMEM] + [HBM] * 4 + [ANY],
                [VMEM] * 5,
                [
                    shape((planes, sz.kb, sz.wl), BF16),
                    shape((planes, sz.kb, sz.wl), BF16),
                    shape((planes, sz.rp, sz.el), BF16),
                    shape((planes, sz.rp, 1), F32),
                    shape((planes, 8, sz.wl), F32),
                ],
                tap_scratch + row_scratch + [pltpu.SemaphoreType.DMA((4,))],
                (strip_arg, *tap_args, own),
                8, 2,
            )
        recvs = [lax.ppermute(part, "depth", pairs) for part, pairs in zip(sends, to_chip)]
        total, *edges = call(
            chip_sum_kernel, sz, "chip_sum",
            [SMEM, ANY] + [VMEM] * (2 + len(recvs)),
            [VMEM] * 3,
            [flat32, edge, edge],
            [], (strip_arg, tables[3], own, meas, *recvs), 4,
        )
        edges = [lax.ppermute(part, "strip", pairs) for part, pairs in zip(edges, swaps)]
        ratio = call(
            ratio_kernel, sz, "ratio",
            [SMEM] + [VMEM] * 4,
            VMEM,
            flat,
            [pltpu.VMEM((sz.ep, sz.wl), F32)] * 2,
            (strip_arg, total, meas, *edges), 4,
        )
        chips = [lax.ppermute(ratio, "depth", pairs) for pairs in to_chip]
        if iteration == 0:
            current = call(
                block_kernel, sz, "blocks",
                [HBM, ANY], VMEM, blocked,
                [vol_scratch, pltpu.SemaphoreType.DMA((planes,))],
                (volume, ratio), 12, 3,
            )
        same = call(
            stack_kernel, sz, "stack",
            [ANY] + [VMEM] * sz.half, VMEM, halves[1],
            [], (current, ratio, *chips), 4,
        )
        other = lax.ppermute(same, "depth", to_core)
        if iteration < ITERS - 1:
            current, keep, send = call(
                middle_kernel, sz, "middle",
                [SMEM] + [VMEM] * 9,
                [VMEM] * 3,
                [blocked, *halves],
                ratio_scratch + [pltpu.VMEM(((n + 2) * sz.rp, sz.wl), BF16), s_scratch],
                (me_arg, same, other, wf, *tables, rc, current),
                16, 5,
            )
        else:
            current = call(
                last_kernel, sz, "last",
                [SMEM] + [VMEM] * 7,
                HBM,
                shape(volume.shape, F32),
                ratio_scratch + [vol_scratch, pltpu.SemaphoreType.DMA((planes,))],
                (me_arg, same, other, *tables, current),
                16, 5,
            )
    return current


def solution(mesh):
    return jax.shard_map(
        local,
        mesh=mesh,
        in_specs=(
            P("depth", "strip", None),
            P("strip", None),
            P("depth", None),
            P("depth", None, None),
            P("depth", None),
            P("depth"),
        ),
        out_specs=P("depth", "strip", None),
        check_vma=False,
    )
```

```python
import functools

import jax
import jax.numpy as jnp
from jax import lax
from jax.experimental import pallas as pl
from jax.experimental.pallas import tpu as pltpu
from jax.sharding import PartitionSpec as P

RMAX = 15
ITERS = 2
SIDE = 16
LANES = 128

F32 = jnp.float32
BF16 = jnp.bfloat16


def round_up(value, step):
    return -(-value // step) * step


class Sizes:
    def __init__(self, planes, rows, strips, cols, devices, pitch):
        self.total = rows * strips
        self.planes, self.rows, self.cols, self.n, self.pitch = planes, rows, cols, devices, pitch
        self.w = cols // devices
        self.half = devices // 2
        assert cols % devices == 0 and self.w % pitch == 0 and self.w >= 2 * SIDE
        assert devices >= 4 and devices & (devices - 1) == 0 and rows >= 2 * RMAX and rows % 8 == 0
        self.wl = round_up(self.w, LANES)
        self.span = self.w + 2 * SIDE
        self.kp = round_up(self.span, LANES)
        self.kb = self.wl + 2 * LANES
        self.rp = round_up(rows, LANES)
        self.e = rows + 2 * RMAX
        self.ep = round_up(self.e, 32)
        self.hr = self.ep // 2
        self.el = round_up(self.ep, LANES)
        assert 32 <= rows - self.hr and rows - self.hr + 32 <= self.hr and (rows - self.hr) % 8 == 0
        self.ar = round_up(max(self.span, self.wl) + pitch, pitch)
        self.starts = [LANES + b * self.w - SIDE for b in range(devices)]
        self.ka = round_up(max(s % LANES for s in self.starts) + self.span, LANES)
        self.xw = max(s // LANES * LANES for s in self.starts) + self.ka


def iota(shape, axis):
    return lax.broadcasted_iota(jnp.int32, shape, axis)


def phase_rows(sz, z, phase_ref, col_ref, t_ref, a_ref):
    taps = col_ref.shape[2]
    t_ref[...] = jnp.zeros_like(t_ref)
    for p in range(sz.pitch):
        row = col_ref[phase_ref[z, p], pl.ds(z, 1), :]
        t_ref[p : p + 1, 0:taps] = row.astype(BF16).astype(F32)
    base = t_ref[0 : sz.pitch, :]
    for k in range(sz.ar // sz.pitch):
        a_ref[k * sz.pitch : (k + 1) * sz.pitch, :] = base


def spread_matrix(sz, reach, a_ref):
    first = (-SIDE) % sz.pitch
    rows = a_ref[first : first + sz.span, 0 : sz.wl]
    rows = pltpu.roll(rows, sz.wl - RMAX - SIDE, 1, stride=1, stride_axis=0)
    col, row = iota(rows.shape, 1), iota(rows.shape, 0)
    return jnp.where((jnp.abs(col - row + SIDE) <= reach) & (col < sz.w), rows, 0.0)


def gather_matrix(sz, reach, a_ref):
    rows = pltpu.roll(a_ref[0 : sz.wl, 0 : sz.kp], SIDE - RMAX, 1, stride=1, stride_axis=0)
    col, row = iota(rows.shape, 1), iota(rows.shape, 0)
    rows = jnp.where((jnp.abs(col - SIDE - row) <= reach) & (row < sz.w), rows, 0.0)
    return rows.T[0 : sz.span, :]


def by_block(sz, matrix):
    def zeros(count):
        return [jnp.zeros((count, sz.wl), F32)] if count else []

    lead = sz.w - (sz.wl - LANES) - SIDE
    parts = [matrix[SIDE : SIDE + sz.w]] + zeros(sz.wl - sz.w)
    parts += [matrix[SIDE + sz.w :]] + zeros(LANES - SIDE)
    parts += zeros(lead) + [matrix[0:SIDE]] + zeros(sz.wl - sz.w)
    return jnp.concatenate(parts, axis=0).astype(BF16)


def row_matrix(sz, z, reach, row_ref):
    taps = row_ref.shape[1]
    lane = iota((1, sz.el), 1)
    row = row_ref[pl.ds(z, 1), :].astype(BF16).astype(F32)
    row = jnp.concatenate([row, jnp.zeros((1, sz.el - taps), F32)], axis=1)
    row = jnp.where(jnp.abs(lane - RMAX) <= reach, row, 0.0)
    wide = jnp.broadcast_to(row, (sz.rp, sz.el))
    wide = pltpu.roll(wide, 0, 1, stride=1, stride_axis=0)
    return jnp.where(iota(wide.shape, 0) < sz.rows, wide, 0.0)


def side_by_side(sz, ref, b, height):
    at = (b + 1) * height
    here = ref[at : at + height, :]
    after = ref[at + height : at + 2 * height, 0:LANES]
    before = ref[at - height : at, sz.wl - LANES :]
    return jnp.concatenate([here, after, before], axis=1)


def rows_forward(sz, rc_ref, s_ref, keep_ref, send_ref):
    coef = rc_ref[...]
    for b in range(sz.n):
        out = jnp.dot(coef, s_ref[b], preferred_element_type=F32)
        send_ref[b] = out[0 : sz.hr, :].astype(BF16)
        keep_ref[b] = out[sz.hr :, :]


def backward(sz, ratio_ref, matrix, rt, g_ref):
    for b in range(sz.n):
        window = side_by_side(sz, ratio_ref, b, sz.ep)
        out = jnp.dot(window, matrix, preferred_element_type=F32)
        g_ref[b, 0 : sz.ep, :] = out.astype(BF16)
    for b in range(sz.n):
        back = jnp.dot(rt, g_ref[b], preferred_element_type=F32)
        yield b, back[0 : sz.rows, :]


def block_norm(sz, b, icn):
    kind = 1 if b == 0 else 2 if b == sz.n - 1 else 0
    return icn[kind : kind + 1, :]


def place_ratio(sz, me, same_ref, other_ref, ratio_ref, g_ref):
    empty = jnp.zeros((sz.ep, sz.wl), BF16)
    ratio_ref[0 : sz.ep, :] = empty
    ratio_ref[(sz.n + 1) * sz.ep :, :] = empty
    g_ref[:, sz.ep :, :] = jnp.zeros((sz.n, sz.el - sz.ep, sz.wl), BF16)
    part = lax.rem(me, 2)
    for j in range(sz.half):
        chip = (me // 2) ^ j
        for ref, rows in ((same_ref, part), (other_ref, 1 - part)):
            for k in range(2):
                at = (2 * chip + k + 1) * sz.ep + rows * sz.hr
                ratio_ref[pl.ds(pl.multiple_of(at, sz.hr), sz.hr), :] = ref[j, k]


def first_kernel(
    sz, me_ref, radius_hbm, phase_hbm, row_hbm, col_hbm, vol_hbm,
    rc_ref, keep_ref, send_ref,
    radius_ref, phase_ref, row_ref, col_ref, vol_ref, t_ref, a_ref, m_ref, x_ref, s_ref, sems,
):
    pairs = ((radius_hbm, radius_ref), (phase_hbm, phase_ref), (row_hbm, row_ref), (col_hbm, col_ref))
    small = [pltpu.make_async_copy(a, b, sems.at[i]) for i, (a, b) in enumerate(pairs)]
    large = [
        pltpu.make_async_copy(vol_hbm.at[z], vol_ref.at[z], sems.at[4 + z])
        for z in range(sz.planes)
    ]
    for copy in small + large:
        copy.start()
    part = lax.rem(me_ref[0], 2)
    m_ref[...] = jnp.zeros_like(m_ref)
    x_ref[...] = jnp.zeros_like(x_ref)
    for copy in small:
        copy.wait()
    for z in range(sz.planes):
        reach = radius_ref[z]
        phase_rows(sz, z, phase_ref, col_ref, t_ref, a_ref)
        matrix = spread_matrix(sz, reach, a_ref)
        rest = jnp.zeros((round_up(sz.span, 16) - sz.span, sz.wl), F32)
        matrix = jnp.concatenate([matrix, rest], axis=0) if rest.shape[0] else matrix
        m_ref[z, LANES : LANES + matrix.shape[0], :] = matrix.astype(BF16)
        rt = row_matrix(sz, z, reach, row_ref)
        rt = rt.T.astype(BF16)
        lanes = slice(z * sz.rp, (z + 1) * sz.rp)
        rc_ref[pl.ds(pl.multiple_of((1 - part) * sz.hr, sz.hr), sz.hr), lanes] = rt[0 : sz.hr, :]
        rc_ref[pl.ds(pl.multiple_of(part * sz.hr, sz.hr), sz.hr), lanes] = rt[sz.hr : sz.ep, :]
    for z in range(sz.planes):
        large[z].wait()
        x = jnp.concatenate([vol_ref[z], jnp.zeros((sz.rp - sz.rows, sz.cols), F32)], axis=0)
        x_ref[z, :, LANES : LANES + sz.cols] = x.astype(BF16)
        for b, start in enumerate(sz.starts):
            shift = start % LANES
            window = x_ref[z, :, start - shift : start - shift + sz.ka]
            matrix = m_ref[z, LANES - shift : LANES - shift + sz.ka, :]
            out = jnp.dot(window, matrix, preferred_element_type=F32)
            s_ref[b, z * sz.rp : (z + 1) * sz.rp, :] = out.astype(BF16)
    rows_forward(sz, rc_ref, s_ref, keep_ref, send_ref)


def table_kernel(
    sz, strip_ref, radius_hbm, phase_hbm, row_hbm, col_hbm, after_ref,
    wf_ref, wb_ref, rt_ref, irn_ref, icn_ref,
    radius_ref, phase_ref, row_ref, col_ref, t_ref, a_ref, sems,
):
    pairs = ((radius_hbm, radius_ref), (phase_hbm, phase_ref), (row_hbm, row_ref), (col_hbm, col_ref))
    small = [pltpu.make_async_copy(a, b, sems.at[i]) for i, (a, b) in enumerate(pairs)]
    for copy in small:
        copy.start()
    for copy in small:
        copy.wait()
    kind, col = iota((8, sz.kb), 0), iota((8, sz.kb), 1)
    after, before = (col >= sz.wl) & (col < sz.wl + LANES), col >= sz.wl + LANES
    ones = jnp.where(((kind == 1) & before) | ((kind == 2) & after), 0.0, 1.0).astype(BF16)
    for z in range(sz.planes):
        reach = radius_ref[z]
        phase_rows(sz, z, phase_ref, col_ref, t_ref, a_ref)
        wf_ref[z] = by_block(sz, spread_matrix(sz, reach, a_ref))
        matrix = by_block(sz, gather_matrix(sz, reach, a_ref))
        wb_ref[z] = matrix
        norm = jnp.dot(ones, matrix, preferred_element_type=F32)
        icn_ref[z] = jnp.where(norm > 0.0, 1.0 / norm, 0.0)
        rt = row_matrix(sz, z, reach, row_ref)
        rt_ref[z] = rt.astype(BF16)
        row = strip_ref[0] * sz.rows + iota(rt.shape, 1) - RMAX
        norm = jnp.sum(jnp.where((row >= 0) & (row < sz.total), rt, 0.0), axis=1, keepdims=True)
        irn_ref[z] = jnp.where(norm > 0.0, 1.0 / norm, 0.0)


def block_kernel(sz, vol_hbm, after_ref, blocks_ref, vol_ref, sems):
    copies = [
        pltpu.make_async_copy(vol_hbm.at[z], vol_ref.at[z], sems.at[z]) for z in range(sz.planes)
    ]
    for copy in copies:
        copy.start()
    for z, copy in enumerate(copies):
        copy.wait()
        for b in range(sz.n):
            block = vol_ref[z, :, b * sz.w : (b + 1) * sz.w]
            if sz.wl > sz.w:
                block = jnp.concatenate([block, jnp.zeros((sz.rows, sz.wl - sz.w), F32)], axis=1)
            blocks_ref[z, b] = block


def core_sum_kernel(sz, me_ref, keep_ref, recv_ref, own_ref, *out_refs):
    mine = me_ref[0] // 2
    for j, ref in enumerate((own_ref, *out_refs)):
        blocks = pl.ds(2 * (mine ^ j), 2)
        ref[...] = (keep_ref[blocks] + recv_ref[blocks].astype(F32)).astype(ref.dtype)


def chip_sum_kernel(sz, me_ref, after_ref, own_ref, meas_ref, *refs, first):
    recv_refs, (sum_ref, edge_ref) = refs[:-2], refs[-2:]
    total = own_ref[...]
    for ref in recv_refs:
        total = total + ref[...].astype(F32)
    sum_ref[...] = total
    edges = []
    for at, row in ((0, 0), (sz.rows - sz.hr, sz.rows - SIDE)):
        parts = [total[:, at : at + 32, :]]
        if first:
            meas = meas_ref[:, row : row + SIDE, :]
            high = meas.astype(BF16).astype(F32)
            parts += [high, meas - high]
        edges.append(jnp.concatenate(parts, axis=1))
    top, bottom = edges
    edge_ref[...] = jnp.where(lax.rem(me_ref[0], 2) == 0, top, bottom).astype(BF16)


def ratio_kernel(
    sz, me_ref, strip_ref, sum_ref, meas_ref, edge_ref, first_edge_ref, ratio_ref, s_ref, m_ref
):
    part = lax.rem(me_ref[0], 2)
    s_ref[...] = sum_ref[...]
    m_ref[...] = jnp.zeros_like(m_ref)
    edge, first_edge = edge_ref[...].astype(F32), first_edge_ref[...].astype(F32)
    alone = jnp.where(part == 0, strip_ref[0] == 0, (strip_ref[0] + 1) * sz.rows == sz.total)
    rows = jnp.where(alone, 0.0, edge[:, 0:32, :])
    meas = first_edge[:, 32:48, :] + first_edge[:, 48:64, :]

    @pl.when(part == 0)
    def _():
        s_ref[:, 0:32, :] += rows
        m_ref[:, 0:RMAX, :] = meas[:, SIDE - RMAX :, :]
        m_ref[:, RMAX : sz.hr, :] = meas_ref[:, 0 : sz.hr - RMAX, :]

    @pl.when(part == 1)
    def _():
        first = sz.rows - sz.hr
        s_ref[:, first : first + 32, :] += rows
        m_ref[:, 0 : first + RMAX, :] = meas_ref[:, sz.hr - RMAX :, :]
        m_ref[:, first + RMAX : first + 2 * RMAX, :] = meas[:, 0:RMAX, :]

    row = part * sz.hr + iota(s_ref.shape, 1)
    spot = strip_ref[0] * sz.rows + row - RMAX
    inside = (row < sz.e) & (spot >= 0) & (spot < sz.total) & (iota(s_ref.shape, 2) < sz.w)
    ratio_ref[...] = jnp.where(inside, m_ref[...] / s_ref[...], 0.0).astype(BF16)


def stack_kernel(sz, after_ref, *refs):
    for j, ref in enumerate(refs[:-1]):
        refs[-1][j] = ref[...]


def middle_kernel(
    sz, me_ref, same_ref, other_ref, wf_ref, wb_ref, rt_ref, irn_ref, icn_ref, rc_ref, vol_ref,
    new_ref, keep_ref, send_ref, ratio_ref, g_ref, x_ref, s_ref,
):
    empty = jnp.zeros((sz.rp, sz.wl), BF16)
    x_ref[0 : sz.rp, :] = empty
    x_ref[(sz.n + 1) * sz.rp :, :] = empty
    place_ratio(sz, me_ref[0], same_ref, other_ref, ratio_ref, g_ref)
    lead = jnp.zeros((sz.rp - sz.rows, sz.wl), F32)

    def step(z, carry):
        icn, irn = icn_ref[z], irn_ref[z][0 : sz.rows]
        for b, back in backward(sz, ratio_ref, wb_ref[z], rt_ref[z], g_ref):
            new = vol_ref[z, b] * back * (irn * block_norm(sz, b, icn))
            new_ref[z, b] = new
            x_ref[(b + 1) * sz.rp : (b + 2) * sz.rp, :] = jnp.concatenate([new, lead]).astype(BF16)
        matrix = wf_ref[z]
        at = pl.ds(pl.multiple_of(z * sz.rp, sz.rp), sz.rp)
        for b in range(sz.n):
            window = side_by_side(sz, x_ref, b, sz.rp)
            out = jnp.dot(window, matrix, preferred_element_type=F32)
            s_ref[b, at, :] = out.astype(BF16)
        return carry

    for z in range(sz.planes):
        step(z, 0)
    rows_forward(sz, rc_ref, s_ref, keep_ref, send_ref)


def last_kernel(
    sz, me_ref, same_ref, other_ref, wb_ref, rt_ref, irn_ref, icn_ref, vol_ref,
    out_hbm, ratio_ref, g_ref, out_ref, sems,
):
    place_ratio(sz, me_ref[0], same_ref, other_ref, ratio_ref, g_ref)

    def copy(z):
        return pltpu.make_async_copy(out_ref.at[z], out_hbm.at[z], sems.at[z])

    def step(z, carry):
        icn, irn = icn_ref[z], irn_ref[z][0 : sz.rows]
        for b, back in backward(sz, ratio_ref, wb_ref[z], rt_ref[z], g_ref):
            new = vol_ref[z, b] * back * (irn * block_norm(sz, b, icn))
            out_ref[z, :, b * sz.w : (b + 1) * sz.w] = new[:, 0 : sz.w]
        copy(z).start()
        return carry

    for z in range(sz.planes):
        step(z, 0)
    for z in range(sz.planes):
        copy(z).wait()


SMEM = pl.BlockSpec(memory_space=pltpu.SMEM)
VMEM = pl.BlockSpec(memory_space=pltpu.VMEM)
ANY = pl.BlockSpec(memory_space=pl.ANY)
HBM = pl.BlockSpec(memory_space=pltpu.HBM)


def shape(dims, dtype):
    return jax.ShapeDtypeStruct(dims, dtype)


def call(kernel, sz, name, in_specs, out_specs, out_shape, scratch, args, mib, micros=1):
    return pl.pallas_call(
        functools.partial(kernel, sz),
        in_specs=in_specs,
        out_specs=out_specs,
        out_shape=out_shape,
        scratch_shapes=scratch,
        compiler_params=pltpu.CompilerParams(vmem_limit_bytes=mib * 1024 * 1024),
        cost_estimate=pl.CostEstimate(
            flops=0, bytes_accessed=micros * 3_000_000, transcendentals=0
        ),
        name=name,
    )(*args)


def local(volume, measured, row_taps, col_taps, phase_map, radius):
    n = lax.axis_size("depth")
    strips = lax.axis_size("strip")
    planes, rows, cols = volume.shape
    sz = Sizes(planes, rows, strips, cols, n, phase_map.shape[1])
    me = lax.axis_index("depth")
    strip = lax.axis_index("strip")
    me_arg = (me ^ (strip % 2)).reshape(1).astype(jnp.int32)
    strip_arg = strip.reshape(1).astype(jnp.int32)
    to_core = [(i, i ^ 1) for i in range(n)]
    to_chip = [[(i, i ^ (2 * j)) for i in range(n)] for j in range(1, sz.half)]
    to_strip = []
    for chip in range(sz.half):
        for lower in range(1, strips):
            row = (2 * chip + lower % 2) * strips
            to_strip += [(row + lower, row + lower - 1), (row + lower - 1, row + lower)]
        for edge, core in ((0, 0), (strips - 1, strips % 2)):
            pair = [(2 * c + core) * strips + edge for c in (chip, chip ^ 1)]
            to_strip.append(tuple(pair))

    volume = pltpu.with_memory_space_constraint(volume, pltpu.HBM)
    meas = lax.dynamic_slice_in_dim(measured, (me // 2) * 2 * sz.w, 2 * sz.w, axis=1)
    meas = jnp.stack([meas[:, 0 : sz.w], meas[:, sz.w :]])
    meas = jnp.pad(meas, ((0, 0), (0, 0), (0, sz.wl - sz.w)))
    by_family = col_taps.transpose(1, 0, 2)

    flat = shape((2, sz.hr, sz.wl), BF16)
    flat32 = shape((2, sz.hr, sz.wl), F32)
    halves = [shape((n, sz.hr, sz.wl), F32), shape((n, sz.hr, sz.wl), BF16)]
    blocked = shape((planes, n, rows, sz.wl), F32)
    tap_args = tuple(
        pltpu.with_memory_space_constraint(x, pltpu.HBM)
        for x in (radius, phase_map, row_taps, by_family)
    )
    tap_scratch = [
        pltpu.SMEM(radius.shape, jnp.int32),
        pltpu.SMEM(phase_map.shape, jnp.int32),
        pltpu.VMEM(row_taps.shape, F32),
        pltpu.VMEM(by_family.shape, F32),
    ]
    row_scratch = [
        pltpu.VMEM((round_up(sz.pitch, 8), sz.kp), F32),
        pltpu.VMEM((sz.ar, sz.kp), F32),
    ]
    s_scratch = pltpu.VMEM((n, planes * sz.rp, sz.wl), BF16)
    ratio_scratch = [
        pltpu.VMEM(((n + 2) * sz.ep, sz.wl), BF16),
        pltpu.VMEM((n, sz.el, sz.wl), BF16),
    ]
    vol_scratch = pltpu.VMEM(volume.shape, F32)

    rc, keep, send = call(
        first_kernel, sz, "first",
        [SMEM] + [HBM] * 5,
        [VMEM] * 3,
        [shape((sz.ep, planes * sz.rp), BF16), *halves],
        tap_scratch + [vol_scratch] + row_scratch
        + [
            pltpu.VMEM((planes, LANES + sz.ka, sz.wl), BF16),
            pltpu.VMEM((planes, sz.rp, sz.xw), BF16),
            s_scratch,
            pltpu.SemaphoreType.DMA((4 + planes,)),
        ],
        (me_arg, *tap_args, volume),
        24, 4,
    )

    tables, current = None, None
    for iteration in range(ITERS):
        recv = lax.ppermute(send, "depth", to_core)
        own, *sends = call(
            core_sum_kernel, sz, "core_sum",
            [SMEM, VMEM, VMEM],
            [VMEM] * sz.half,
            [flat32] + [flat] * (sz.half - 1),
            [], (me_arg, keep, recv), 4,
        )
        if tables is None:
            wf, *tables = call(
                table_kernel, sz, "tables",
                [SMEM] + [HBM] * 4 + [ANY],
                [VMEM] * 5,
                [
                    shape((planes, sz.kb, sz.wl), BF16),
                    shape((planes, sz.kb, sz.wl), BF16),
                    shape((planes, sz.rp, sz.el), BF16),
                    shape((planes, sz.rp, 1), F32),
                    shape((planes, 8, sz.wl), F32),
                ],
                tap_scratch + row_scratch + [pltpu.SemaphoreType.DMA((4,))],
                (strip_arg, *tap_args, own),
                8, 2,
            )
        recvs = [lax.ppermute(part, "depth", pairs) for part, pairs in zip(sends, to_chip)][::-1]
        total, edge = call(
            functools.partial(chip_sum_kernel, first=iteration == 0), sz, "chip_sum",
            [SMEM, ANY] + [VMEM] * (2 + len(recvs)),
            [VMEM] * 2,
            [flat32, shape((2, 64 if iteration == 0 else 32, sz.wl), BF16)],
            [], (me_arg, tables[3], own, meas, *recvs), 4,
        )
        edge = lax.ppermute(edge, ("depth", "strip"), to_strip)
        first_edge = edge if iteration == 0 else first_edge
        ratio = call(
            ratio_kernel, sz, "ratio",
            [SMEM] * 2 + [VMEM] * 4,
            VMEM,
            flat,
            [pltpu.VMEM(flat32.shape, F32)] * 2,
            (me_arg, strip_arg, total, meas, edge, first_edge), 4,
        )
        chips = [lax.ppermute(ratio, "depth", pairs) for pairs in to_chip]
        if iteration == 0:
            current = call(
                block_kernel, sz, "blocks",
                [HBM, ANY], VMEM, blocked,
                [vol_scratch, pltpu.SemaphoreType.DMA((planes,))],
                (volume, ratio), 12, 3,
            )
        same = call(
            stack_kernel, sz, "stack",
            [ANY] + [VMEM] * sz.half, VMEM, shape((sz.half,) + flat.shape, BF16),
            [], (current, ratio, *chips), 4,
        )
        other = lax.ppermute(same, "depth", to_core)
        if iteration < ITERS - 1:
            current, keep, send = call(
                middle_kernel, sz, "middle",
                [SMEM] + [VMEM] * 9,
                [VMEM] * 3,
                [blocked, *halves],
                ratio_scratch + [pltpu.VMEM(((n + 2) * sz.rp, sz.wl), BF16), s_scratch],
                (me_arg, same, other, wf, *tables, rc, current),
                16, 5,
            )
        else:
            current = call(
                last_kernel, sz, "last",
                [SMEM] + [VMEM] * 7,
                HBM,
                shape(volume.shape, F32),
                ratio_scratch + [vol_scratch, pltpu.SemaphoreType.DMA((planes,))],
                (me_arg, same, other, *tables, current),
                16, 5,
            )
    return current


def solution(mesh):
    return jax.shard_map(
        local,
        mesh=mesh,
        in_specs=(
            P("depth", "strip", None),
            P("strip", None),
            P("depth", None),
            P("depth", None, None),
            P("depth", None),
            P("depth"),
        ),
        out_specs=P("depth", "strip", None),
        check_vma=False,
    )
```

```python
import functools

import jax
import jax.numpy as jnp
from jax import lax
from jax.experimental import pallas as pl
from jax.experimental.pallas import tpu as pltpu
from jax.sharding import PartitionSpec as P

RMAX = 15
ITERS = 2
SIDE = 16
LANES = 128
HALF = LANES // 2
GROUP = 2

F32 = jnp.float32
BF16 = jnp.bfloat16


def round_up(value, step):
    return -(-value // step) * step


class Sizes:
    def __init__(self, planes, rows, strips, cols, devices, pitch):
        self.total = rows * strips
        self.planes, self.rows, self.cols, self.n, self.pitch = planes, rows, cols, devices, pitch
        self.w = cols // devices
        self.half = devices // 2
        assert cols % devices == 0 and self.w % pitch == 0 and self.w >= 2 * SIDE
        assert devices >= 4 and devices & (devices - 1) == 0 and rows >= 2 * RMAX and rows % 8 == 0
        self.wl = round_up(self.w, LANES)
        self.span = self.w + 2 * SIDE
        self.kp = round_up(self.span, LANES)
        self.kb = self.wl + LANES
        self.group = 1 if devices % GROUP else GROUP
        self.rp = round_up(rows, LANES)
        self.e = rows + 2 * RMAX
        self.ep = round_up(self.e, 32)
        self.hr = self.ep // 2
        self.hp = round_up(self.hr, LANES)
        self.el = round_up(self.ep, LANES)
        assert self.el == 2 * self.hp
        assert 32 <= rows - self.hr and rows - self.hr + 32 <= self.hr and (rows - self.hr) % 8 == 0
        self.ar = round_up(max(self.span, self.wl) + pitch, pitch)
        self.starts = [LANES + b * self.w - SIDE for b in range(devices)]
        self.ka = round_up(max(s % LANES for s in self.starts) + self.span, LANES)
        self.xw = max(s // LANES * LANES for s in self.starts) + self.ka


def iota(shape, axis):
    return lax.broadcasted_iota(jnp.int32, shape, axis)


def phase_rows(sz, z, phase_ref, col_ref, t_ref, a_ref):
    taps = col_ref.shape[2]
    t_ref[...] = jnp.zeros_like(t_ref)
    for p in range(sz.pitch):
        row = col_ref[phase_ref[z, p], pl.ds(z, 1), :]
        t_ref[p : p + 1, 0:taps] = row.astype(BF16).astype(F32)
    base = t_ref[0 : sz.pitch, :]
    for k in range(sz.ar // sz.pitch):
        a_ref[k * sz.pitch : (k + 1) * sz.pitch, :] = base


def spread_matrix(sz, reach, a_ref):
    first = (-SIDE) % sz.pitch
    rows = a_ref[first : first + sz.span, 0 : sz.wl]
    rows = pltpu.roll(rows, sz.wl - RMAX - SIDE, 1, stride=1, stride_axis=0)
    col, row = iota(rows.shape, 1), iota(rows.shape, 0)
    return jnp.where((jnp.abs(col - row + SIDE) <= reach) & (col < sz.w), rows, 0.0)


def gather_matrix(sz, reach, a_ref):
    rows = pltpu.roll(a_ref[0 : sz.wl, 0 : sz.kp], SIDE - RMAX, 1, stride=1, stride_axis=0)
    col, row = iota(rows.shape, 1), iota(rows.shape, 0)
    rows = jnp.where((jnp.abs(col - SIDE - row) <= reach) & (row < sz.w), rows, 0.0)
    return rows.T[0 : sz.span, :]


def by_block(sz, matrix):
    def zeros(count):
        return [jnp.zeros((count, sz.wl), F32)] if count else []

    lead = sz.w - (sz.wl - LANES) - 2 * SIDE
    parts = [matrix[SIDE : SIDE + sz.w]] + zeros(sz.wl - sz.w)
    parts += [matrix[SIDE + sz.w :]] + zeros(lead) + [matrix[0:SIDE]] + zeros(sz.wl - sz.w)
    return jnp.concatenate(parts, axis=0).astype(BF16)


def row_matrix(sz, z, reach, row_ref):
    taps = row_ref.shape[1]
    lane = iota((1, sz.el), 1)
    row = row_ref[pl.ds(z, 1), :].astype(BF16).astype(F32)
    row = jnp.concatenate([row, jnp.zeros((1, sz.el - taps), F32)], axis=1)
    row = jnp.where(jnp.abs(lane - RMAX) <= reach, row, 0.0)
    wide = jnp.broadcast_to(row, (sz.rp, sz.el))
    wide = pltpu.roll(wide, 0, 1, stride=1, stride_axis=0)
    return jnp.where(iota(wide.shape, 0) < sz.rows, wide, 0.0)


class Windows:
    def __init__(self, sz, height, main_ref, side_ref):
        self.sz, self.height, self.main, self.side = sz, height, main_ref, side_ref

    def clear_sides(self):
        self.side[...] = jnp.zeros_like(self.side)

    def put(self, b, row, x):
        sz = self.sz

        def rows(block):
            at = block * self.height + row
            if not isinstance(at, int):
                at = pl.multiple_of(at, 16)
            return pl.ds(at, x.shape[0])

        self.main[rows(b), :] = x
        self.side[rows(b), 0:HALF] = x[:, 0:HALF]
        self.side[rows(b + 2), HALF:] = x[:, sz.wl - HALF :]

    def products(self, matrix):
        sz, height = self.sz, self.height
        for first in range(0, sz.n, sz.group):
            count = sz.group * height
            main = self.main[first * height : first * height + count, :]
            side = self.side[(first + 1) * height : (first + 1) * height + count, :]
            window = jnp.concatenate([main, side], axis=1)
            out = jnp.dot(window, matrix, preferred_element_type=F32).astype(BF16)
            for k in range(sz.group):
                yield first + k, out[k * height : (k + 1) * height, :]


def rows_forward(sz, rc_ref, s_ref, keep_ref, send_ref):
    coef = rc_ref[...]
    for b in range(sz.n):
        out = jnp.dot(coef, s_ref[b], preferred_element_type=F32)
        send_ref[b] = out[0 : sz.hr, :].astype(BF16)
        keep_ref[b] = out[sz.hr :, :]


def backward(sz, z, ratio, matrix, rt, own_ref, g_ref):
    for b, out in ratio.products(matrix):
        g_ref[b, 0 : sz.hr, :] = out
    for b in range(sz.n):
        rows = jnp.concatenate([own_ref[z, b], g_ref[b]], axis=0)
        back = jnp.dot(rt, rows, preferred_element_type=F32)
        yield b, back[0 : sz.rows, :]


def block_norm(sz, b, icn):
    kind = 1 if b == 0 else 2 if b == sz.n - 1 else 0
    return icn[kind : kind + 1, :]


def place_ratio(sz, me, stack_ref, main_ref, side_ref):
    ratio = Windows(sz, sz.hr, main_ref, side_ref)
    ratio.clear_sides()
    for j in range(sz.half):
        for k in range(2):
            ratio.put(2 * ((me // 2) ^ j) + k, 0, stack_ref[j, k])
    return ratio


def first_kernel(
    sz, me_ref, radius_hbm, phase_hbm, row_hbm, col_hbm, vol_hbm,
    rc_ref, keep_ref, send_ref,
    radius_ref, phase_ref, row_ref, col_ref, vol_ref, t_ref, a_ref, m_ref, x_ref, s_ref, sems,
):
    pairs = ((radius_hbm, radius_ref), (phase_hbm, phase_ref), (row_hbm, row_ref), (col_hbm, col_ref))
    small = [pltpu.make_async_copy(a, b, sems.at[i]) for i, (a, b) in enumerate(pairs)]
    large = [
        pltpu.make_async_copy(vol_hbm.at[z], vol_ref.at[z], sems.at[4 + z])
        for z in range(sz.planes)
    ]
    for copy in small + large:
        copy.start()
    part = lax.rem(me_ref[0], 2)
    m_ref[...] = jnp.zeros_like(m_ref)
    x_ref[...] = jnp.zeros_like(x_ref)
    for copy in small:
        copy.wait()
    for z in range(sz.planes):
        reach = radius_ref[z]
        phase_rows(sz, z, phase_ref, col_ref, t_ref, a_ref)
        matrix = spread_matrix(sz, reach, a_ref)
        rest = jnp.zeros((round_up(sz.span, 16) - sz.span, sz.wl), F32)
        matrix = jnp.concatenate([matrix, rest], axis=0) if rest.shape[0] else matrix
        m_ref[z, LANES : LANES + matrix.shape[0], :] = matrix.astype(BF16)
        rt = row_matrix(sz, z, reach, row_ref)
        rt = rt.T.astype(BF16)
        lanes = slice(z * sz.rp, (z + 1) * sz.rp)
        rc_ref[pl.ds(pl.multiple_of((1 - part) * sz.hr, sz.hr), sz.hr), lanes] = rt[0 : sz.hr, :]
        rc_ref[pl.ds(pl.multiple_of(part * sz.hr, sz.hr), sz.hr), lanes] = rt[sz.hr : sz.ep, :]
    for z in range(sz.planes):
        large[z].wait()
        x = jnp.concatenate([vol_ref[z], jnp.zeros((sz.rp - sz.rows, sz.cols), F32)], axis=0)
        x_ref[z, :, LANES : LANES + sz.cols] = x.astype(BF16)
        for b, start in enumerate(sz.starts):
            shift = start % LANES
            window = x_ref[z, :, start - shift : start - shift + sz.ka]
            matrix = m_ref[z, LANES - shift : LANES - shift + sz.ka, :]
            out = jnp.dot(window, matrix, preferred_element_type=F32)
            s_ref[b, z * sz.rp : (z + 1) * sz.rp, :] = out.astype(BF16)
    rows_forward(sz, rc_ref, s_ref, keep_ref, send_ref)


def table_kernel(
    sz, me_ref, strip_ref, radius_hbm, phase_hbm, row_hbm, col_hbm, after_ref,
    wf_ref, wb_ref, rt_ref, irn_ref, icn_ref,
    radius_ref, phase_ref, row_ref, col_ref, t_ref, a_ref, sems,
):
    pairs = ((radius_hbm, radius_ref), (phase_hbm, phase_ref), (row_hbm, row_ref), (col_hbm, col_ref))
    small = [pltpu.make_async_copy(a, b, sems.at[i]) for i, (a, b) in enumerate(pairs)]
    for copy in small:
        copy.start()
    for copy in small:
        copy.wait()
    kind, col = iota((8, sz.kb), 0), iota((8, sz.kb), 1)
    after, before = (col >= sz.wl) & (col < sz.wl + HALF), col >= sz.wl + HALF
    ones = jnp.where(((kind == 1) & before) | ((kind == 2) & after), 0.0, 1.0).astype(BF16)
    for z in range(sz.planes):
        reach = radius_ref[z]
        phase_rows(sz, z, phase_ref, col_ref, t_ref, a_ref)
        wf_ref[z] = by_block(sz, spread_matrix(sz, reach, a_ref))
        matrix = by_block(sz, gather_matrix(sz, reach, a_ref))
        wb_ref[z] = matrix
        norm = jnp.dot(ones, matrix, preferred_element_type=F32)
        icn_ref[z] = jnp.where(norm > 0.0, 1.0 / norm, 0.0)
        rt = row_matrix(sz, z, reach, row_ref)
        lane = iota(rt.shape, 1)
        top = jnp.where(lane < sz.hr, rt, 0.0)
        bottom = jnp.where((lane >= sz.hr) & (lane < sz.ep), rt, 0.0)
        bottom = pltpu.roll(bottom, sz.hp - sz.hr, 1)
        both = top + bottom
        turned = pltpu.roll(both, sz.hp, 1)
        rt_ref[z] = jnp.where(lax.rem(me_ref[0], 2) == 0, both, turned).astype(BF16)
        row = strip_ref[0] * sz.rows + iota(rt.shape, 1) - RMAX
        norm = jnp.sum(jnp.where((row >= 0) & (row < sz.total), rt, 0.0), axis=1, keepdims=True)
        irn_ref[z] = jnp.where(norm > 0.0, 1.0 / norm, 0.0)


def block_kernel(sz, vol_hbm, after_ref, blocks_ref, vol_ref, sems):
    copies = [
        pltpu.make_async_copy(vol_hbm.at[z], vol_ref.at[z], sems.at[z]) for z in range(sz.planes)
    ]
    for copy in copies:
        copy.start()
    for z, copy in enumerate(copies):
        copy.wait()
        for b in range(sz.n):
            block = vol_ref[z, :, b * sz.w : (b + 1) * sz.w]
            if sz.wl > sz.w:
                block = jnp.concatenate([block, jnp.zeros((sz.rows, sz.wl - sz.w), F32)], axis=1)
            blocks_ref[z, b] = block


def core_sum_kernel(sz, me_ref, keep_ref, recv_ref, own_ref, *out_refs):
    mine = me_ref[0] // 2
    for j, ref in enumerate((own_ref, *out_refs)):
        blocks = pl.ds(2 * (mine ^ j), 2)
        ref[...] = (keep_ref[blocks] + recv_ref[blocks].astype(F32)).astype(ref.dtype)


def chip_sum_kernel(sz, me_ref, after_ref, own_ref, meas_ref, *refs, first):
    recv_refs, (sum_ref, edge_ref) = refs[:-2], refs[-2:]
    total = own_ref[...]
    for ref in recv_refs:
        total = total + ref[...].astype(F32)
    sum_ref[...] = total
    edges = []
    for at, row in ((0, 0), (sz.rows - sz.hr, sz.rows - SIDE)):
        parts = [total[:, at : at + 32, :]]
        if first:
            meas = meas_ref[:, row : row + SIDE, :]
            high = meas.astype(BF16).astype(F32)
            parts += [high, meas - high]
        edges.append(jnp.concatenate(parts, axis=1))
    top, bottom = edges
    edge_ref[...] = jnp.where(lax.rem(me_ref[0], 2) == 0, top, bottom).astype(BF16)


def ratio_kernel(
    sz, me_ref, strip_ref, after_ref, sum_ref, meas_ref, edge_ref, first_edge_ref,
    ratio_ref, s_ref, m_ref,
):
    part = lax.rem(me_ref[0], 2)
    s_ref[...] = sum_ref[...]
    m_ref[...] = jnp.zeros_like(m_ref)
    edge, first_edge = edge_ref[...].astype(F32), first_edge_ref[...].astype(F32)
    alone = jnp.where(part == 0, strip_ref[0] == 0, (strip_ref[0] + 1) * sz.rows == sz.total)
    rows = jnp.where(alone, 0.0, edge[:, 0:32, :])
    meas = first_edge[:, 32:48, :] + first_edge[:, 48:64, :]

    @pl.when(part == 0)
    def _():
        s_ref[:, 0:32, :] += rows
        m_ref[:, 0:RMAX, :] = meas[:, SIDE - RMAX :, :]
        m_ref[:, RMAX : sz.hr, :] = meas_ref[:, 0 : sz.hr - RMAX, :]

    @pl.when(part == 1)
    def _():
        first = sz.rows - sz.hr
        s_ref[:, first : first + 32, :] += rows
        m_ref[:, 0 : first + RMAX, :] = meas_ref[:, sz.hr - RMAX :, :]
        m_ref[:, first + RMAX : first + 2 * RMAX, :] = meas[:, 0:RMAX, :]

    row = part * sz.hr + iota(s_ref.shape, 1)
    spot = strip_ref[0] * sz.rows + row - RMAX
    inside = (row < sz.e) & (spot >= 0) & (spot < sz.total) & (iota(s_ref.shape, 2) < sz.w)
    ratio_ref[...] = jnp.where(inside, m_ref[...] / s_ref[...], 0.0).astype(BF16)


def stack_kernel(sz, *refs):
    for j, ref in enumerate(refs[:-1]):
        refs[-1][j] = ref[...]


def ahead_kernel(sz, me_ref, same_ref, wb_ref, own_ref, ratio_ref, ratio_side_ref):
    ratio = place_ratio(sz, me_ref[0], same_ref, ratio_ref, ratio_side_ref)
    own_ref[:, :, sz.hr :, :] = jnp.zeros((sz.planes, sz.n, sz.hp - sz.hr, sz.wl), BF16)
    for z in range(sz.planes):
        for b, out in ratio.products(wb_ref[z]):
            own_ref[z, b, 0 : sz.hr, :] = out


def middle_kernel(
    sz, me_ref, own_ref, other_ref, wf_ref, wb_ref, rt_ref, irn_ref, icn_ref, rc_ref, vol_ref,
    new_ref, keep_ref, send_ref,
    ratio_ref, ratio_side_ref, g_ref, x_ref, x_side_ref, s_ref,
):
    ratio = place_ratio(sz, me_ref[0], other_ref, ratio_ref, ratio_side_ref)
    g_ref[:, sz.hr :, :] = jnp.zeros((sz.n, sz.hp - sz.hr, sz.wl), BF16)
    estimate = Windows(sz, sz.rp, x_ref, x_side_ref)
    estimate.clear_sides()
    lead = jnp.zeros((sz.rp - sz.rows, sz.wl), F32)
    for z in range(sz.planes):
        icn, irn = icn_ref[z], irn_ref[z][0 : sz.rows]
        for b, back in backward(sz, z, ratio, wb_ref[z], rt_ref[z], own_ref, g_ref):
            new = vol_ref[z, b] * back * (irn * block_norm(sz, b, icn))
            new_ref[z, b] = new
            estimate.put(b, 0, jnp.concatenate([new, lead]).astype(BF16))
        for b, out in estimate.products(wf_ref[z]):
            s_ref[b, z * sz.rp : (z + 1) * sz.rp, :] = out
    rows_forward(sz, rc_ref, s_ref, keep_ref, send_ref)


def last_kernel(
    sz, me_ref, own_ref, other_ref, wb_ref, rt_ref, irn_ref, icn_ref, vol_ref,
    out_hbm, ratio_ref, ratio_side_ref, g_ref, out_ref, sems,
):
    ratio = place_ratio(sz, me_ref[0], other_ref, ratio_ref, ratio_side_ref)
    g_ref[:, sz.hr :, :] = jnp.zeros((sz.n, sz.hp - sz.hr, sz.wl), BF16)
    copies = [
        pltpu.make_async_copy(out_ref.at[z], out_hbm.at[z], sems.at[z]) for z in range(sz.planes)
    ]
    for z in range(sz.planes):
        icn, irn = icn_ref[z], irn_ref[z][0 : sz.rows]
        for b, back in backward(sz, z, ratio, wb_ref[z], rt_ref[z], own_ref, g_ref):
            new = vol_ref[z, b] * back * (irn * block_norm(sz, b, icn))
            out_ref[z, :, b * sz.w : (b + 1) * sz.w] = new[:, 0 : sz.w]
        copies[z].start()
    for copy in copies:
        copy.wait()


SMEM = pl.BlockSpec(memory_space=pltpu.SMEM)
VMEM = pl.BlockSpec(memory_space=pltpu.VMEM)
ANY = pl.BlockSpec(memory_space=pl.ANY)
HBM = pl.BlockSpec(memory_space=pltpu.HBM)


def shape(dims, dtype):
    return jax.ShapeDtypeStruct(dims, dtype)


def call(kernel, sz, name, in_specs, out_specs, out_shape, scratch, args, mib, micros=1):
    return pl.pallas_call(
        functools.partial(kernel, sz),
        in_specs=in_specs,
        out_specs=out_specs,
        out_shape=out_shape,
        scratch_shapes=scratch,
        compiler_params=pltpu.CompilerParams(vmem_limit_bytes=mib * 1024 * 1024),
        cost_estimate=pl.CostEstimate(
            flops=0, bytes_accessed=micros * 3_000_000, transcendentals=0
        ),
        name=name,
    )(*args)


def local(volume, measured, row_taps, col_taps, phase_map, radius):
    n = lax.axis_size("depth")
    strips = lax.axis_size("strip")
    planes, rows, cols = volume.shape
    sz = Sizes(planes, rows, strips, cols, n, phase_map.shape[1])
    me = lax.axis_index("depth")
    strip = lax.axis_index("strip")
    me_arg = (me ^ (strip % 2)).reshape(1).astype(jnp.int32)
    strip_arg = strip.reshape(1).astype(jnp.int32)
    to_core = [(i, i ^ 1) for i in range(n)]
    to_chip = [[(i, i ^ (2 * j)) for i in range(n)] for j in range(1, sz.half)]
    to_strip = []
    for chip in range(sz.half):
        for lower in range(1, strips):
            row = (2 * chip + lower % 2) * strips
            to_strip += [(row + lower, row + lower - 1), (row + lower - 1, row + lower)]
        for edge, core in ((0, 0), (strips - 1, strips % 2)):
            pair = [(2 * c + core) * strips + edge for c in (chip, chip ^ 1)]
            to_strip.append(tuple(pair))

    volume = pltpu.with_memory_space_constraint(volume, pltpu.HBM)
    meas = lax.dynamic_slice_in_dim(measured, (me // 2) * 2 * sz.w, 2 * sz.w, axis=1)
    meas = jnp.stack([meas[:, 0 : sz.w], meas[:, sz.w :]])
    meas = jnp.pad(meas, ((0, 0), (0, 0), (0, sz.wl - sz.w)))
    by_family = col_taps.transpose(1, 0, 2)

    flat = shape((2, sz.hr, sz.wl), BF16)
    flat32 = shape((2, sz.hr, sz.wl), F32)
    halves = [shape((n, sz.hr, sz.wl), F32), shape((n, sz.hr, sz.wl), BF16)]
    blocked = shape((planes, n, rows, sz.wl), F32)
    tap_args = tuple(
        pltpu.with_memory_space_constraint(x, pltpu.HBM)
        for x in (radius, phase_map, row_taps, by_family)
    )
    tap_scratch = [
        pltpu.SMEM(radius.shape, jnp.int32),
        pltpu.SMEM(phase_map.shape, jnp.int32),
        pltpu.VMEM(row_taps.shape, F32),
        pltpu.VMEM(by_family.shape, F32),
    ]
    row_scratch = [
        pltpu.VMEM((round_up(sz.pitch, 8), sz.kp), F32),
        pltpu.VMEM((sz.ar, sz.kp), F32),
    ]
    s_scratch = pltpu.VMEM((n, planes * sz.rp, sz.wl), BF16)
    place_scratch = [
        pltpu.VMEM((n * sz.hr, sz.wl), BF16),
        pltpu.VMEM(((n + 2) * sz.hr, LANES), BF16),
    ]
    ratio_scratch = place_scratch + [pltpu.VMEM((n, sz.hp, sz.wl), BF16)]
    x_scratch = [
        pltpu.VMEM((n * sz.rp, sz.wl), BF16),
        pltpu.VMEM(((n + 2) * sz.rp, LANES), BF16),
    ]
    vol_scratch = pltpu.VMEM(volume.shape, F32)

    rc, keep, send = call(
        first_kernel, sz, "first",
        [SMEM] + [HBM] * 5,
        [VMEM] * 3,
        [shape((sz.ep, planes * sz.rp), BF16), *halves],
        tap_scratch + [vol_scratch] + row_scratch
        + [
            pltpu.VMEM((planes, LANES + sz.ka, sz.wl), BF16),
            pltpu.VMEM((planes, sz.rp, sz.xw), BF16),
            s_scratch,
            pltpu.SemaphoreType.DMA((4 + planes,)),
        ],
        (me_arg, *tap_args, volume),
        24, 4,
    )

    tables, current = None, None
    for iteration in range(ITERS):
        recv = lax.ppermute(send, "depth", to_core)
        own, *sends = call(
            core_sum_kernel, sz, "core_sum",
            [SMEM, VMEM, VMEM],
            [VMEM] * sz.half,
            [flat32] + [flat] * (sz.half - 1),
            [], (me_arg, keep, recv), 4,
        )
        if tables is None:
            wf, *tables = call(
                table_kernel, sz, "tables",
                [SMEM] * 2 + [HBM] * 4 + [ANY],
                [VMEM] * 5,
                [
                    shape((planes, sz.kb, sz.wl), BF16),
                    shape((planes, sz.kb, sz.wl), BF16),
                    shape((planes, sz.rp, sz.el), BF16),
                    shape((planes, sz.rp, 1), F32),
                    shape((planes, 8, sz.wl), F32),
                ],
                tap_scratch + row_scratch + [pltpu.SemaphoreType.DMA((4,))],
                (me_arg, strip_arg, *tap_args, own),
                8, 2,
            )
        recvs = [lax.ppermute(part, "depth", pairs) for part, pairs in zip(sends, to_chip)][::-1]
        total, edge = call(
            functools.partial(chip_sum_kernel, first=iteration == 0), sz, "chip_sum",
            [SMEM, ANY] + [VMEM] * (2 + len(recvs)),
            [VMEM] * 2,
            [flat32, shape((2, 64 if iteration == 0 else 32, sz.wl), BF16)],
            [], (me_arg, tables[3], own, meas, *recvs), 4,
        )
        edge = lax.ppermute(edge, ("depth", "strip"), to_strip)
        first_edge = edge if iteration == 0 else first_edge
        if iteration == 0:
            current = call(
                block_kernel, sz, "blocks",
                [HBM, ANY], VMEM, blocked,
                [vol_scratch, pltpu.SemaphoreType.DMA((planes,))],
                (volume, total), 12, 3,
            )
        ratio = call(
            ratio_kernel, sz, "ratio",
            [SMEM] * 2 + [ANY] + [VMEM] * 4,
            VMEM,
            flat,
            [pltpu.VMEM(flat32.shape, F32)] * 2,
            (me_arg, strip_arg, current, total, meas, edge, first_edge), 4,
        )
        chips = [lax.ppermute(ratio, "depth", pairs) for pairs in to_chip]
        same = call(
            stack_kernel, sz, "stack",
            [VMEM] * sz.half, VMEM, shape((sz.half,) + flat.shape, BF16),
            [], (ratio, *chips), 4,
        )
        other = lax.ppermute(same, "depth", to_core)
        own = call(
            ahead_kernel, sz, "ahead",
            [SMEM] + [VMEM] * 2, VMEM,
            shape((planes, n, sz.hp, sz.wl), BF16),
            place_scratch, (me_arg, same, tables[0]), 8,
        )
        if iteration < ITERS - 1:
            current, keep, send = call(
                middle_kernel, sz, "middle",
                [SMEM] + [VMEM] * 9,
                [VMEM] * 3,
                [blocked, *halves],
                ratio_scratch + x_scratch + [s_scratch],
                (me_arg, own, other, wf, *tables, rc, current),
                16, 5,
            )
        else:
            current = call(
                last_kernel, sz, "last",
                [SMEM] + [VMEM] * 7,
                HBM,
                shape(volume.shape, F32),
                ratio_scratch + [vol_scratch, pltpu.SemaphoreType.DMA((planes,))],
                (me_arg, own, other, *tables, current),
                16, 5,
            )
    return current


def solution(mesh):
    return jax.shard_map(
        local,
        mesh=mesh,
        in_specs=(
            P("depth", "strip", None),
            P("strip", None),
            P("depth", None),
            P("depth", None, None),
            P("depth", None),
            P("depth"),
        ),
        out_specs=P("depth", "strip", None),
        check_vma=False,
    )
```

```python
import functools

import jax
import jax.numpy as jnp
from jax import lax
from jax.experimental import pallas as pl
from jax.experimental.pallas import tpu as pltpu
from jax.sharding import PartitionSpec as P

RMAX = 15
ITERS = 2
SIDE = 16
LANES = 128
HALF = LANES // 2

F32 = jnp.float32
BF16 = jnp.bfloat16


def round_up(value, step):
    return -(-value // step) * step


class Sizes:
    def __init__(self, planes, rows, strips, cols, devices, pitch):
        self.total = rows * strips
        self.planes, self.rows, self.cols, self.n, self.pitch = planes, rows, cols, devices, pitch
        self.w = cols // devices
        self.half = devices // 2
        assert cols % devices == 0 and self.w % pitch == 0 and self.w >= 2 * SIDE
        assert devices >= 4 and devices & (devices - 1) == 0 and rows >= 2 * RMAX and rows % 8 == 0
        self.wl = round_up(self.w, LANES)
        self.span = self.w + 2 * SIDE
        self.kp = round_up(self.span, LANES)
        self.kb = self.wl + LANES
        self.tiles = self.wl // LANES
        assert self.tiles <= 2 and planes % 2 == 0
        self.rp = round_up(rows, LANES)
        self.e = rows + 2 * RMAX
        self.ep = round_up(self.e, 32)
        self.hr = self.ep // 2
        self.hp = round_up(self.hr, LANES)
        self.el = round_up(self.ep, LANES)
        assert self.el == 2 * self.hp
        assert 32 <= rows - self.hr and rows - self.hr + 32 <= self.hr and (rows - self.hr) % 8 == 0
        self.ar = round_up(max(self.span, self.wl) + pitch, pitch)
        self.starts = [LANES + b * self.w - SIDE for b in range(devices)]
        self.ka = round_up(max(s % LANES for s in self.starts) + self.span, LANES)
        self.xw = max(s // LANES * LANES for s in self.starts) + self.ka


def iota(shape, axis):
    return lax.broadcasted_iota(jnp.int32, shape, axis)


def phase_rows(sz, z, phase_ref, col_ref, t_ref, a_ref):
    taps = col_ref.shape[2]
    t_ref[...] = jnp.zeros_like(t_ref)
    for p in range(sz.pitch):
        row = col_ref[phase_ref[z, p], pl.ds(z, 1), :]
        t_ref[p : p + 1, 0:taps] = row.astype(BF16).astype(F32)
    base = t_ref[0 : sz.pitch, :]
    for k in range(sz.ar // sz.pitch):
        a_ref[k * sz.pitch : (k + 1) * sz.pitch, :] = base


def spread_matrix(sz, reach, a_ref):
    first = (-SIDE) % sz.pitch
    rows = a_ref[first : first + sz.span, 0 : sz.wl]
    rows = pltpu.roll(rows, sz.wl - RMAX - SIDE, 1, stride=1, stride_axis=0)
    col, row = iota(rows.shape, 1), iota(rows.shape, 0)
    return jnp.where((jnp.abs(col - row + SIDE) <= reach) & (col < sz.w), rows, 0.0)


def gather_matrix(sz, reach, a_ref):
    rows = pltpu.roll(a_ref[0 : sz.wl, 0 : sz.kp], SIDE - RMAX, 1, stride=1, stride_axis=0)
    col, row = iota(rows.shape, 1), iota(rows.shape, 0)
    rows = jnp.where((jnp.abs(col - SIDE - row) <= reach) & (row < sz.w), rows, 0.0)
    return rows.T[0 : sz.span, :]


def by_block(sz, matrix):
    def zeros(count):
        return [jnp.zeros((count, sz.wl), F32)] if count else []

    lead = sz.w - (sz.wl - LANES) - 2 * SIDE
    parts = [matrix[SIDE : SIDE + sz.w]] + zeros(sz.wl - sz.w)
    parts += [matrix[SIDE + sz.w :]] + zeros(lead) + [matrix[0:SIDE]] + zeros(sz.wl - sz.w)
    return jnp.concatenate(parts, axis=0).astype(BF16)


def by_tile(sz, matrix):
    def zeros(count):
        return [jnp.zeros((count, sz.wl), F32)] if count else []

    here = min(sz.w, LANES)
    lead = sz.w - (sz.wl - LANES) - 2 * SIDE
    first = [matrix[SIDE : SIDE + here]] + zeros(LANES - here)
    first += [matrix[SIDE + here : SIDE + here + SIDE]] + zeros(lead)
    first += [matrix[0:SIDE]] + zeros(sz.wl - sz.w)
    parts = [jnp.concatenate(first, axis=0)[:, 0:LANES]]
    if sz.tiles == 2:
        second = [matrix[SIDE : 2 * SIDE + sz.w]] + zeros(sz.wl - sz.w - SIDE)
        parts.append(jnp.concatenate(second, axis=0)[:, LANES:])
    return [part.astype(BF16) for part in parts]


def row_matrix(sz, z, reach, row_ref):
    taps = row_ref.shape[1]
    lane = iota((1, sz.el), 1)
    row = row_ref[pl.ds(z, 1), :].astype(BF16).astype(F32)
    row = jnp.concatenate([row, jnp.zeros((1, sz.el - taps), F32)], axis=1)
    row = jnp.where(jnp.abs(lane - RMAX) <= reach, row, 0.0)
    wide = jnp.broadcast_to(row, (sz.rp, sz.el))
    wide = pltpu.roll(wide, 0, 1, stride=1, stride_axis=0)
    return jnp.where(iota(wide.shape, 0) < sz.rows, wide, 0.0)


class Windows:
    def __init__(self, sz, height, main_ref, side_ref, group):
        self.group = group
        self.sz, self.height, self.main, self.side = sz, height, main_ref, side_ref

    def clear_sides(self):
        self.side[...] = jnp.zeros_like(self.side)

    def put(self, b, row, x):
        sz = self.sz

        def rows(block):
            at = block * self.height + row
            if not isinstance(at, int):
                at = pl.multiple_of(at, 16)
            return pl.ds(at, x.shape[0])

        self.main[rows(b), :] = x
        self.side[rows(b), 0:HALF] = x[:, 0:HALF]
        self.side[rows(b + 2), HALF:] = x[:, sz.wl - HALF :]

    def products(self, matrix):
        sz, height = self.sz, self.height
        for first in range(0, sz.n, self.group):
            count = self.group * height
            main = self.main[first * height : first * height + count, :]
            side = self.side[(first + 1) * height : (first + 1) * height + count, :]
            window = jnp.concatenate([main, side], axis=1)
            out = jnp.dot(window, matrix, preferred_element_type=F32).astype(BF16)
            for k in range(self.group):
                yield first + k, out[k * height : (k + 1) * height, :]


class PairWindows:
    def __init__(self, sz, main_ref, side_ref):
        self.sz, self.main, self.side = sz, main_ref, side_ref

    def clear(self):
        sz = self.sz
        self.main[sz.n * sz.hr :, :] = jnp.zeros((sz.hr, sz.wl), BF16)
        self.side[...] = jnp.zeros_like(self.side)

    def put(self, b, x):
        sz = self.sz

        def rows(block):
            return pl.ds(pl.multiple_of(block * sz.hr, 16), sz.hr)

        self.main[rows(b + 1), 0 : sz.w] = x[:, 0 : sz.w]
        if sz.tiles == 2:
            self.main[rows(b), sz.w : sz.w + SIDE] = x[:, 0:SIDE]
            self.side[rows(b + 1), 0:HALF] = x[:, LANES : LANES + HALF]
        else:
            self.side[rows(b), 0:HALF] = x[:, 0:HALF]
        self.side[rows(b + 2), HALF:] = x[:, sz.wl - HALF :]

    def products(self, pair_ref, group):
        sz = self.sz
        for first in range(0, sz.n, group):
            rows = slice((first + 1) * sz.hr, (first + 1 + group) * sz.hr)
            for tile in range(sz.tiles):
                if tile == 0:
                    window = jnp.concatenate([self.main[rows, 0:LANES], self.side[rows, :]], axis=1)
                else:
                    window = self.main[rows, :]
                out = jnp.dot(window, pair_ref[tile], preferred_element_type=F32).astype(BF16)
                for k in range(group):
                    for plane in range(2):
                        lanes = slice(plane * LANES, (plane + 1) * LANES)
                        yield first + k, plane, tile, out[k * sz.hr : (k + 1) * sz.hr, lanes]


def rows_forward(sz, rc_ref, s_ref, keep_ref, send_ref):
    coef = rc_ref[...]
    for b in range(sz.n):
        out = jnp.dot(coef, s_ref[b], preferred_element_type=F32)
        send_ref[b] = out[0 : sz.hr, :].astype(BF16)
        keep_ref[b] = out[sz.hr :, :]


def backward(sz, pair, ratio, wb_ref, rt_ref, own_ref, g_ref):
    for b, plane, tile, out in ratio.products(wb_ref.at[pair], 2):
        g_ref[plane, b, 0 : sz.hr, tile * LANES : (tile + 1) * LANES] = out
    for plane in range(2):
        z = 2 * pair + plane
        for b in range(sz.n):
            rows = jnp.concatenate([own_ref[z, b], g_ref[plane, b]], axis=0)
            back = jnp.dot(rt_ref[z], rows, preferred_element_type=F32)
            yield z, b, back[0 : sz.rows, :]


def block_norm(sz, b, icn):
    kind = 1 if b == 0 else 2 if b == sz.n - 1 else 0
    return icn[kind : kind + 1, :]


def place_ratio(sz, me, stack_ref, main_ref, side_ref):
    ratio = PairWindows(sz, main_ref, side_ref)
    ratio.clear()
    for j in range(sz.half):
        for k in range(2):
            ratio.put(2 * ((me // 2) ^ j) + k, stack_ref[j, k])
    return ratio


def first_kernel(
    sz, me_ref, radius_hbm, phase_hbm, row_hbm, col_hbm, vol_hbm,
    rc_ref, keep_ref, send_ref,
    radius_ref, phase_ref, row_ref, col_ref, vol_ref, t_ref, a_ref, m_ref, x_ref, s_ref, sems,
):
    pairs = ((radius_hbm, radius_ref), (phase_hbm, phase_ref), (row_hbm, row_ref), (col_hbm, col_ref))
    small = [pltpu.make_async_copy(a, b, sems.at[i]) for i, (a, b) in enumerate(pairs)]
    large = [
        pltpu.make_async_copy(vol_hbm.at[z], vol_ref.at[z], sems.at[4 + z])
        for z in range(sz.planes)
    ]
    for copy in small + large:
        copy.start()
    part = lax.rem(me_ref[0], 2)
    m_ref[...] = jnp.zeros_like(m_ref)
    x_ref[...] = jnp.zeros_like(x_ref)
    for copy in small:
        copy.wait()
    for z in range(sz.planes):
        reach = radius_ref[z]
        phase_rows(sz, z, phase_ref, col_ref, t_ref, a_ref)
        matrix = spread_matrix(sz, reach, a_ref)
        rest = jnp.zeros((round_up(sz.span, 16) - sz.span, sz.wl), F32)
        matrix = jnp.concatenate([matrix, rest], axis=0) if rest.shape[0] else matrix
        m_ref[z, LANES : LANES + matrix.shape[0], :] = matrix.astype(BF16)
        rt = row_matrix(sz, z, reach, row_ref)
        rt = rt.T.astype(BF16)
        lanes = slice(z * sz.rp, (z + 1) * sz.rp)
        rc_ref[pl.ds(pl.multiple_of((1 - part) * sz.hr, sz.hr), sz.hr), lanes] = rt[0 : sz.hr, :]
        rc_ref[pl.ds(pl.multiple_of(part * sz.hr, sz.hr), sz.hr), lanes] = rt[sz.hr : sz.ep, :]
    for z in range(sz.planes):
        large[z].wait()
        x = jnp.concatenate([vol_ref[z], jnp.zeros((sz.rp - sz.rows, sz.cols), F32)], axis=0)
        x_ref[z, :, LANES : LANES + sz.cols] = x.astype(BF16)
        for b, start in enumerate(sz.starts):
            shift = start % LANES
            window = x_ref[z, :, start - shift : start - shift + sz.ka]
            matrix = m_ref[z, LANES - shift : LANES - shift + sz.ka, :]
            out = jnp.dot(window, matrix, preferred_element_type=F32)
            s_ref[b, z * sz.rp : (z + 1) * sz.rp, :] = out.astype(BF16)
    rows_forward(sz, rc_ref, s_ref, keep_ref, send_ref)


def table_kernel(
    sz, me_ref, strip_ref, radius_hbm, phase_hbm, row_hbm, col_hbm, after_ref,
    wf_ref, wb_ref, rt_ref, irn_ref, icn_ref,
    radius_ref, phase_ref, row_ref, col_ref, t_ref, a_ref, sems,
):
    pairs = ((radius_hbm, radius_ref), (phase_hbm, phase_ref), (row_hbm, row_ref), (col_hbm, col_ref))
    small = [pltpu.make_async_copy(a, b, sems.at[i]) for i, (a, b) in enumerate(pairs)]
    for copy in small:
        copy.start()
    for copy in small:
        copy.wait()
    kind, col = iota((8, 2 * LANES), 0), iota((8, 2 * LANES), 1)
    missing = [(kind == 1) & (col >= LANES + HALF)]
    if sz.tiles == 2:
        missing.append((kind == 2) & (col >= sz.w))
    else:
        missing[0] |= (kind == 2) & (col >= LANES) & (col < LANES + HALF)
    ones = [jnp.where(part, 0.0, 1.0).astype(BF16) for part in missing]
    for z in range(sz.planes):
        reach = radius_ref[z]
        phase_rows(sz, z, phase_ref, col_ref, t_ref, a_ref)
        wf_ref[z] = by_block(sz, spread_matrix(sz, reach, a_ref))
        parts = by_tile(sz, gather_matrix(sz, reach, a_ref))
        for tile, part in enumerate(parts):
            lanes = slice(z % 2 * LANES, (z % 2 + 1) * LANES)
            wb_ref[z // 2, tile, :, lanes] = part
        norm = [jnp.dot(a, b, preferred_element_type=F32) for a, b in zip(ones, parts)]
        norm = jnp.concatenate(norm, axis=1)
        icn_ref[z] = jnp.where(norm > 0.0, 1.0 / norm, 0.0)
        rt = row_matrix(sz, z, reach, row_ref)
        lane = iota(rt.shape, 1)
        top = jnp.where(lane < sz.hr, rt, 0.0)
        bottom = jnp.where((lane >= sz.hr) & (lane < sz.ep), rt, 0.0)
        bottom = pltpu.roll(bottom, sz.hp - sz.hr, 1)
        both = top + bottom
        turned = pltpu.roll(both, sz.hp, 1)
        rt_ref[z] = jnp.where(lax.rem(me_ref[0], 2) == 0, both, turned).astype(BF16)
        row = strip_ref[0] * sz.rows + iota(rt.shape, 1) - RMAX
        norm = jnp.sum(jnp.where((row >= 0) & (row < sz.total), rt, 0.0), axis=1, keepdims=True)
        irn_ref[z] = jnp.where(norm > 0.0, 1.0 / norm, 0.0)


def block_kernel(sz, vol_hbm, after_ref, blocks_ref, vol_ref, sems, planes):
    copies = [
        pltpu.make_async_copy(vol_hbm.at[z], vol_ref.at[i], sems.at[i])
        for i, z in enumerate(planes)
    ]
    for copy in copies:
        copy.start()
    for z, copy in enumerate(copies):
        copy.wait()
        for b in range(sz.n):
            block = vol_ref[z, :, b * sz.w : (b + 1) * sz.w]
            if sz.wl > sz.w:
                block = jnp.concatenate([block, jnp.zeros((sz.rows, sz.wl - sz.w), F32)], axis=1)
            blocks_ref[z, b] = block


def core_sum_kernel(sz, me_ref, keep_ref, recv_ref, own_ref, *out_refs):
    mine = me_ref[0] // 2
    for j, ref in enumerate((own_ref, *out_refs)):
        blocks = pl.ds(2 * (mine ^ j), 2)
        ref[...] = (keep_ref[blocks] + recv_ref[blocks].astype(F32)).astype(ref.dtype)


def chip_sum_kernel(sz, me_ref, after_ref, own_ref, meas_ref, *refs, first):
    recv_refs, (sum_ref, edge_ref) = refs[:-2], refs[-2:]
    total = own_ref[...]
    for ref in recv_refs:
        total = total + ref[...].astype(F32)
    sum_ref[...] = total
    edges = []
    for at, row in ((0, 0), (sz.rows - sz.hr, sz.rows - SIDE)):
        parts = [total[:, at : at + 32, :]]
        if first:
            meas = meas_ref[:, row : row + SIDE, :]
            high = meas.astype(BF16).astype(F32)
            parts += [high, meas - high]
        edges.append(jnp.concatenate(parts, axis=1))
    top, bottom = edges
    edge_ref[...] = jnp.where(lax.rem(me_ref[0], 2) == 0, top, bottom).astype(BF16)


def ratio_kernel(
    sz, me_ref, strip_ref, after_ref, sum_ref, meas_ref, edge_ref, first_edge_ref,
    ratio_ref, s_ref, m_ref,
):
    part = lax.rem(me_ref[0], 2)
    s_ref[...] = sum_ref[...]
    m_ref[...] = jnp.zeros_like(m_ref)
    edge, first_edge = edge_ref[...].astype(F32), first_edge_ref[...].astype(F32)
    alone = jnp.where(part == 0, strip_ref[0] == 0, (strip_ref[0] + 1) * sz.rows == sz.total)
    rows = jnp.where(alone, 0.0, edge[:, 0:32, :])
    meas = first_edge[:, 32:48, :] + first_edge[:, 48:64, :]

    @pl.when(part == 0)
    def _():
        s_ref[:, 0:32, :] += rows
        m_ref[:, 0:RMAX, :] = meas[:, SIDE - RMAX :, :]
        m_ref[:, RMAX : sz.hr, :] = meas_ref[:, 0 : sz.hr - RMAX, :]

    @pl.when(part == 1)
    def _():
        first = sz.rows - sz.hr
        s_ref[:, first : first + 32, :] += rows
        m_ref[:, 0 : first + RMAX, :] = meas_ref[:, sz.hr - RMAX :, :]
        m_ref[:, first + RMAX : first + 2 * RMAX, :] = meas[:, 0:RMAX, :]

    row = part * sz.hr + iota(s_ref.shape, 1)
    spot = strip_ref[0] * sz.rows + row - RMAX
    inside = (row < sz.e) & (spot >= 0) & (spot < sz.total) & (iota(s_ref.shape, 2) < sz.w)
    ratio_ref[...] = jnp.where(inside, m_ref[...] / s_ref[...], 0.0).astype(BF16)


def stack_kernel(sz, after_ref, *refs, order):
    for j, ref in zip(order, refs[:-1]):
        refs[-1][j] = ref[...]


def ahead_kernel(sz, me_ref, same_ref, wb_ref, own_ref, ratio_ref, ratio_side_ref):
    ratio = place_ratio(sz, me_ref[0], same_ref, ratio_ref, ratio_side_ref)
    own_ref[:, :, sz.hr :, :] = jnp.zeros((sz.planes, sz.n, sz.hp - sz.hr, sz.wl), BF16)
    for pair in range(sz.planes // 2):
        for b, plane, tile, out in ratio.products(wb_ref.at[pair], 2):
            lanes = slice(tile * LANES, (tile + 1) * LANES)
            own_ref[2 * pair + plane, b, 0 : sz.hr, lanes] = out


def middle_kernel(
    sz, me_ref, own_ref, other_ref, wf_ref, wb_ref, rt_ref, irn_ref, icn_ref, rc_ref, before_ref, after_ref,
    new_ref, keep_ref, send_ref,
    ratio_ref, ratio_side_ref, g_ref, x_ref, x_side_ref, s_ref,
):
    ratio = place_ratio(sz, me_ref[0], other_ref, ratio_ref, ratio_side_ref)
    g_ref[:, :, sz.hr :, :] = jnp.zeros((2, sz.n, sz.hp - sz.hr, sz.wl), BF16)
    estimate = Windows(sz, sz.rp, x_ref, x_side_ref, 4)
    estimate.clear_sides()
    lead = jnp.zeros((sz.rp - sz.rows, sz.wl), F32)
    split = before_ref.shape[0]
    for pair in range(sz.planes // 2):
        for z, b, back in backward(sz, pair, ratio, wb_ref, rt_ref, own_ref, g_ref):
            old = before_ref[z, b] if z < split else after_ref[z - split, b]
            if b == 0:
                icn, irn = icn_ref[z], irn_ref[z][0 : sz.rows]
            norm = irn * block_norm(sz, b, icn)
            new = old * back * norm
            new_ref[z, b] = new
            estimate.put(b, 0, jnp.concatenate([new, lead]).astype(BF16))
            if b == sz.n - 1:
                for k, out in estimate.products(wf_ref[z]):
                    s_ref[k, z * sz.rp : (z + 1) * sz.rp, :] = out
    rows_forward(sz, rc_ref, s_ref, keep_ref, send_ref)


def last_kernel(
    sz, me_ref, own_ref, other_ref, wb_ref, rt_ref, irn_ref, icn_ref, vol_ref,
    out_hbm, ratio_ref, ratio_side_ref, g_ref, out_ref, sems,
):
    ratio = place_ratio(sz, me_ref[0], other_ref, ratio_ref, ratio_side_ref)
    g_ref[:, :, sz.hr :, :] = jnp.zeros((2, sz.n, sz.hp - sz.hr, sz.wl), BF16)
    middle = sz.cols // 2 // LANES * LANES
    lanes = (slice(0, middle), slice(middle, sz.cols))
    copies = [
        [
            pltpu.make_async_copy(out_ref.at[z, :, k], out_hbm.at[z, :, k], sems.at[z, i])
            for i, k in enumerate(lanes)
        ]
        for z in range(sz.planes)
    ]
    for pair in range(sz.planes // 2):
        for z, b, back in backward(sz, pair, ratio, wb_ref, rt_ref, own_ref, g_ref):
            if b == 0:
                icn, irn = icn_ref[z], irn_ref[z][0 : sz.rows]
            norm = irn * block_norm(sz, b, icn)
            new = vol_ref[z, b] * back * norm
            out_ref[z, :, b * sz.w : (b + 1) * sz.w] = new[:, 0 : sz.w]
            if b == sz.n // 2 - 1:
                copies[z][0].start()
            if b == sz.n - 1:
                copies[z][1].start()
    for plane in copies:
        for copy in plane:
            copy.wait()


SMEM = pl.BlockSpec(memory_space=pltpu.SMEM)
VMEM = pl.BlockSpec(memory_space=pltpu.VMEM)
ANY = pl.BlockSpec(memory_space=pl.ANY)
HBM = pl.BlockSpec(memory_space=pltpu.HBM)


def shape(dims, dtype):
    return jax.ShapeDtypeStruct(dims, dtype)


def call(kernel, sz, name, in_specs, out_specs, out_shape, scratch, args, mib, micros=1):
    return pl.pallas_call(
        functools.partial(kernel, sz),
        in_specs=in_specs,
        out_specs=out_specs,
        out_shape=out_shape,
        scratch_shapes=scratch,
        compiler_params=pltpu.CompilerParams(vmem_limit_bytes=mib * 1024 * 1024),
        cost_estimate=pl.CostEstimate(
            flops=0, bytes_accessed=micros * 3_000_000, transcendentals=0
        ),
        name=name,
    )(*args)


def local(volume, measured, row_taps, col_taps, phase_map, radius):
    n = lax.axis_size("depth")
    strips = lax.axis_size("strip")
    planes, rows, cols = volume.shape
    sz = Sizes(planes, rows, strips, cols, n, phase_map.shape[1])
    me = lax.axis_index("depth")
    strip = lax.axis_index("strip")
    me_arg = (me ^ (strip % 2)).reshape(1).astype(jnp.int32)
    strip_arg = strip.reshape(1).astype(jnp.int32)
    to_core = [(i, i ^ 1) for i in range(n)]
    to_chip = [[(i, i ^ (2 * j)) for i in range(n)] for j in range(1, sz.half)]
    order_rs = range(sz.half - 1)[::-1]
    order_ag = range(sz.half - 1)
    to_strip = []
    for chip in range(sz.half):
        for lower in range(1, strips):
            row = (2 * chip + lower % 2) * strips
            to_strip += [(row + lower, row + lower - 1), (row + lower - 1, row + lower)]
        for edge, core in ((0, 0), (strips - 1, strips % 2)):
            pair = [(2 * c + core) * strips + edge for c in (chip, chip ^ 1)]
            to_strip.append(tuple(pair))

    volume = pltpu.with_memory_space_constraint(volume, pltpu.HBM)
    meas = lax.dynamic_slice_in_dim(measured, (me // 2) * 2 * sz.w, 2 * sz.w, axis=1)
    meas = jnp.stack([meas[:, 0 : sz.w], meas[:, sz.w :]])
    meas = jnp.pad(meas, ((0, 0), (0, 0), (0, sz.wl - sz.w)))
    by_family = col_taps.transpose(1, 0, 2)

    flat = shape((2, sz.hr, sz.wl), BF16)
    flat32 = shape((2, sz.hr, sz.wl), F32)
    halves = [shape((n, sz.hr, sz.wl), F32), shape((n, sz.hr, sz.wl), BF16)]
    blocked = shape((planes, n, rows, sz.wl), F32)
    tap_args = tuple(
        pltpu.with_memory_space_constraint(x, pltpu.HBM)
        for x in (radius, phase_map, row_taps, by_family)
    )
    tap_scratch = [
        pltpu.SMEM(radius.shape, jnp.int32),
        pltpu.SMEM(phase_map.shape, jnp.int32),
        pltpu.VMEM(row_taps.shape, F32),
        pltpu.VMEM(by_family.shape, F32),
    ]
    row_scratch = [
        pltpu.VMEM((round_up(sz.pitch, 8), sz.kp), F32),
        pltpu.VMEM((sz.ar, sz.kp), F32),
    ]
    s_scratch = pltpu.VMEM((n, planes * sz.rp, sz.wl), BF16)
    place_scratch = [
        pltpu.VMEM(((n + 1) * sz.hr, sz.wl), BF16),
        pltpu.VMEM(((n + 2) * sz.hr, LANES), BF16),
    ]
    ratio_scratch = place_scratch + [pltpu.VMEM((2, n, sz.hp, sz.wl), BF16)]
    x_scratch = [
        pltpu.VMEM((n * sz.rp, sz.wl), BF16),
        pltpu.VMEM(((n + 2) * sz.rp, LANES), BF16),
    ]
    vol_scratch = pltpu.VMEM(volume.shape, F32)

    rc, keep, send = call(
        first_kernel, sz, "first",
        [SMEM] + [HBM] * 5,
        [VMEM] * 3,
        [shape((sz.ep, planes * sz.rp), BF16), *halves],
        tap_scratch + [vol_scratch] + row_scratch
        + [
            pltpu.VMEM((planes, LANES + sz.ka, sz.wl), BF16),
            pltpu.VMEM((planes, sz.rp, sz.xw), BF16),
            s_scratch,
            pltpu.SemaphoreType.DMA((4 + planes,)),
        ],
        (me_arg, *tap_args, volume),
        24, 4,
    )

    def block_planes(which, after):
        return call(
            functools.partial(block_kernel, planes=tuple(which)), sz, "blocks",
            [HBM, ANY], VMEM, shape((len(which), n, rows, sz.wl), F32),
            [
                pltpu.VMEM((len(which), rows, cols), F32),
                pltpu.SemaphoreType.DMA((len(which),)),
            ],
            (volume, after), 12, 2,
        )

    tables, current = None, None
    for iteration in range(ITERS):
        recv = lax.ppermute(send, "depth", to_core)
        own, *sends = call(
            core_sum_kernel, sz, "core_sum",
            [SMEM, VMEM, VMEM],
            [VMEM] * sz.half,
            [flat32] + [flat] * (sz.half - 1),
            [], (me_arg, keep, recv), 4,
        )
        if tables is None:
            wf, *tables = call(
                table_kernel, sz, "tables",
                [SMEM] * 2 + [HBM] * 4 + [ANY],
                [VMEM] * 5,
                [
                    shape((planes, sz.kb, sz.wl), BF16),
                    shape((planes // 2, sz.tiles, 2 * LANES, 2 * LANES), BF16),
                    shape((planes, sz.rp, sz.el), BF16),
                    shape((planes, sz.rp, 1), F32),
                    shape((planes, 8, sz.wl), F32),
                ],
                tap_scratch + row_scratch + [pltpu.SemaphoreType.DMA((4,))],
                (me_arg, strip_arg, *tap_args, own),
                8, 2,
            )
        recvs = [lax.ppermute(sends[j], "depth", to_chip[j]) for j in order_rs]
        total, edge = call(
            functools.partial(chip_sum_kernel, first=iteration == 0), sz, "chip_sum",
            [SMEM, ANY] + [VMEM] * (2 + len(recvs)),
            [VMEM] * 2,
            [flat32, shape((2, 64 if iteration == 0 else 32, sz.wl), BF16)],
            [], (me_arg, tables[3], own, meas, *recvs), 4,
        )
        edge = lax.ppermute(edge, ("depth", "strip"), to_strip)
        first_edge = edge if iteration == 0 else first_edge
        if iteration == 0:
            before = block_planes(range(planes // 2), total)
        ratio = call(
            ratio_kernel, sz, "ratio",
            [SMEM] * 2 + [ANY] + [VMEM] * 4,
            VMEM,
            flat,
            [pltpu.VMEM(flat32.shape, F32)] * 2,
            (me_arg, strip_arg, before, total, meas, edge, first_edge), 4,
        )
        chips = [lax.ppermute(ratio, "depth", to_chip[j]) for j in order_ag]
        if iteration == 0:
            after = block_planes(range(planes // 2, planes), ratio)
        same = call(
            functools.partial(stack_kernel, order=(0, *[j + 1 for j in order_ag])), sz, "stack",
            [ANY] + [VMEM] * sz.half, VMEM, shape((sz.half,) + flat.shape, BF16),
            [], (after, ratio, *chips), 4,
        )
        other = lax.ppermute(same, "depth", to_core)
        own = call(
            ahead_kernel, sz, "ahead",
            [SMEM] + [VMEM] * 2, VMEM,
            shape((planes, n, sz.hp, sz.wl), BF16),
            place_scratch, (me_arg, same, tables[0]), 8,
        )
        if iteration < ITERS - 1:
            current, keep, send = call(
                middle_kernel, sz, "middle",
                [SMEM] + [VMEM] * 10,
                [VMEM] * 3,
                [blocked, *halves],
                ratio_scratch + x_scratch + [s_scratch],
                (me_arg, own, other, wf, *tables, rc, before, after),
                16, 5,
            )
        else:
            current = call(
                last_kernel, sz, "last",
                [SMEM] + [VMEM] * 7,
                HBM,
                shape(volume.shape, F32),
                ratio_scratch + [vol_scratch, pltpu.SemaphoreType.DMA((planes, 2))],
                (me_arg, own, other, *tables, current),
                16, 5,
            )
    return current


def solution(mesh):
    return jax.shard_map(
        local,
        mesh=mesh,
        in_specs=(
            P("depth", "strip", None),
            P("strip", None),
            P("depth", None),
            P("depth", None, None),
            P("depth", None),
            P("depth"),
        ),
        out_specs=P("depth", "strip", None),
        check_vma=False,
    )
```

```python
import functools

import jax
import jax.numpy as jnp
from jax import lax
from jax.experimental import pallas as pl
from jax.experimental.pallas import tpu as pltpu
from jax.sharding import PartitionSpec as P

RMAX = 15
ITERS = 2
SIDE = 16
LANES = 128
HALF = LANES // 2

F32 = jnp.float32
BF16 = jnp.bfloat16


def round_up(value, step):
    return -(-value // step) * step


class Sizes:
    def __init__(self, planes, rows, strips, cols, devices, pitch):
        self.total = rows * strips
        self.planes, self.rows, self.cols, self.n, self.pitch = planes, rows, cols, devices, pitch
        self.w = cols // devices
        self.half = devices // 2
        assert cols % devices == 0 and self.w % pitch == 0 and self.w >= 2 * SIDE
        assert devices >= 4 and devices & (devices - 1) == 0 and rows >= 2 * RMAX and rows % 8 == 0
        self.wl = round_up(self.w, LANES)
        self.span = self.w + 2 * SIDE
        self.kp = round_up(self.span, LANES)
        self.kb = self.wl + LANES
        self.tiles = self.wl // LANES
        assert self.tiles <= 2 and planes % 2 == 0 and self.wl > self.w
        self.rp = round_up(rows, LANES)
        self.e = rows + 2 * RMAX
        self.ep = round_up(self.e, 32)
        self.hr = self.ep // 2
        self.hp = round_up(self.hr, LANES)
        self.el = round_up(self.ep, LANES)
        assert self.el == 2 * self.hp
        assert 32 <= rows - self.hr and rows - self.hr + 32 <= self.hr and (rows - self.hr) % 8 == 0
        self.ar = round_up(max(self.span, self.wl) + pitch, pitch)
        self.starts = [LANES + b * self.w - SIDE for b in range(devices)]
        self.ka = round_up(max(s % LANES for s in self.starts) + self.span, LANES)
        self.xw = max(s // LANES * LANES for s in self.starts) + self.ka


def iota(shape, axis):
    return lax.broadcasted_iota(jnp.int32, shape, axis)


def phase_rows(sz, z, phase_ref, col_ref, t_ref, a_ref):
    taps = col_ref.shape[2]
    t_ref[...] = jnp.zeros_like(t_ref)
    for p in range(sz.pitch):
        row = col_ref[phase_ref[z, p], pl.ds(z, 1), :]
        t_ref[p : p + 1, 0:taps] = row.astype(BF16).astype(F32)
    base = t_ref[0 : sz.pitch, :]
    for k in range(sz.ar // sz.pitch):
        a_ref[k * sz.pitch : (k + 1) * sz.pitch, :] = base


def spread_matrix(sz, reach, a_ref):
    first = (-SIDE) % sz.pitch
    rows = a_ref[first : first + sz.span, 0 : sz.wl]
    rows = pltpu.roll(rows, sz.wl - RMAX - SIDE, 1, stride=1, stride_axis=0)
    col, row = iota(rows.shape, 1), iota(rows.shape, 0)
    return jnp.where((jnp.abs(col - row + SIDE) <= reach) & (col < sz.w), rows, 0.0)


def gather_matrix(sz, reach, a_ref):
    rows = pltpu.roll(a_ref[0 : sz.wl, 0 : sz.kp], SIDE - RMAX, 1, stride=1, stride_axis=0)
    col, row = iota(rows.shape, 1), iota(rows.shape, 0)
    rows = jnp.where((jnp.abs(col - SIDE - row) <= reach) & (row < sz.w), rows, 0.0)
    return rows.T[0 : sz.span, :]


def by_block(sz, matrix):
    def zeros(count):
        return [jnp.zeros((count, sz.wl), F32)] if count else []

    lead = sz.w - (sz.wl - LANES) - 2 * SIDE
    parts = [matrix[SIDE : SIDE + sz.w]] + zeros(sz.wl - sz.w)
    parts += [matrix[SIDE + sz.w :]] + zeros(lead) + [matrix[0:SIDE]] + zeros(sz.wl - sz.w)
    return jnp.concatenate(parts, axis=0).astype(BF16)


def by_tile(sz, matrix):
    def zeros(count):
        return [jnp.zeros((count, sz.wl), F32)] if count else []

    here = min(sz.w, LANES)
    lead = sz.w - (sz.wl - LANES) - 2 * SIDE
    first = [matrix[SIDE : SIDE + here]] + zeros(LANES - here)
    first += [matrix[SIDE + here : SIDE + here + SIDE]] + zeros(lead)
    first += [matrix[0:SIDE]] + zeros(sz.wl - sz.w)
    parts = [jnp.concatenate(first, axis=0)[:, 0:LANES]]
    if sz.tiles == 2:
        second = [matrix[SIDE : 2 * SIDE + sz.w]] + zeros(sz.wl - sz.w - SIDE)
        parts.append(jnp.concatenate(second, axis=0)[:, LANES:])
    return [part.astype(BF16) for part in parts]


def row_matrix(sz, z, reach, row_ref):
    taps = row_ref.shape[1]
    lane = iota((1, sz.el), 1)
    row = row_ref[pl.ds(z, 1), :].astype(BF16).astype(F32)
    row = jnp.concatenate([row, jnp.zeros((1, sz.el - taps), F32)], axis=1)
    row = jnp.where(jnp.abs(lane - RMAX) <= reach, row, 0.0)
    wide = jnp.broadcast_to(row, (sz.rp, sz.el))
    wide = pltpu.roll(wide, 0, 1, stride=1, stride_axis=0)
    return jnp.where(iota(wide.shape, 0) < sz.rows, wide, 0.0)


class Windows:
    def __init__(self, sz, height, main_ref, side_ref, group):
        self.group = group
        self.sz, self.height, self.main, self.side = sz, height, main_ref, side_ref

    def clear_sides(self):
        self.side[...] = jnp.zeros_like(self.side)

    def put(self, b, row, x):
        sz = self.sz

        def rows(block):
            at = block * self.height + row
            if not isinstance(at, int):
                at = pl.multiple_of(at, 16)
            return pl.ds(at, x.shape[0])

        self.main[rows(b), :] = x
        self.side[rows(b), 0:HALF] = x[:, 0:HALF]
        self.side[rows(b + 2), HALF:] = x[:, sz.wl - HALF :]

    def products(self, matrix):
        sz, height = self.sz, self.height
        for first in range(0, sz.n, self.group):
            count = self.group * height
            main = self.main[first * height : first * height + count, :]
            side = self.side[(first + 1) * height : (first + 1) * height + count, :]
            window = jnp.concatenate([main, side], axis=1)
            out = jnp.dot(window, matrix, preferred_element_type=F32).astype(BF16)
            for k in range(self.group):
                yield first + k, out[k * height : (k + 1) * height, :]


class PairWindows:
    def __init__(self, sz, main_ref, side_ref):
        self.sz, self.main, self.side = sz, main_ref, side_ref

    def clear(self):
        sz = self.sz
        self.main[sz.n * sz.hr :, :] = jnp.zeros((sz.hr, sz.wl), BF16)
        self.side[...] = jnp.zeros_like(self.side)

    def put(self, b, x):
        sz = self.sz

        def rows(block):
            return pl.ds(pl.multiple_of(block * sz.hr, 16), sz.hr)

        self.main[rows(b + 1), 0 : sz.w] = x[:, 0 : sz.w]
        if sz.tiles == 2:
            self.main[rows(b), sz.w : sz.w + SIDE] = x[:, 0:SIDE]
            self.side[rows(b + 1), 0:HALF] = x[:, LANES : LANES + HALF]
        else:
            self.side[rows(b), 0:HALF] = x[:, 0:HALF]
        self.side[rows(b + 2), HALF:] = x[:, sz.wl - HALF :]

    def products(self, pair_ref, group):
        sz = self.sz
        for first in range(0, sz.n, group):
            rows = slice((first + 1) * sz.hr, (first + 1 + group) * sz.hr)
            for tile in range(sz.tiles):
                if tile == 0:
                    window = jnp.concatenate([self.main[rows, 0:LANES], self.side[rows, :]], axis=1)
                else:
                    window = self.main[rows, :]
                out = jnp.dot(window, pair_ref[tile], preferred_element_type=F32).astype(BF16)
                for k in range(group):
                    for plane in range(2):
                        lanes = slice(plane * LANES, (plane + 1) * LANES)
                        yield first + k, plane, tile, out[k * sz.hr : (k + 1) * sz.hr, lanes]


def pack(sz, x):
    valid = iota(x.shape, x.ndim - 1) < sz.w
    least = jnp.min(jnp.where(valid, x, jnp.inf), axis=-1, keepdims=True)
    base = (2.0 * least).astype(BF16).astype(F32)
    return jnp.where(valid, x - base, base).astype(BF16)


def unpack(sz, y):
    y = y.astype(F32)
    valid = iota(y.shape, y.ndim - 1) < sz.w
    return jnp.where(valid, y + y[..., sz.w : sz.w + 1], 0.0)


def rows_forward(sz, rc_ref, s_ref, keep_ref, send_ref):
    coef = rc_ref[...]
    for b in range(sz.n):
        out = jnp.dot(coef, s_ref[b], preferred_element_type=F32)
        send_ref[b] = pack(sz, out[0 : sz.hr, :])
        keep_ref[b] = out[sz.hr :, :]


def backward(sz, pair, ratio, wb_ref, rt_ref, own_ref, g_ref):
    for b, plane, tile, out in ratio.products(wb_ref.at[pair], 2):
        g_ref[plane, b, 0 : sz.hr, tile * LANES : (tile + 1) * LANES] = out
    for plane in range(2):
        z = 2 * pair + plane
        for b in range(sz.n):
            rows = jnp.concatenate([own_ref[z, b], g_ref[plane, b]], axis=0)
            back = jnp.dot(rt_ref[z], rows, preferred_element_type=F32)
            yield z, b, back[0 : sz.rows, :]


def block_norm(sz, b, icn):
    kind = 1 if b == 0 else 2 if b == sz.n - 1 else 0
    return icn[kind : kind + 1, :]


def place_ratio(sz, me, stack_ref, main_ref, side_ref):
    ratio = PairWindows(sz, main_ref, side_ref)
    ratio.clear()
    for j in range(sz.half):
        for k in range(2):
            ratio.put(2 * ((me // 2) ^ j) + k, stack_ref[j, k])
    return ratio


def first_kernel(
    sz, me_ref, radius_hbm, phase_hbm, row_hbm, col_hbm, vol_hbm,
    rc_ref, keep_ref, send_ref,
    radius_ref, phase_ref, row_ref, col_ref, vol_ref, t_ref, a_ref, m_ref, x_ref, s_ref, sems,
):
    pairs = ((radius_hbm, radius_ref), (phase_hbm, phase_ref), (row_hbm, row_ref), (col_hbm, col_ref))
    small = [pltpu.make_async_copy(a, b, sems.at[i]) for i, (a, b) in enumerate(pairs)]
    large = [
        pltpu.make_async_copy(vol_hbm.at[z], vol_ref.at[z], sems.at[4 + z])
        for z in range(sz.planes)
    ]
    for copy in small + large:
        copy.start()
    part = lax.rem(me_ref[0], 2)
    m_ref[...] = jnp.zeros_like(m_ref)
    x_ref[...] = jnp.zeros_like(x_ref)
    for copy in small:
        copy.wait()
    for z in range(sz.planes):
        reach = radius_ref[z]
        phase_rows(sz, z, phase_ref, col_ref, t_ref, a_ref)
        matrix = spread_matrix(sz, reach, a_ref)
        rest = jnp.zeros((round_up(sz.span, 16) - sz.span, sz.wl), F32)
        matrix = jnp.concatenate([matrix, rest], axis=0) if rest.shape[0] else matrix
        m_ref[z, LANES : LANES + matrix.shape[0], :] = matrix.astype(BF16)
        rt = row_matrix(sz, z, reach, row_ref)
        rt = rt.T.astype(BF16)
        lanes = slice(z * sz.rp, (z + 1) * sz.rp)
        rc_ref[pl.ds(pl.multiple_of((1 - part) * sz.hr, sz.hr), sz.hr), lanes] = rt[0 : sz.hr, :]
        rc_ref[pl.ds(pl.multiple_of(part * sz.hr, sz.hr), sz.hr), lanes] = rt[sz.hr : sz.ep, :]
    for z in range(sz.planes):
        large[z].wait()
        x = jnp.concatenate([vol_ref[z], jnp.zeros((sz.rp - sz.rows, sz.cols), F32)], axis=0)
        x_ref[z, :, LANES : LANES + sz.cols] = x.astype(BF16)
        for b, start in enumerate(sz.starts):
            shift = start % LANES
            window = x_ref[z, :, start - shift : start - shift + sz.ka]
            matrix = m_ref[z, LANES - shift : LANES - shift + sz.ka, :]
            out = jnp.dot(window, matrix, preferred_element_type=F32)
            s_ref[b, z * sz.rp : (z + 1) * sz.rp, :] = out.astype(BF16)
    rows_forward(sz, rc_ref, s_ref, keep_ref, send_ref)


def table_kernel(
    sz, me_ref, strip_ref, radius_hbm, phase_hbm, row_hbm, col_hbm, after_ref,
    wf_ref, wb_ref, rt_ref, irn_ref, icn_ref,
    radius_ref, phase_ref, row_ref, col_ref, t_ref, a_ref, sems,
):
    pairs = ((radius_hbm, radius_ref), (phase_hbm, phase_ref), (row_hbm, row_ref), (col_hbm, col_ref))
    small = [pltpu.make_async_copy(a, b, sems.at[i]) for i, (a, b) in enumerate(pairs)]
    for copy in small:
        copy.start()
    for copy in small:
        copy.wait()
    kind, col = iota((8, 2 * LANES), 0), iota((8, 2 * LANES), 1)
    missing = [(kind == 1) & (col >= LANES + HALF)]
    if sz.tiles == 2:
        missing.append((kind == 2) & (col >= sz.w))
    else:
        missing[0] |= (kind == 2) & (col >= LANES) & (col < LANES + HALF)
    ones = [jnp.where(part, 0.0, 1.0).astype(BF16) for part in missing]
    for z in range(sz.planes):
        reach = radius_ref[z]
        phase_rows(sz, z, phase_ref, col_ref, t_ref, a_ref)
        wf_ref[z] = by_block(sz, spread_matrix(sz, reach, a_ref))
        parts = by_tile(sz, gather_matrix(sz, reach, a_ref))
        for tile, part in enumerate(parts):
            lanes = slice(z % 2 * LANES, (z % 2 + 1) * LANES)
            wb_ref[z // 2, tile, :, lanes] = part
        norm = [jnp.dot(a, b, preferred_element_type=F32) for a, b in zip(ones, parts)]
        norm = jnp.concatenate(norm, axis=1)
        icn_ref[z] = jnp.where(norm > 0.0, 1.0 / norm, 0.0)
        rt = row_matrix(sz, z, reach, row_ref)
        lane = iota(rt.shape, 1)
        top = jnp.where(lane < sz.hr, rt, 0.0)
        bottom = jnp.where((lane >= sz.hr) & (lane < sz.ep), rt, 0.0)
        bottom = pltpu.roll(bottom, sz.hp - sz.hr, 1)
        both = top + bottom
        turned = pltpu.roll(both, sz.hp, 1)
        rt_ref[z] = jnp.where(lax.rem(me_ref[0], 2) == 0, both, turned).astype(BF16)
        row = strip_ref[0] * sz.rows + iota(rt.shape, 1) - RMAX
        norm = jnp.sum(jnp.where((row >= 0) & (row < sz.total), rt, 0.0), axis=1, keepdims=True)
        irn_ref[z] = jnp.where(norm > 0.0, 1.0 / norm, 0.0)


def block_kernel(sz, vol_hbm, after_ref, blocks_ref, vol_ref, sems, planes):
    copies = [
        pltpu.make_async_copy(vol_hbm.at[z], vol_ref.at[i], sems.at[i])
        for i, z in enumerate(planes)
    ]
    for copy in copies:
        copy.start()
    for z, copy in enumerate(copies):
        copy.wait()
        for b in range(sz.n):
            block = vol_ref[z, :, b * sz.w : (b + 1) * sz.w]
            if sz.wl > sz.w:
                block = jnp.concatenate([block, jnp.zeros((sz.rows, sz.wl - sz.w), F32)], axis=1)
            blocks_ref[z, b] = block


def core_sum_kernel(sz, me_ref, keep_ref, recv_ref, own_ref, *out_refs):
    mine = me_ref[0] // 2
    for j, ref in enumerate((own_ref, *out_refs)):
        blocks = pl.ds(2 * (mine ^ j), 2)
        total = keep_ref[blocks] + unpack(sz, recv_ref[blocks])
        ref[...] = total if j == 0 else pack(sz, total)


def chip_sum_kernel(sz, me_ref, after_ref, own_ref, meas_ref, *refs, first):
    recv_refs, (sum_ref, edge_ref) = refs[:-2], refs[-2:]
    total = own_ref[...]
    for ref in recv_refs:
        total = total + unpack(sz, ref[...])
    sum_ref[...] = total
    edges = []
    for at, row in ((0, 0), (sz.rows - sz.hr, sz.rows - SIDE)):
        parts = [total[:, at : at + 32, :]]
        if first:
            meas = meas_ref[:, row : row + SIDE, :]
            high = meas.astype(BF16).astype(F32)
            parts += [high, meas - high]
        edges.append(jnp.concatenate(parts, axis=1))
    top, bottom = edges
    edge_ref[...] = jnp.where(lax.rem(me_ref[0], 2) == 0, top, bottom).astype(BF16)


def ratio_kernel(
    sz, me_ref, strip_ref, after_ref, sum_ref, meas_ref, edge_ref, first_edge_ref,
    ratio_ref, s_ref, m_ref,
):
    part = lax.rem(me_ref[0], 2)
    s_ref[...] = sum_ref[...]
    m_ref[...] = jnp.zeros_like(m_ref)
    edge, first_edge = edge_ref[...].astype(F32), first_edge_ref[...].astype(F32)
    alone = jnp.where(part == 0, strip_ref[0] == 0, (strip_ref[0] + 1) * sz.rows == sz.total)
    rows = jnp.where(alone, 0.0, edge[:, 0:32, :])
    meas = first_edge[:, 32:48, :] + first_edge[:, 48:64, :]

    @pl.when(part == 0)
    def _():
        s_ref[:, 0:32, :] += rows
        m_ref[:, 0:RMAX, :] = meas[:, SIDE - RMAX :, :]
        m_ref[:, RMAX : sz.hr, :] = meas_ref[:, 0 : sz.hr - RMAX, :]

    @pl.when(part == 1)
    def _():
        first = sz.rows - sz.hr
        s_ref[:, first : first + 32, :] += rows
        m_ref[:, 0 : first + RMAX, :] = meas_ref[:, sz.hr - RMAX :, :]
        m_ref[:, first + RMAX : first + 2 * RMAX, :] = meas[:, 0:RMAX, :]

    row = part * sz.hr + iota(s_ref.shape, 1)
    spot = strip_ref[0] * sz.rows + row - RMAX
    inside = (row < sz.e) & (spot >= 0) & (spot < sz.total) & (iota(s_ref.shape, 2) < sz.w)
    ratio_ref[...] = jnp.where(inside, m_ref[...] / s_ref[...], 0.0).astype(BF16)


def stack_kernel(sz, after_ref, *refs, order):
    for j, ref in zip(order, refs[:-1]):
        refs[-1][j] = ref[...]


def ahead_kernel(sz, me_ref, same_ref, wb_ref, own_ref, ratio_ref, ratio_side_ref):
    ratio = place_ratio(sz, me_ref[0], same_ref, ratio_ref, ratio_side_ref)
    own_ref[:, :, sz.hr :, :] = jnp.zeros((sz.planes, sz.n, sz.hp - sz.hr, sz.wl), BF16)
    for pair in range(sz.planes // 2):
        for b, plane, tile, out in ratio.products(wb_ref.at[pair], 2):
            lanes = slice(tile * LANES, (tile + 1) * LANES)
            own_ref[2 * pair + plane, b, 0 : sz.hr, lanes] = out


def middle_kernel(
    sz, me_ref, own_ref, other_ref, wf_ref, wb_ref, rt_ref, irn_ref, icn_ref, rc_ref, before_ref, after_ref,
    new_ref, keep_ref, send_ref,
    ratio_ref, ratio_side_ref, g_ref, x_ref, x_side_ref, s_ref,
):
    ratio = place_ratio(sz, me_ref[0], other_ref, ratio_ref, ratio_side_ref)
    g_ref[:, :, sz.hr :, :] = jnp.zeros((2, sz.n, sz.hp - sz.hr, sz.wl), BF16)
    estimate = Windows(sz, sz.rp, x_ref, x_side_ref, 4)
    estimate.clear_sides()
    lead = jnp.zeros((sz.rp - sz.rows, sz.wl), F32)
    split = before_ref.shape[0]
    for pair in range(sz.planes // 2):
        for z, b, back in backward(sz, pair, ratio, wb_ref, rt_ref, own_ref, g_ref):
            old = before_ref[z, b] if z < split else after_ref[z - split, b]
            if b == 0:
                icn, irn = icn_ref[z], irn_ref[z][0 : sz.rows]
            norm = irn * block_norm(sz, b, icn)
            new = old * back * norm
            new_ref[z, b] = new
            estimate.put(b, 0, jnp.concatenate([new, lead]).astype(BF16))
            if b == sz.n - 1:
                for k, out in estimate.products(wf_ref[z]):
                    s_ref[k, z * sz.rp : (z + 1) * sz.rp, :] = out
    rows_forward(sz, rc_ref, s_ref, keep_ref, send_ref)


def last_kernel(
    sz, me_ref, own_ref, other_ref, wb_ref, rt_ref, irn_ref, icn_ref, vol_ref,
    out_hbm, ratio_ref, ratio_side_ref, g_ref, out_ref, sems,
):
    ratio = place_ratio(sz, me_ref[0], other_ref, ratio_ref, ratio_side_ref)
    g_ref[:, :, sz.hr :, :] = jnp.zeros((2, sz.n, sz.hp - sz.hr, sz.wl), BF16)
    middle = sz.cols // 2 // LANES * LANES
    lanes = (slice(0, middle), slice(middle, sz.cols))
    copies = [
        [
            pltpu.make_async_copy(out_ref.at[z, :, k], out_hbm.at[z, :, k], sems.at[z, i])
            for i, k in enumerate(lanes)
        ]
        for z in range(sz.planes)
    ]
    for pair in range(sz.planes // 2):
        for z, b, back in backward(sz, pair, ratio, wb_ref, rt_ref, own_ref, g_ref):
            if b == 0:
                icn, irn = icn_ref[z], irn_ref[z][0 : sz.rows]
            norm = irn * block_norm(sz, b, icn)
            new = vol_ref[z, b] * back * norm
            out_ref[z, :, b * sz.w : (b + 1) * sz.w] = new[:, 0 : sz.w]
            if b == sz.n // 2 - 1:
                copies[z][0].start()
            if b == sz.n - 1:
                copies[z][1].start()
    for plane in copies:
        for copy in plane:
            copy.wait()


SMEM = pl.BlockSpec(memory_space=pltpu.SMEM)
VMEM = pl.BlockSpec(memory_space=pltpu.VMEM)
ANY = pl.BlockSpec(memory_space=pl.ANY)
HBM = pl.BlockSpec(memory_space=pltpu.HBM)


def shape(dims, dtype):
    return jax.ShapeDtypeStruct(dims, dtype)


def call(kernel, sz, name, in_specs, out_specs, out_shape, scratch, args, mib, micros=1):
    return pl.pallas_call(
        functools.partial(kernel, sz),
        in_specs=in_specs,
        out_specs=out_specs,
        out_shape=out_shape,
        scratch_shapes=scratch,
        compiler_params=pltpu.CompilerParams(vmem_limit_bytes=mib * 1024 * 1024),
        cost_estimate=pl.CostEstimate(
            flops=0, bytes_accessed=micros * 3_000_000, transcendentals=0
        ),
        name=name,
    )(*args)


def local(volume, measured, row_taps, col_taps, phase_map, radius):
    n = lax.axis_size("depth")
    strips = lax.axis_size("strip")
    planes, rows, cols = volume.shape
    sz = Sizes(planes, rows, strips, cols, n, phase_map.shape[1])
    me = lax.axis_index("depth")
    strip = lax.axis_index("strip")
    me_arg = (me ^ (strip % 2)).reshape(1).astype(jnp.int32)
    strip_arg = strip.reshape(1).astype(jnp.int32)
    to_core = [(i, i ^ 1) for i in range(n)]
    to_chip = [[(i, i ^ (2 * j)) for i in range(n)] for j in range(1, sz.half)]
    order_rs = range(sz.half - 1)[::-1]
    order_ag = range(sz.half - 1)
    to_strip = []
    for chip in range(sz.half):
        for lower in range(1, strips):
            row = (2 * chip + lower % 2) * strips
            to_strip += [(row + lower, row + lower - 1), (row + lower - 1, row + lower)]
        for edge, core in ((0, 0), (strips - 1, strips % 2)):
            pair = [(2 * c + core) * strips + edge for c in (chip, chip ^ 1)]
            to_strip.append(tuple(pair))

    volume = pltpu.with_memory_space_constraint(volume, pltpu.HBM)
    meas = lax.dynamic_slice_in_dim(measured, (me // 2) * 2 * sz.w, 2 * sz.w, axis=1)
    meas = jnp.stack([meas[:, 0 : sz.w], meas[:, sz.w :]])
    meas = jnp.pad(meas, ((0, 0), (0, 0), (0, sz.wl - sz.w)))
    by_family = col_taps.transpose(1, 0, 2)

    flat = shape((2, sz.hr, sz.wl), BF16)
    flat32 = shape((2, sz.hr, sz.wl), F32)
    halves = [shape((n, sz.hr, sz.wl), F32), shape((n, sz.hr, sz.wl), BF16)]
    blocked = shape((planes, n, rows, sz.wl), F32)
    tap_args = tuple(
        pltpu.with_memory_space_constraint(x, pltpu.HBM)
        for x in (radius, phase_map, row_taps, by_family)
    )
    tap_scratch = [
        pltpu.SMEM(radius.shape, jnp.int32),
        pltpu.SMEM(phase_map.shape, jnp.int32),
        pltpu.VMEM(row_taps.shape, F32),
        pltpu.VMEM(by_family.shape, F32),
    ]
    row_scratch = [
        pltpu.VMEM((round_up(sz.pitch, 8), sz.kp), F32),
        pltpu.VMEM((sz.ar, sz.kp), F32),
    ]
    s_scratch = pltpu.VMEM((n, planes * sz.rp, sz.wl), BF16)
    place_scratch = [
        pltpu.VMEM(((n + 1) * sz.hr, sz.wl), BF16),
        pltpu.VMEM(((n + 2) * sz.hr, LANES), BF16),
    ]
    ratio_scratch = place_scratch + [pltpu.VMEM((2, n, sz.hp, sz.wl), BF16)]
    x_scratch = [
        pltpu.VMEM((n * sz.rp, sz.wl), BF16),
        pltpu.VMEM(((n + 2) * sz.rp, LANES), BF16),
    ]
    vol_scratch = pltpu.VMEM(volume.shape, F32)

    rc, keep, send = call(
        first_kernel, sz, "first",
        [SMEM] + [HBM] * 5,
        [VMEM] * 3,
        [shape((sz.ep, planes * sz.rp), BF16), *halves],
        tap_scratch + [vol_scratch] + row_scratch
        + [
            pltpu.VMEM((planes, LANES + sz.ka, sz.wl), BF16),
            pltpu.VMEM((planes, sz.rp, sz.xw), BF16),
            s_scratch,
            pltpu.SemaphoreType.DMA((4 + planes,)),
        ],
        (me_arg, *tap_args, volume),
        24, 4,
    )

    def block_planes(which, after):
        return call(
            functools.partial(block_kernel, planes=tuple(which)), sz, "blocks",
            [HBM, ANY], VMEM, shape((len(which), n, rows, sz.wl), F32),
            [
                pltpu.VMEM((len(which), rows, cols), F32),
                pltpu.SemaphoreType.DMA((len(which),)),
            ],
            (volume, after), 12, 2,
        )

    tables, current = None, None
    for iteration in range(ITERS):
        recv = lax.ppermute(send, "depth", to_core)
        own, *sends = call(
            core_sum_kernel, sz, "core_sum",
            [SMEM, VMEM, VMEM],
            [VMEM] * sz.half,
            [flat32] + [flat] * (sz.half - 1),
            [], (me_arg, keep, recv), 4,
        )
        if tables is None:
            wf, *tables = call(
                table_kernel, sz, "tables",
                [SMEM] * 2 + [HBM] * 4 + [ANY],
                [VMEM] * 5,
                [
                    shape((planes, sz.kb, sz.wl), BF16),
                    shape((planes // 2, sz.tiles, 2 * LANES, 2 * LANES), BF16),
                    shape((planes, sz.rp, sz.el), BF16),
                    shape((planes, sz.rp, 1), F32),
                    shape((planes, 8, sz.wl), F32),
                ],
                tap_scratch + row_scratch + [pltpu.SemaphoreType.DMA((4,))],
                (me_arg, strip_arg, *tap_args, own),
                8, 2,
            )
        recvs = [lax.ppermute(sends[j], "depth", to_chip[j]) for j in order_rs]
        total, edge = call(
            functools.partial(chip_sum_kernel, first=iteration == 0), sz, "chip_sum",
            [SMEM, ANY] + [VMEM] * (2 + len(recvs)),
            [VMEM] * 2,
            [flat32, shape((2, 64 if iteration == 0 else 32, sz.wl), BF16)],
            [], (me_arg, tables[3], own, meas, *recvs), 4,
        )
        edge = lax.ppermute(edge, ("depth", "strip"), to_strip)
        first_edge = edge if iteration == 0 else first_edge
        if iteration == 0:
            before = block_planes(range(planes // 2), total)
        ratio = call(
            ratio_kernel, sz, "ratio",
            [SMEM] * 2 + [ANY] + [VMEM] * 4,
            VMEM,
            flat,
            [pltpu.VMEM(flat32.shape, F32)] * 2,
            (me_arg, strip_arg, before, total, meas, edge, first_edge), 4,
        )
        chips = [lax.ppermute(ratio, "depth", to_chip[j]) for j in order_ag]
        if iteration == 0:
            after = block_planes(range(planes // 2, planes), ratio)
        same = call(
            functools.partial(stack_kernel, order=(0, *[j + 1 for j in order_ag])), sz, "stack",
            [ANY] + [VMEM] * sz.half, VMEM, shape((sz.half,) + flat.shape, BF16),
            [], (after, ratio, *chips), 4,
        )
        other = lax.ppermute(same, "depth", to_core)
        own = call(
            ahead_kernel, sz, "ahead",
            [SMEM] + [VMEM] * 2, VMEM,
            shape((planes, n, sz.hp, sz.wl), BF16),
            place_scratch, (me_arg, same, tables[0]), 8,
        )
        if iteration < ITERS - 1:
            current, keep, send = call(
                middle_kernel, sz, "middle",
                [SMEM] + [VMEM] * 10,
                [VMEM] * 3,
                [blocked, *halves],
                ratio_scratch + x_scratch + [s_scratch],
                (me_arg, own, other, wf, *tables, rc, before, after),
                16, 5,
            )
        else:
            current = call(
                last_kernel, sz, "last",
                [SMEM] + [VMEM] * 7,
                HBM,
                shape(volume.shape, F32),
                ratio_scratch + [vol_scratch, pltpu.SemaphoreType.DMA((planes, 2))],
                (me_arg, own, other, *tables, current),
                16, 5,
            )
    return current


def solution(mesh):
    return jax.shard_map(
        local,
        mesh=mesh,
        in_specs=(
            P("depth", "strip", None),
            P("strip", None),
            P("depth", None),
            P("depth", None, None),
            P("depth", None),
            P("depth"),
        ),
        out_specs=P("depth", "strip", None),
        check_vma=False,
    )
```

```python
import functools

import jax
import jax.numpy as jnp
from jax import lax
from jax.experimental import pallas as pl
from jax.experimental.pallas import tpu as pltpu
from jax.sharding import PartitionSpec as P

RMAX = 15
ITERS = 2
SIDE = 16
LANES = 128
HALF = LANES // 2

F32 = jnp.float32
BF16 = jnp.bfloat16


def round_up(value, step):
    return -(-value // step) * step


class Sizes:
    def __init__(self, planes, rows, strips, cols, devices, pitch):
        self.total = rows * strips
        self.planes, self.rows, self.cols, self.n, self.pitch = planes, rows, cols, devices, pitch
        self.w = cols // devices
        self.half = devices // 2
        assert cols % devices == 0 and self.w % pitch == 0 and self.w >= 2 * SIDE
        assert devices >= 4 and devices & (devices - 1) == 0 and rows >= 2 * RMAX and rows % 8 == 0
        self.wl = round_up(self.w, LANES)
        self.span = self.w + 2 * SIDE
        self.kp = round_up(self.span, LANES)
        self.kb = self.wl + LANES
        self.tiles = self.wl // LANES
        assert self.tiles <= 2 and planes % 2 == 0 and self.wl > self.w
        self.rp = round_up(rows, LANES)
        self.e = rows + 2 * RMAX
        self.ep = round_up(self.e, 32)
        self.hr = self.ep // 2
        self.hp = round_up(self.hr, LANES)
        self.el = round_up(self.ep, LANES)
        assert self.el == 2 * self.hp
        assert 32 <= rows - self.hr and rows - self.hr + 32 <= self.hr and (rows - self.hr) % 8 == 0
        self.ar = round_up(max(self.span, self.wl) + pitch, pitch)
        self.starts = [LANES + b * self.w - SIDE for b in range(devices)]
        self.ka = round_up(max(s % LANES for s in self.starts) + self.span, LANES)
        self.xw = max(s // LANES * LANES for s in self.starts) + self.ka


def iota(shape, axis):
    return lax.broadcasted_iota(jnp.int32, shape, axis)


def phase_rows(sz, z, phase_ref, col_ref, t_ref, a_ref):
    taps = col_ref.shape[2]
    t_ref[...] = jnp.zeros_like(t_ref)
    for p in range(sz.pitch):
        row = col_ref[phase_ref[z, p], pl.ds(z, 1), :]
        t_ref[p : p + 1, 0:taps] = row.astype(BF16).astype(F32)
    base = t_ref[0 : sz.pitch, :]
    for k in range(sz.ar // sz.pitch):
        a_ref[k * sz.pitch : (k + 1) * sz.pitch, :] = base


def spread_matrix(sz, reach, a_ref):
    first = (-SIDE) % sz.pitch
    rows = a_ref[first : first + sz.span, 0 : sz.wl]
    rows = pltpu.roll(rows, sz.wl - RMAX - SIDE, 1, stride=1, stride_axis=0)
    col, row = iota(rows.shape, 1), iota(rows.shape, 0)
    return jnp.where((jnp.abs(col - row + SIDE) <= reach) & (col < sz.w), rows, 0.0)


def gather_matrix(sz, reach, a_ref):
    rows = pltpu.roll(a_ref[0 : sz.wl, 0 : sz.kp], SIDE - RMAX, 1, stride=1, stride_axis=0)
    col, row = iota(rows.shape, 1), iota(rows.shape, 0)
    rows = jnp.where((jnp.abs(col - SIDE - row) <= reach) & (row < sz.w), rows, 0.0)
    return rows.T[0 : sz.span, :]


def by_block(sz, matrix):
    def zeros(count):
        return [jnp.zeros((count, sz.wl), F32)] if count else []

    lead = sz.w - (sz.wl - LANES) - 2 * SIDE
    parts = [matrix[SIDE : SIDE + sz.w]] + zeros(sz.wl - sz.w)
    parts += [matrix[SIDE + sz.w :]] + zeros(lead) + [matrix[0:SIDE]] + zeros(sz.wl - sz.w)
    return jnp.concatenate(parts, axis=0).astype(BF16)


def by_tile(sz, matrix):
    def zeros(count):
        return [jnp.zeros((count, sz.wl), F32)] if count else []

    here = min(sz.w, LANES)
    lead = sz.w - (sz.wl - LANES) - 2 * SIDE
    first = [matrix[SIDE : SIDE + here]] + zeros(LANES - here)
    first += [matrix[SIDE + here : SIDE + here + SIDE]] + zeros(lead)
    first += [matrix[0:SIDE]] + zeros(sz.wl - sz.w)
    parts = [jnp.concatenate(first, axis=0)[:, 0:LANES]]
    if sz.tiles == 2:
        second = [matrix[SIDE : 2 * SIDE + sz.w]] + zeros(sz.wl - sz.w - SIDE)
        parts.append(jnp.concatenate(second, axis=0)[:, LANES:])
    return [part.astype(BF16) for part in parts]


def row_matrix(sz, z, reach, row_ref):
    taps = row_ref.shape[1]
    lane = iota((1, sz.el), 1)
    row = row_ref[pl.ds(z, 1), :].astype(BF16).astype(F32)
    row = jnp.concatenate([row, jnp.zeros((1, sz.el - taps), F32)], axis=1)
    row = jnp.where(jnp.abs(lane - RMAX) <= reach, row, 0.0)
    wide = jnp.broadcast_to(row, (sz.rp, sz.el))
    wide = pltpu.roll(wide, 0, 1, stride=1, stride_axis=0)
    return jnp.where(iota(wide.shape, 0) < sz.rows, wide, 0.0)


class Windows:
    def __init__(self, sz, height, main_ref, side_ref, group):
        self.group = group
        self.sz, self.height, self.main, self.side = sz, height, main_ref, side_ref

    def clear_sides(self):
        self.side[...] = jnp.zeros_like(self.side)

    def put(self, b, row, x):
        sz = self.sz

        def rows(block):
            at = block * self.height + row
            if not isinstance(at, int):
                at = pl.multiple_of(at, 16)
            return pl.ds(at, x.shape[0])

        self.main[rows(b), :] = x
        self.side[rows(b), 0:HALF] = x[:, 0:HALF]
        self.side[rows(b + 2), HALF:] = x[:, sz.wl - HALF :]

    def products(self, matrix):
        sz, height = self.sz, self.height
        for first in range(0, sz.n, self.group):
            count = self.group * height
            main = self.main[first * height : first * height + count, :]
            side = self.side[(first + 1) * height : (first + 1) * height + count, :]
            window = jnp.concatenate([main, side], axis=1)
            out = jnp.dot(window, matrix, preferred_element_type=F32).astype(BF16)
            for k in range(self.group):
                yield first + k, out[k * height : (k + 1) * height, :]


class PairWindows:
    def __init__(self, sz, main_ref, side_ref):
        self.sz, self.main, self.side = sz, main_ref, side_ref

    def clear(self):
        sz = self.sz
        self.main[sz.n * sz.hr :, :] = jnp.zeros((sz.hr, sz.wl), BF16)
        self.side[...] = jnp.zeros_like(self.side)

    def put(self, b, x):
        sz = self.sz

        def rows(block):
            return pl.ds(pl.multiple_of(block * sz.hr, 16), sz.hr)

        self.main[rows(b + 1), 0 : sz.w] = x[:, 0 : sz.w]
        if sz.tiles == 2:
            self.main[rows(b), sz.w : sz.w + SIDE] = x[:, 0:SIDE]
            self.side[rows(b + 1), 0:HALF] = x[:, LANES : LANES + HALF]
        else:
            self.side[rows(b), 0:HALF] = x[:, 0:HALF]
        self.side[rows(b + 2), HALF:] = x[:, sz.wl - HALF :]

    def products(self, pair_ref, group):
        sz = self.sz
        for first in range(0, sz.n, group):
            rows = slice((first + 1) * sz.hr, (first + 1 + group) * sz.hr)
            for tile in range(sz.tiles):
                if tile == 0:
                    window = jnp.concatenate([self.main[rows, 0:LANES], self.side[rows, :]], axis=1)
                else:
                    window = self.main[rows, :]
                out = jnp.dot(window, pair_ref[tile], preferred_element_type=F32).astype(BF16)
                for k in range(group):
                    for plane in range(2):
                        lanes = slice(plane * LANES, (plane + 1) * LANES)
                        yield first + k, plane, tile, out[k * sz.hr : (k + 1) * sz.hr, lanes]


def pack(sz, x):
    valid = iota(x.shape, x.ndim - 1) < sz.w
    least = jnp.min(jnp.where(valid, x, jnp.inf), axis=-1, keepdims=True)
    base = (2.0 * least).astype(BF16).astype(F32)
    return jnp.where(valid, x - base, base).astype(BF16)


def unpack(sz, y):
    y = y.astype(F32)
    valid = iota(y.shape, y.ndim - 1) < sz.w
    return jnp.where(valid, y + y[..., sz.w : sz.w + 1], 0.0)


def rows_forward(sz, rc_ref, s_ref, keep_ref, send_ref):
    coef = rc_ref[...]
    for b in range(sz.n):
        out = jnp.dot(coef, s_ref[b], preferred_element_type=F32)
        send_ref[b] = out[0 : sz.hr, :].astype(BF16)
        keep_ref[b] = out[sz.hr :, :]


def backward(sz, pair, ratio, wb_ref, rt_ref, own_ref, g_ref):
    for b, plane, tile, out in ratio.products(wb_ref.at[pair], 2):
        g_ref[plane, b, 0 : sz.hr, tile * LANES : (tile + 1) * LANES] = out
    for plane in range(2):
        z = 2 * pair + plane
        for b in range(sz.n):
            rows = jnp.concatenate([own_ref[z, b], g_ref[plane, b]], axis=0)
            back = jnp.dot(rt_ref[z], rows, preferred_element_type=F32)
            yield z, b, back[0 : sz.rows, :]


def block_norm(sz, b, icn):
    kind = 1 if b == 0 else 2 if b == sz.n - 1 else 0
    return icn[kind : kind + 1, :]


def place_ratio(sz, me, stack_ref, main_ref, side_ref):
    ratio = PairWindows(sz, main_ref, side_ref)
    ratio.clear()
    for j in range(sz.half):
        for k in range(2):
            ratio.put(2 * ((me // 2) ^ j) + k, stack_ref[j, k])
    return ratio


def first_kernel(
    sz, me_ref, radius_hbm, phase_hbm, row_hbm, col_hbm, vol_hbm,
    rc_ref, keep_ref, send_ref,
    radius_ref, phase_ref, row_ref, col_ref, vol_ref, t_ref, a_ref, m_ref, x_ref, s_ref, sems,
):
    pairs = ((radius_hbm, radius_ref), (phase_hbm, phase_ref), (row_hbm, row_ref), (col_hbm, col_ref))
    small = [pltpu.make_async_copy(a, b, sems.at[i]) for i, (a, b) in enumerate(pairs)]
    large = [
        pltpu.make_async_copy(vol_hbm.at[z], vol_ref.at[z], sems.at[4 + z])
        for z in range(sz.planes)
    ]
    for copy in small + large:
        copy.start()
    part = lax.rem(me_ref[0], 2)
    m_ref[...] = jnp.zeros_like(m_ref)
    x_ref[...] = jnp.zeros_like(x_ref)
    for copy in small:
        copy.wait()
    for z in range(sz.planes):
        reach = radius_ref[z]
        phase_rows(sz, z, phase_ref, col_ref, t_ref, a_ref)
        matrix = spread_matrix(sz, reach, a_ref)
        rest = jnp.zeros((round_up(sz.span, 16) - sz.span, sz.wl), F32)
        matrix = jnp.concatenate([matrix, rest], axis=0) if rest.shape[0] else matrix
        m_ref[z, LANES : LANES + matrix.shape[0], :] = matrix.astype(BF16)
        rt = row_matrix(sz, z, reach, row_ref)
        rt = rt.T.astype(BF16)
        lanes = slice(z * sz.rp, (z + 1) * sz.rp)
        rc_ref[pl.ds(pl.multiple_of((1 - part) * sz.hr, sz.hr), sz.hr), lanes] = rt[0 : sz.hr, :]
        rc_ref[pl.ds(pl.multiple_of(part * sz.hr, sz.hr), sz.hr), lanes] = rt[sz.hr : sz.ep, :]
    for z in range(sz.planes):
        large[z].wait()
        x = jnp.concatenate([vol_ref[z], jnp.zeros((sz.rp - sz.rows, sz.cols), F32)], axis=0)
        x_ref[z, :, LANES : LANES + sz.cols] = x.astype(BF16)
        for b, start in enumerate(sz.starts):
            shift = start % LANES
            window = x_ref[z, :, start - shift : start - shift + sz.ka]
            matrix = m_ref[z, LANES - shift : LANES - shift + sz.ka, :]
            out = jnp.dot(window, matrix, preferred_element_type=F32)
            s_ref[b, z * sz.rp : (z + 1) * sz.rp, :] = out.astype(BF16)
    rows_forward(sz, rc_ref, s_ref, keep_ref, send_ref)


def table_kernel(
    sz, me_ref, strip_ref, radius_hbm, phase_hbm, row_hbm, col_hbm, after_ref,
    wf_ref, wb_ref, rt_ref, irn_ref, icn_ref,
    radius_ref, phase_ref, row_ref, col_ref, t_ref, a_ref, sems,
):
    pairs = ((radius_hbm, radius_ref), (phase_hbm, phase_ref), (row_hbm, row_ref), (col_hbm, col_ref))
    small = [pltpu.make_async_copy(a, b, sems.at[i]) for i, (a, b) in enumerate(pairs)]
    for copy in small:
        copy.start()
    for copy in small:
        copy.wait()
    kind, col = iota((8, 2 * LANES), 0), iota((8, 2 * LANES), 1)
    missing = [(kind == 1) & (col >= LANES + HALF)]
    if sz.tiles == 2:
        missing.append((kind == 2) & (col >= sz.w))
    else:
        missing[0] |= (kind == 2) & (col >= LANES) & (col < LANES + HALF)
    ones = [jnp.where(part, 0.0, 1.0).astype(BF16) for part in missing]
    for z in range(sz.planes):
        reach = radius_ref[z]
        phase_rows(sz, z, phase_ref, col_ref, t_ref, a_ref)
        wf_ref[z] = by_block(sz, spread_matrix(sz, reach, a_ref))
        parts = by_tile(sz, gather_matrix(sz, reach, a_ref))
        for tile, part in enumerate(parts):
            lanes = slice(z % 2 * LANES, (z % 2 + 1) * LANES)
            wb_ref[z // 2, tile, :, lanes] = part
        norm = [jnp.dot(a, b, preferred_element_type=F32) for a, b in zip(ones, parts)]
        norm = jnp.concatenate(norm, axis=1)
        icn_ref[z] = jnp.where(norm > 0.0, 1.0 / norm, 0.0)
        rt = row_matrix(sz, z, reach, row_ref)
        lane = iota(rt.shape, 1)
        top = jnp.where(lane < sz.hr, rt, 0.0)
        bottom = jnp.where((lane >= sz.hr) & (lane < sz.ep), rt, 0.0)
        bottom = pltpu.roll(bottom, sz.hp - sz.hr, 1)
        both = top + bottom
        turned = pltpu.roll(both, sz.hp, 1)
        rt_ref[z] = jnp.where(lax.rem(me_ref[0], 2) == 0, both, turned).astype(BF16)
        row = strip_ref[0] * sz.rows + iota(rt.shape, 1) - RMAX
        norm = jnp.sum(jnp.where((row >= 0) & (row < sz.total), rt, 0.0), axis=1, keepdims=True)
        irn_ref[z] = jnp.where(norm > 0.0, 1.0 / norm, 0.0)


def block_kernel(sz, vol_hbm, after_ref, blocks_ref, vol_ref, sems, planes):
    copies = [
        pltpu.make_async_copy(vol_hbm.at[z], vol_ref.at[i], sems.at[i])
        for i, z in enumerate(planes)
    ]
    for copy in copies:
        copy.start()
    for z, copy in enumerate(copies):
        copy.wait()
        for b in range(sz.n):
            block = vol_ref[z, :, b * sz.w : (b + 1) * sz.w]
            if sz.wl > sz.w:
                block = jnp.concatenate([block, jnp.zeros((sz.rows, sz.wl - sz.w), F32)], axis=1)
            blocks_ref[z, b] = block


def core_sum_kernel(sz, me_ref, keep_ref, recv_ref, own_ref, *out_refs):
    mine = me_ref[0] // 2
    for j, ref in enumerate((own_ref, *out_refs)):
        blocks = pl.ds(2 * (mine ^ j), 2)
        total = keep_ref[blocks] + recv_ref[blocks].astype(F32)
        ref[...] = total if j == 0 else pack(sz, total)


def chip_sum_kernel(sz, me_ref, after_ref, own_ref, meas_ref, *refs, first):
    recv_refs, (sum_ref, edge_ref) = refs[:-2], refs[-2:]
    total = own_ref[...]
    for ref in recv_refs:
        total = total + unpack(sz, ref[...])
    sum_ref[...] = total
    edges = []
    for at, row in ((0, 0), (sz.rows - sz.hr, sz.rows - SIDE)):
        parts = [total[:, at : at + 32, :]]
        if first:
            meas = meas_ref[:, row : row + SIDE, :]
            high = meas.astype(BF16).astype(F32)
            parts += [high, meas - high]
        edges.append(jnp.concatenate(parts, axis=1))
    top, bottom = edges
    edge_ref[...] = jnp.where(lax.rem(me_ref[0], 2) == 0, top, bottom).astype(BF16)


def ratio_kernel(
    sz, me_ref, strip_ref, after_ref, sum_ref, meas_ref, edge_ref, first_edge_ref,
    ratio_ref, s_ref, m_ref,
):
    part = lax.rem(me_ref[0], 2)
    s_ref[...] = sum_ref[...]
    m_ref[...] = jnp.zeros_like(m_ref)
    edge, first_edge = edge_ref[...].astype(F32), first_edge_ref[...].astype(F32)
    alone = jnp.where(part == 0, strip_ref[0] == 0, (strip_ref[0] + 1) * sz.rows == sz.total)
    rows = jnp.where(alone, 0.0, edge[:, 0:32, :])
    meas = first_edge[:, 32:48, :] + first_edge[:, 48:64, :]

    @pl.when(part == 0)
    def _():
        s_ref[:, 0:32, :] += rows
        m_ref[:, 0:RMAX, :] = meas[:, SIDE - RMAX :, :]
        m_ref[:, RMAX : sz.hr, :] = meas_ref[:, 0 : sz.hr - RMAX, :]

    @pl.when(part == 1)
    def _():
        first = sz.rows - sz.hr
        s_ref[:, first : first + 32, :] += rows
        m_ref[:, 0 : first + RMAX, :] = meas_ref[:, sz.hr - RMAX :, :]
        m_ref[:, first + RMAX : first + 2 * RMAX, :] = meas[:, 0:RMAX, :]

    row = part * sz.hr + iota(s_ref.shape, 1)
    spot = strip_ref[0] * sz.rows + row - RMAX
    inside = (row < sz.e) & (spot >= 0) & (spot < sz.total) & (iota(s_ref.shape, 2) < sz.w)
    ratio_ref[...] = jnp.where(inside, m_ref[...] / s_ref[...], 0.0).astype(BF16)


def stack_kernel(sz, after_ref, *refs, order):
    for j, ref in zip(order, refs[:-1]):
        refs[-1][j] = ref[...]


def ahead_kernel(sz, me_ref, same_ref, wb_ref, own_ref, ratio_ref, ratio_side_ref):
    ratio = place_ratio(sz, me_ref[0], same_ref, ratio_ref, ratio_side_ref)
    own_ref[:, :, sz.hr :, :] = jnp.zeros((sz.planes, sz.n, sz.hp - sz.hr, sz.wl), BF16)
    for pair in range(sz.planes // 2):
        for b, plane, tile, out in ratio.products(wb_ref.at[pair], 2):
            lanes = slice(tile * LANES, (tile + 1) * LANES)
            own_ref[2 * pair + plane, b, 0 : sz.hr, lanes] = out


def middle_kernel(
    sz, me_ref, own_ref, other_ref, wf_ref, wb_ref, rt_ref, irn_ref, icn_ref, rc_ref, before_ref, after_ref,
    new_ref, keep_ref, send_ref,
    ratio_ref, ratio_side_ref, g_ref, x_ref, x_side_ref, s_ref,
):
    ratio = place_ratio(sz, me_ref[0], other_ref, ratio_ref, ratio_side_ref)
    g_ref[:, :, sz.hr :, :] = jnp.zeros((2, sz.n, sz.hp - sz.hr, sz.wl), BF16)
    estimate = Windows(sz, sz.rp, x_ref, x_side_ref, 4)
    estimate.clear_sides()
    lead = jnp.zeros((sz.rp - sz.rows, sz.wl), F32)
    split = before_ref.shape[0]
    for pair in range(sz.planes // 2):
        for z, b, back in backward(sz, pair, ratio, wb_ref, rt_ref, own_ref, g_ref):
            old = before_ref[z, b] if z < split else after_ref[z - split, b]
            if b == 0:
                icn, irn = icn_ref[z], irn_ref[z][0 : sz.rows]
            norm = irn * block_norm(sz, b, icn)
            new = old * back * norm
            new_ref[z, b] = new
            estimate.put(b, 0, jnp.concatenate([new, lead]).astype(BF16))
            if b == sz.n - 1:
                for k, out in estimate.products(wf_ref[z]):
                    s_ref[k, z * sz.rp : (z + 1) * sz.rp, :] = out
    rows_forward(sz, rc_ref, s_ref, keep_ref, send_ref)


def last_kernel(
    sz, me_ref, own_ref, other_ref, wb_ref, rt_ref, irn_ref, icn_ref, vol_ref,
    out_hbm, ratio_ref, ratio_side_ref, g_ref, out_ref, sems,
):
    ratio = place_ratio(sz, me_ref[0], other_ref, ratio_ref, ratio_side_ref)
    g_ref[:, :, sz.hr :, :] = jnp.zeros((2, sz.n, sz.hp - sz.hr, sz.wl), BF16)
    middle = sz.cols // 2 // LANES * LANES
    lanes = (slice(0, middle), slice(middle, sz.cols))
    copies = [
        [
            pltpu.make_async_copy(out_ref.at[z, :, k], out_hbm.at[z, :, k], sems.at[z, i])
            for i, k in enumerate(lanes)
        ]
        for z in range(sz.planes)
    ]
    for pair in range(sz.planes // 2):
        for z, b, back in backward(sz, pair, ratio, wb_ref, rt_ref, own_ref, g_ref):
            if b == 0:
                icn, irn = icn_ref[z], irn_ref[z][0 : sz.rows]
            norm = irn * block_norm(sz, b, icn)
            new = vol_ref[z, b] * back * norm
            out_ref[z, :, b * sz.w : (b + 1) * sz.w] = new[:, 0 : sz.w]
            if b == sz.n // 2 - 1:
                copies[z][0].start()
            if b == sz.n - 1:
                copies[z][1].start()
    for plane in copies:
        for copy in plane:
            copy.wait()


SMEM = pl.BlockSpec(memory_space=pltpu.SMEM)
VMEM = pl.BlockSpec(memory_space=pltpu.VMEM)
ANY = pl.BlockSpec(memory_space=pl.ANY)
HBM = pl.BlockSpec(memory_space=pltpu.HBM)


def shape(dims, dtype):
    return jax.ShapeDtypeStruct(dims, dtype)


def call(kernel, sz, name, in_specs, out_specs, out_shape, scratch, args, mib, micros=1):
    return pl.pallas_call(
        functools.partial(kernel, sz),
        in_specs=in_specs,
        out_specs=out_specs,
        out_shape=out_shape,
        scratch_shapes=scratch,
        compiler_params=pltpu.CompilerParams(vmem_limit_bytes=mib * 1024 * 1024),
        cost_estimate=pl.CostEstimate(
            flops=0, bytes_accessed=micros * 3_000_000, transcendentals=0
        ),
        name=name,
    )(*args)


def local(volume, measured, row_taps, col_taps, phase_map, radius):
    n = lax.axis_size("depth")
    strips = lax.axis_size("strip")
    planes, rows, cols = volume.shape
    sz = Sizes(planes, rows, strips, cols, n, phase_map.shape[1])
    me = lax.axis_index("depth")
    strip = lax.axis_index("strip")
    me_arg = (me ^ (strip % 2)).reshape(1).astype(jnp.int32)
    strip_arg = strip.reshape(1).astype(jnp.int32)
    to_core = [(i, i ^ 1) for i in range(n)]
    to_chip = [[(i, i ^ (2 * j)) for i in range(n)] for j in range(1, sz.half)]
    order_rs = range(sz.half - 1)[::-1]
    order_ag = range(sz.half - 1)
    to_strip = []
    for chip in range(sz.half):
        for lower in range(1, strips):
            row = (2 * chip + lower % 2) * strips
            to_strip += [(row + lower, row + lower - 1), (row + lower - 1, row + lower)]
        for edge, core in ((0, 0), (strips - 1, strips % 2)):
            pair = [(2 * c + core) * strips + edge for c in (chip, chip ^ 1)]
            to_strip.append(tuple(pair))

    volume = pltpu.with_memory_space_constraint(volume, pltpu.HBM)
    meas = lax.dynamic_slice_in_dim(measured, (me // 2) * 2 * sz.w, 2 * sz.w, axis=1)
    meas = jnp.stack([meas[:, 0 : sz.w], meas[:, sz.w :]])
    meas = jnp.pad(meas, ((0, 0), (0, 0), (0, sz.wl - sz.w)))
    by_family = col_taps.transpose(1, 0, 2)

    flat = shape((2, sz.hr, sz.wl), BF16)
    flat32 = shape((2, sz.hr, sz.wl), F32)
    halves = [shape((n, sz.hr, sz.wl), F32), shape((n, sz.hr, sz.wl), BF16)]
    blocked = shape((planes, n, rows, sz.wl), F32)
    tap_args = tuple(
        pltpu.with_memory_space_constraint(x, pltpu.HBM)
        for x in (radius, phase_map, row_taps, by_family)
    )
    tap_scratch = [
        pltpu.SMEM(radius.shape, jnp.int32),
        pltpu.SMEM(phase_map.shape, jnp.int32),
        pltpu.VMEM(row_taps.shape, F32),
        pltpu.VMEM(by_family.shape, F32),
    ]
    row_scratch = [
        pltpu.VMEM((round_up(sz.pitch, 8), sz.kp), F32),
        pltpu.VMEM((sz.ar, sz.kp), F32),
    ]
    s_scratch = pltpu.VMEM((n, planes * sz.rp, sz.wl), BF16)
    place_scratch = [
        pltpu.VMEM(((n + 1) * sz.hr, sz.wl), BF16),
        pltpu.VMEM(((n + 2) * sz.hr, LANES), BF16),
    ]
    ratio_scratch = place_scratch + [pltpu.VMEM((2, n, sz.hp, sz.wl), BF16)]
    x_scratch = [
        pltpu.VMEM((n * sz.rp, sz.wl), BF16),
        pltpu.VMEM(((n + 2) * sz.rp, LANES), BF16),
    ]
    vol_scratch = pltpu.VMEM(volume.shape, F32)

    rc, keep, send = call(
        first_kernel, sz, "first",
        [SMEM] + [HBM] * 5,
        [VMEM] * 3,
        [shape((sz.ep, planes * sz.rp), BF16), *halves],
        tap_scratch + [vol_scratch] + row_scratch
        + [
            pltpu.VMEM((planes, LANES + sz.ka, sz.wl), BF16),
            pltpu.VMEM((planes, sz.rp, sz.xw), BF16),
            s_scratch,
            pltpu.SemaphoreType.DMA((4 + planes,)),
        ],
        (me_arg, *tap_args, volume),
        24, 4,
    )

    def block_planes(which, after):
        return call(
            functools.partial(block_kernel, planes=tuple(which)), sz, "blocks",
            [HBM, ANY], VMEM, shape((len(which), n, rows, sz.wl), F32),
            [
                pltpu.VMEM((len(which), rows, cols), F32),
                pltpu.SemaphoreType.DMA((len(which),)),
            ],
            (volume, after), 12, 2,
        )

    tables, current = None, None
    for iteration in range(ITERS):
        recv = lax.ppermute(send, "depth", to_core)
        own, *sends = call(
            core_sum_kernel, sz, "core_sum",
            [SMEM, VMEM, VMEM],
            [VMEM] * sz.half,
            [flat32] + [flat] * (sz.half - 1),
            [], (me_arg, keep, recv), 4,
        )
        if tables is None:
            wf, *tables = call(
                table_kernel, sz, "tables",
                [SMEM] * 2 + [HBM] * 4 + [ANY],
                [VMEM] * 5,
                [
                    shape((planes, sz.kb, sz.wl), BF16),
                    shape((planes // 2, sz.tiles, 2 * LANES, 2 * LANES), BF16),
                    shape((planes, sz.rp, sz.el), BF16),
                    shape((planes, sz.rp, 1), F32),
                    shape((planes, 8, sz.wl), F32),
                ],
                tap_scratch + row_scratch + [pltpu.SemaphoreType.DMA((4,))],
                (me_arg, strip_arg, *tap_args, own),
                8, 2,
            )
        recvs = [lax.ppermute(sends[j], "depth", to_chip[j]) for j in order_rs]
        total, edge = call(
            functools.partial(chip_sum_kernel, first=iteration == 0), sz, "chip_sum",
            [SMEM, ANY] + [VMEM] * (2 + len(recvs)),
            [VMEM] * 2,
            [flat32, shape((2, 64 if iteration == 0 else 32, sz.wl), BF16)],
            [], (me_arg, tables[3], own, meas, *recvs), 4,
        )
        edge = lax.ppermute(edge, ("depth", "strip"), to_strip)
        first_edge = edge if iteration == 0 else first_edge
        if iteration == 0:
            before = block_planes(range(planes // 2), total)
        ratio = call(
            ratio_kernel, sz, "ratio",
            [SMEM] * 2 + [ANY] + [VMEM] * 4,
            VMEM,
            flat,
            [pltpu.VMEM(flat32.shape, F32)] * 2,
            (me_arg, strip_arg, before, total, meas, edge, first_edge), 4,
        )
        chips = [lax.ppermute(ratio, "depth", to_chip[j]) for j in order_ag]
        if iteration == 0:
            after = block_planes(range(planes // 2, planes), ratio)
        same = call(
            functools.partial(stack_kernel, order=(0, *[j + 1 for j in order_ag])), sz, "stack",
            [ANY] + [VMEM] * sz.half, VMEM, shape((sz.half,) + flat.shape, BF16),
            [], (after, ratio, *chips), 4,
        )
        other = lax.ppermute(same, "depth", to_core)
        own = call(
            ahead_kernel, sz, "ahead",
            [SMEM] + [VMEM] * 2, VMEM,
            shape((planes, n, sz.hp, sz.wl), BF16),
            place_scratch, (me_arg, same, tables[0]), 8,
        )
        if iteration < ITERS - 1:
            current, keep, send = call(
                middle_kernel, sz, "middle",
                [SMEM] + [VMEM] * 10,
                [VMEM] * 3,
                [blocked, *halves],
                ratio_scratch + x_scratch + [s_scratch],
                (me_arg, own, other, wf, *tables, rc, before, after),
                16, 5,
            )
        else:
            current = call(
                last_kernel, sz, "last",
                [SMEM] + [VMEM] * 7,
                HBM,
                shape(volume.shape, F32),
                ratio_scratch + [vol_scratch, pltpu.SemaphoreType.DMA((planes, 2))],
                (me_arg, own, other, *tables, current),
                16, 5,
            )
    return current


def solution(mesh):
    return jax.shard_map(
        local,
        mesh=mesh,
        in_specs=(
            P("depth", "strip", None),
            P("strip", None),
            P("depth", None),
            P("depth", None, None),
            P("depth", None),
            P("depth"),
        ),
        out_specs=P("depth", "strip", None),
        check_vma=False,
    )
```
